32 devices in a mesh: head: 2 (over core), blk: 2 (over x), dp: 8 (over z, y).
Axes of the slice: x: 2, y: 2, z: 4, core: 2. Of those that a mesh axis runs over, the one named last changes fastest.
Arguments:
- layer_in: bfloat16 [32, 1024, 768], P('dp', 'blk', 'head'), may hold values from -6 to 6
- segments: int32 [32, 1024], P('dp'), may hold values from 0 to 6, as said below
- block_perm: int32 [12, 2], P('head'), may hold values from 0 to 1, as said below
- w_query: bfloat16 [768, 768], P(None, 'head'), may hold values from -0.21875 to 0.21875
- b_query: float32 [768], P('head'), may hold values from -3 to 3
- w_key: bfloat16 [768, 768], P(None, 'head'), may hold values from -0.21875 to 0.21875
- w_value: bfloat16 [768, 768], P(None, 'head'), may hold values from -0.21875 to 0.21875
- b_value: float32 [768], P('head'), may hold values from -3 to 3
- w_attn_out: bfloat16 [768, 768], P('head'), may hold values from -0.625 to 0.625
- b_attn_out: float32 [768], P('head'), may hold values from -3 to 3
- norm1_gain: float32 [768], P('head'), may hold values from 0.5 to 1.5
- norm1_bias: float32 [768], P('head'), may hold values from -3 to 3
- w_up: bfloat16 [768, 3072], P(None, 'head'), may hold values from -0.21875 to 0.21875
- b_up: float32 [3072], P('head'), may hold values from -3 to 3
- w_down: bfloat16 [3072, 768], P('head'), may hold values from -0.109375 to 0.109375
- b_down: float32 [768], P('head'), may hold values from -3 to 3
- norm2_gain: float32 [768], P('head'), may hold values from 0.5 to 1.5
- norm2_bias: float32 [768], P('head'), may hold values from -3 to 3
- grad_out: float32 [32, 1024, 768], P('dp', 'blk', 'head'), may hold values from -6 to 6
Outputs:
- layer_out: float32 [32, 1024, 768], P('dp', 'blk', 'head')
- grad_in: float32 [32, 1024, 768], P('dp', 'blk', 'head')
- grad_w_query: float32 [768, 768], P(None, 'head')
- grad_b_query: float32 [768], P('head')
- grad_w_key: float32 [768, 768], P(None, 'head')
- grad_w_value: float32 [768, 768], P(None, 'head')
- grad_b_value: float32 [768], P('head')
- grad_w_attn_out: float32 [768, 768], P('head')
- grad_b_attn_out: float32 [768], P('head')
- grad_norm1_gain: float32 [768], P('head')
- grad_norm1_bias: float32 [768], P('head')
- grad_w_up: float32 [768, 3072], P(None, 'head')
- grad_b_up: float32 [3072], P('head')
- grad_w_down: float32 [3072, 768], P('head')
- grad_b_down: float32 [768], P('head')
- grad_norm2_gain: float32 [768], P('head')
- grad_norm2_bias: float32 [768], P('head')
The draws below stay inside these ranges and needn't reach their ends.
Inputs may be any that keep to these rules, and one draw needn't show every extreme that they name: `segments`: within each sequence the numbers start at 0 at the first position, never fall, and rise by one at six positions: three in 1 to 383 and three in 640 to 1023. `block_perm`: each row is a permutation of the block numbers; exactly 6 rows exchange the two blocks and the others keep them in place.
All inputs are finite; a program needn't handle non-finite values.
Results may differ from the reference program's by a relative error of at most 0.014.
Values may be sent and summed in bfloat16 or wider, within the bound.
A program may use at most 192 MiB of HBM per device.

```python
import jax
import jax.numpy as jnp
from jax import lax

D = 768
HEADS = 12
HD = 64
FF = 3072
BLOCK = 512
SEQ = 1024
SEQS = 32
N_BLK = 2


def draw_segments(key, part):
    key = jax.random.fold_in(key, 11)
    seq_len = BLOCK * N_BLK
    lower_end = seq_len // 2 - seq_len // 8
    upper_start = seq_len // 2 + seq_len // 8

    def one_sequence(subkey):
        early_key, late_key = jax.random.split(subkey)
        early_cuts = 1 + jax.random.choice(early_key, lower_end - 1, (3,), replace=False)
        late_cuts = upper_start + jax.random.choice(late_key, seq_len - upper_start, (3,), replace=False)
        cut_places = jnp.concatenate([early_cuts, late_cuts]).astype(jnp.int32)
        positions = jnp.arange(seq_len, dtype=jnp.int32)
        return jnp.sum((positions[:, None] >= cut_places[None, :]).astype(jnp.int32), axis=1)
    return jax.vmap(one_sequence)(jax.random.split(key, SEQS)).astype(jnp.int32)


def draw_block_perm(key, part):
    key = jax.random.fold_in(key, 23)
    ordering = jax.random.permutation(key, HEADS)
    swapped = ordering < HEADS // 2
    block_ids = jnp.arange(N_BLK, dtype=jnp.int32)
    return jnp.where(swapped[:, None], N_BLK - 1 - block_ids[None, :], block_ids[None, :]).astype(jnp.int32)


def block_levels(stream_key, shape, shards, least, high):
    factor_of, own = 1.0, jax.random.fold_in(stream_key, 6)
    for axis_at, shards_of in shards:
        steps = jnp.exp(jax.random.uniform(jax.random.fold_in(own, axis_at), (shards_of,), jnp.float32, least / len(shards), high / len(shards)))
        factor_of = factor_of * jnp.repeat(steps, shape[axis_at] // shards_of).reshape([-1 if axis == axis_at else 1 for axis in range(len(shape))])
    return factor_of


def centred(rng, dims, deviation, reach, cuts=(), kind=jnp.bfloat16):
    values = jax.random.normal(rng, dims, jnp.float32) * deviation
    if len(cuts) > 0:
        values = block_levels(rng, dims, cuts, -0.22, 0.18) * values
    return jnp.clip(values, min=-reach, max=reach).astype(kind)


def setup_inputs(seed: int = 0) -> dict:
    seeds = jax.random.split(jax.random.key(seed), 20)
    layer_in = centred(seeds[0], (SEQS, SEQ, D), 1.0, 6.0, ((0, 8), (1, 2), (2, 2)))
    segments = draw_segments(jax.random.fold_in(seeds[19], 71), 0)
    block_perm = draw_block_perm(jax.random.fold_in(seeds[19], 71), 0)
    w_query = centred(seeds[3], (D, D), D ** -0.5, 0.21875, ((1, 2),))
    b_query = centred(seeds[4], (D,), 0.5, 3.0, ((0, 2),), jnp.float32)
    w_key = centred(seeds[5], (D, D), D ** -0.5, 0.21875, ((1, 2),))
    w_value = centred(seeds[6], (D, D), D ** -0.5, 0.21875, ((1, 2),))
    b_value = centred(seeds[7], (D,), 0.5, 3.0, ((0, 2),), jnp.float32)
    w_attn_out = centred(seeds[8], (D, D), (D // 8) ** -0.5, 0.625, ((0, 2),))
    b_attn_out = centred(seeds[9], (D,), 0.5, 3.0, ((0, 2),), jnp.float32)
    norm1_gain = jnp.clip(1.0 + 0.1 * jax.random.normal(seeds[10], (D,), jnp.float32), 0.5, 1.5)
    norm1_bias = centred(seeds[11], (D,), 0.5, 3.0, ((0, 2),), jnp.float32)
    w_up = centred(seeds[12], (D, FF), D ** -0.5, 0.21875, ((1, 2),))
    b_up = centred(seeds[13], (FF,), 0.5, 3.0, ((0, 2),), jnp.float32)
    w_down = centred(seeds[14], (FF, D), FF ** -0.5, 0.109375, ((0, 2),))
    b_down = centred(seeds[15], (D,), 0.5, 3.0, ((0, 2),), jnp.float32)
    norm2_gain = jnp.clip(1.0 + 0.1 * jax.random.normal(seeds[16], (D,), jnp.float32), 0.5, 1.5)
    norm2_bias = centred(seeds[17], (D,), 0.5, 3.0, ((0, 2),), jnp.float32)
    grad_out = centred(seeds[18], (SEQS, SEQ, D), 1.0, 6.0, ((0, 8), (1, 2), (2, 2)), jnp.float32)
    return dict(layer_in=layer_in, segments=segments, block_perm=block_perm, w_query=w_query, b_query=b_query, w_key=w_key, w_value=w_value, b_value=b_value, w_attn_out=w_attn_out, b_attn_out=b_attn_out, norm1_gain=norm1_gain, norm1_bias=norm1_bias, w_up=w_up, b_up=b_up, w_down=w_down, b_down=b_down, norm2_gain=norm2_gain, norm2_bias=norm2_bias, grad_out=grad_out)


@jax.custom_vjp
def low(v):
    return lax.optimization_barrier(v.astype(jnp.bfloat16)).astype(jnp.float32)

@jax.custom_vjp
def low_back(v):
    return v

def low_keep(v):
    return (low(v), None)

def low_pass(kept, grad):
    return (grad,)

def back_keep(v):
    return (v, None)

def back_low(kept, grad):
    return (low(grad),)
low.defvjp(low_keep, low_pass)
low_back.defvjp(back_keep, back_low)
EPSILON = 1e-05
NEGATIVE = -1e+30

def rounded_both(values):
    return low(low_back(values))

def matmul(left, right):
    return jnp.dot(left, right, precision=lax.Precision.HIGHEST)

def normalize(summed, gain, bias):
    mean = lax.optimization_barrier(jnp.mean(summed, axis=-1, keepdims=True))
    centered = summed - mean
    variance = lax.optimization_barrier(jnp.mean(centered * centered, axis=-1, keepdims=True))
    return centered * lax.rsqrt(variance + EPSILON) * gain + bias

def layer_forward(rows_in, params, seg_group, block_perm):
    w_query, b_query, w_key, w_value, b_value, w_attn_out, b_attn_out, norm1_gain, norm1_bias, w_up, b_up, w_down, b_down, norm2_gain, norm2_bias = params
    group_size = rows_in.shape[0]
    seq_len = rows_in.shape[1]
    flat_rows = rows_in.reshape(-1, D)
    score_scale = HD ** (-0.5)
    head_shape = (group_size, N_BLK, BLOCK, HEADS, HD)
    query_heads = rounded_both((matmul(flat_rows, w_query) + b_query) * score_scale).reshape(head_shape)
    key_heads = rounded_both(matmul(flat_rows, w_key)).reshape(head_shape)
    value_heads = rounded_both(matmul(flat_rows, w_value) + b_value).reshape(head_shape)
    block_ids = jnp.arange(N_BLK, dtype=jnp.int32)
    picker = (block_perm[:, :, None] == block_ids[None, None, :]).astype(jnp.float32)
    key_chosen = jnp.einsum('hij,gjbhd->gibhd', picker, key_heads, precision=lax.Precision.HIGHEST)
    value_chosen = jnp.einsum('hij,gjbhd->gibhd', picker, value_heads, precision=lax.Precision.HIGHEST)
    seg_blocks = seg_group.reshape(group_size, N_BLK, BLOCK)
    key_seg = seg_blocks[:, block_perm]
    allowed = seg_blocks[:, None, :, :, None] == key_seg[:, :, :, None, :]
    covered = jnp.any(allowed, axis=-1, keepdims=True)
    usable = jnp.logical_or(allowed, jnp.logical_not(covered))
    scores = low_back(jnp.einsum('gibhd,gichd->ghibc', query_heads, key_chosen, precision=lax.Precision.HIGHEST))
    mixing = jax.nn.softmax(jnp.where(usable, scores, NEGATIVE), axis=-1)
    context = rounded_both(jnp.einsum('ghibc,gichd->gibhd', low(mixing), value_chosen, precision=lax.Precision.HIGHEST)).reshape(-1, D)
    attended = low_back(matmul(context, w_attn_out)) + b_attn_out
    normed_attn = normalize(flat_rows + attended, norm1_gain, norm1_bias)
    up_proj = low_back(matmul(low(normed_attn), w_up) + b_up)
    activated = low(jax.nn.gelu(up_proj, approximate=False))
    reduced_ffn = low_back(matmul(activated, w_down)) + b_down
    return normalize(normed_attn + reduced_ffn, norm2_gain, norm2_bias).reshape(group_size, seq_len, D)

def reference(layer_in, segments, block_perm, w_query, b_query, w_key, w_value, b_value, w_attn_out, b_attn_out, norm1_gain, norm1_bias, w_up, b_up, w_down, b_down, norm2_gain, norm2_bias, grad_out):
    weights = (w_query.astype(jnp.float32), b_query.astype(jnp.float32), w_key.astype(jnp.float32), w_value.astype(jnp.float32), b_value.astype(jnp.float32), w_attn_out.astype(jnp.float32), b_attn_out.astype(jnp.float32), norm1_gain.astype(jnp.float32), norm1_bias.astype(jnp.float32), w_up.astype(jnp.float32), b_up.astype(jnp.float32), w_down.astype(jnp.float32), b_down.astype(jnp.float32), norm2_gain.astype(jnp.float32), norm2_bias.astype(jnp.float32))
    seq_total = layer_in.shape[0]
    seq_len = layer_in.shape[1]
    group_size = 4 if seq_total % 4 == 0 else 2 if seq_total % 2 == 0 else 1
    groups = seq_total // group_size
    inputs = (layer_in.astype(jnp.float32).reshape(groups, group_size, seq_len, D), segments.reshape(groups, group_size, seq_len), grad_out.astype(jnp.float32).reshape(groups, group_size, seq_len, D))

    def step(totals, packed):
        rows_in, seg_group, cotangent = packed

        def forward(rows_value, params):
            return layer_forward(rows_value, params, seg_group, block_perm)
        result, pullback = jax.vjp(forward, rows_in, weights)
        grad_rows, grad_params = pullback(cotangent)
        updated = tuple((total + grad for total, grad in zip(totals, grad_params)))
        return (updated, (result, grad_rows))
    initial = tuple((jnp.zeros_like(weight) for weight in weights))
    totals, (results, grad_rows) = lax.scan(step, initial, inputs)
    return (results.reshape(layer_in.shape), grad_rows.reshape(layer_in.shape), totals[0], totals[1], totals[2], totals[3], totals[4], totals[5], totals[6], totals[7], totals[8], totals[9], totals[10], totals[11], totals[12], totals[13], totals[14])
```

```python
import functools

import jax
import jax.numpy as jnp
from jax import lax
from jax.experimental import pallas as pl
from jax.experimental.pallas import tpu as pltpu
from jax.sharding import PartitionSpec as P

EPSILON = 1e-05
NEGATIVE = -1e30
ROOT_HALF = 0.7071067811865476
DENSITY_SCALE = 0.3989422804014327
F32 = jnp.float32
BF16 = jnp.bfloat16
MIB = 1 << 20


def dot(left, right, left_dim=1, right_dim=0):
    return lax.dot_general(
        left, right, (((left_dim,), (right_dim,)), ((), ())), preferred_element_type=F32
    )


def fill_bias(bias_ref, query_seg, keys_seg):
    same = keys_seg == query_seg
    covered = jnp.max(jnp.where(same, 1.0, 0.0), axis=0, keepdims=True)
    bias_ref[...] = jnp.where(same, 0.0, covered * NEGATIVE)


def attend_kernel(head_width, q_ref, k_ref, v_ref, qseg_ref, kseg_ref, ctx_ref, lse_ref, bias_ref):
    @pl.when(pl.program_id(1) == 0)
    def _():
        fill_bias(bias_ref, qseg_ref[0], kseg_ref[...])

    queries, keys = q_ref[...], k_ref[...]
    pair_width = queries.shape[1]
    value_cols = v_ref[...].astype(F32).T.astype(BF16)
    lane = lax.broadcasted_iota(jnp.int32, (1, pair_width), 1)
    parts, logs = [], []
    for low in range(0, pair_width, head_width):
        chosen = jnp.logical_and(lane >= low, lane < low + head_width)
        scores = dot(keys, jnp.where(chosen, queries, 0), 1, 1) + bias_ref[...]
        top = jnp.max(scores, axis=0, keepdims=True)
        shifted = jnp.exp(scores - top)
        total = jnp.sum(shifted, axis=0, keepdims=True)
        context = dot(value_cols[low : low + head_width], shifted.astype(BF16))
        parts.append(context * (1.0 / total))
        logs.append(top + jnp.log(total))
    ctx_ref[...] = jnp.concatenate(parts, axis=0).T.astype(BF16)
    lse_ref[0, 0] = jnp.concatenate(logs, axis=0)


def attend(queries, first_pair, keys, values, query_seg, keys_seg, head_width):
    seq_count, block_len = query_seg.shape
    pair = 2 * head_width
    pairs = keys.shape[1] // pair
    spec = pl.BlockSpec((block_len, pair), lambda s, p: (s, p))
    return pl.pallas_call(
        functools.partial(attend_kernel, head_width),
        grid=(seq_count, pairs),
        in_specs=[
            pl.BlockSpec((block_len, pair), lambda s, p: (s, p + first_pair)),
            spec,
            spec,
            pl.BlockSpec((1, 1, block_len), lambda s, p: (s, 0, 0)),
            pl.BlockSpec((block_len, 1), lambda s, p: (s, 0)),
        ],
        out_specs=[spec, pl.BlockSpec((1, 1, 2, block_len), lambda s, p: (s, p, 0, 0))],
        out_shape=[
            jax.ShapeDtypeStruct(keys.shape, BF16),
            jax.ShapeDtypeStruct((seq_count, pairs, 2, block_len), F32),
        ],
        scratch_shapes=[pltpu.VMEM((block_len, block_len), F32)],
        compiler_params=pltpu.CompilerParams(vmem_limit_bytes=48 * MIB),
        name="attend",
    )(queries, keys, values, query_seg[:, None, :], keys_seg.reshape(-1, 1))


def attend_back_kernel(
    head_width, scale, q_ref, k_ref, v_ref, g_ref, lse_ref, qseg_ref, kseg_ref,
    dq_ref, dk_ref, dv_ref, bias_ref,
):
    @pl.when(pl.program_id(1) == 0)
    def _():
        fill_bias(bias_ref, qseg_ref[0], kseg_ref[...])

    queries, keys, values, grads = q_ref[...], k_ref[...], v_ref[...], g_ref[...]
    pair_width = queries.shape[1]
    key_cols = keys.astype(F32).T.astype(BF16)
    lane = lax.broadcasted_iota(jnp.int32, (1, pair_width), 1)
    query_parts = []
    for at, low in enumerate(range(0, pair_width, head_width)):
        chosen = jnp.logical_and(lane >= low, lane < low + head_width)
        scores = dot(keys, jnp.where(chosen, queries, 0), 1, 1) + bias_ref[...]
        mixing = jnp.exp(scores - lse_ref[0, 0, at : at + 1, :])
        grad_mixing = dot(values, jnp.where(chosen, grads, 0), 1, 1)
        inner = jnp.sum(mixing * grad_mixing, axis=0, keepdims=True)
        grad_scores = (mixing * (grad_mixing - inner)).astype(BF16)
        grad_value = dot(mixing.astype(BF16), grads)
        grad_key = dot(grad_scores, queries)
        query_parts.append(dot(key_cols[low : low + head_width], grad_scores))
        if at == 0:
            all_value, all_key = grad_value, grad_key
        else:
            all_value = jnp.where(chosen, grad_value, all_value)
            all_key = jnp.where(chosen, grad_key, all_key)
    dq_ref[...] = (jnp.concatenate(query_parts, axis=0).T.astype(BF16) * scale).astype(BF16)
    dk_ref[...] = all_key.astype(BF16)
    dv_ref[...] = all_value.astype(BF16)


def attend_back(
    queries, first_pair, keys, values, grads, logs, query_seg, keys_seg, head_width, scale
):
    seq_count, block_len = query_seg.shape
    pair = 2 * head_width
    pairs = keys.shape[1] // pair
    spec = pl.BlockSpec((block_len, pair), lambda s, p: (s, p))
    return pl.pallas_call(
        functools.partial(attend_back_kernel, head_width, scale),
        grid=(seq_count, pairs),
        in_specs=[
            pl.BlockSpec((block_len, pair), lambda s, p: (s, p + first_pair)),
            spec,
            spec,
            pl.BlockSpec((block_len, pair), lambda s, p: (s, p + first_pair)),
            pl.BlockSpec((1, 1, 2, block_len), lambda s, p: (s, p, 0, 0)),
            pl.BlockSpec((1, 1, block_len), lambda s, p: (s, 0, 0)),
            pl.BlockSpec((block_len, 1), lambda s, p: (s, 0)),
        ],
        out_specs=[spec] * 3,
        out_shape=[jax.ShapeDtypeStruct(keys.shape, BF16)] * 3,
        scratch_shapes=[pltpu.VMEM((block_len, block_len), F32)],
        compiler_params=pltpu.CompilerParams(vmem_limit_bytes=48 * MIB),
        name="attend_back",
    )(queries, keys, values, grads, logs, query_seg[:, None, :], keys_seg.reshape(-1, 1))


def unit_rows(rows, width):
    mean = jnp.sum(rows, axis=1, keepdims=True) * (1.0 / width)
    centered = rows - mean
    variance = jnp.sum(centered * centered, axis=1, keepdims=True) * (1.0 / width)
    inverse = lax.rsqrt(variance + EPSILON)
    return centered * inverse, inverse


def unit_back(grad, unit, inverse, gain, width):
    scaled = grad * gain
    plain = jnp.sum(scaled, axis=1, keepdims=True) * (1.0 / width)
    along = jnp.sum(scaled * unit, axis=1, keepdims=True) * (1.0 / width)
    return (scaled - plain - unit * along) * inverse


def middle_kernel(
    chunk, ctxu_ref, ctxc_ref, x_ref, gout_ref, vec_ref, bup_ref, wo_ref,
    wup0_ref, wup1_ref, wdn0_ref, wdn1_ref,
    out_ref, act0_ref, act1_ref, gup0_ref, gup1_ref, normed_ref, gffn_ref, gattn_ref, gattnb_ref,
    gctx_ref, gvec_ref, gbup_ref, slope_ref,
):
    width = x_ref.shape[1]
    half = ctxu_ref.shape[1]
    part = wup0_ref.shape[1]

    @pl.when(pl.program_id(0) == 0)
    def _():
        gvec_ref[...] = jnp.zeros_like(gvec_ref)
        gbup_ref[...] = jnp.zeros_like(gbup_ref)

    def vec(i):
        return vec_ref[i : i + 1, :]

    def add_vec(i, rows):
        gvec_ref[i : i + 1, :] += jnp.sum(rows, axis=0, keepdims=True)

    attended = dot(ctxu_ref[...], wo_ref[:half]) + dot(ctxc_ref[...], wo_ref[half:])
    unit1, inverse1 = unit_rows(x_ref[...].astype(F32) + attended + vec(0), width)
    normed = unit1 * vec(1) + vec(2)
    normed_low = normed.astype(BF16)
    normed_ref[...] = normed_low
    pieces = ((wup0_ref, wdn0_ref, act0_ref, gup0_ref), (wup1_ref, wdn1_ref, act1_ref, gup1_ref))
    down = jnp.zeros_like(normed)
    for at, (wup, wdn, act_ref, _) in enumerate(pieces):
        for low in range(0, part, chunk):
            cols = slice(at * part + low, at * part + low + chunk)
            up = dot(normed_low, wup[:, low : low + chunk]) + bup_ref[:, cols]
            cumulative = 0.5 + 0.5 * lax.erf(up * ROOT_HALF)
            slope_ref[:, cols] = cumulative + up * (jnp.exp(-0.5 * up * up) * DENSITY_SCALE)
            activated = (up * cumulative).astype(BF16)
            act_ref[:, low : low + chunk] = activated
            down += dot(activated, wdn[low : low + chunk, :])
    unit2, inverse2 = unit_rows(normed + down + vec(3), width)
    out_ref[...] = unit2 * vec(4) + vec(5)
    grad_out = gout_ref[...]
    add_vec(4, grad_out * unit2)
    add_vec(5, grad_out)
    grad_ffn = unit_back(grad_out, unit2, inverse2, vec(4), width)
    add_vec(3, grad_ffn)
    grad_ffn_low = grad_ffn.astype(BF16)
    gffn_ref[...] = grad_ffn_low
    back = jnp.zeros_like(normed)
    for at, (wup, wdn, _, gup_ref) in enumerate(pieces):
        for low in range(0, part, chunk):
            cols = slice(at * part + low, at * part + low + chunk)
            grad_act = dot(grad_ffn_low, wdn[low : low + chunk, :], 1, 1)
            grad_up = (grad_act * slope_ref[:, cols]).astype(BF16)
            gup_ref[:, low : low + chunk] = grad_up
            gbup_ref[:, cols] += jnp.sum(grad_up.astype(F32), axis=0, keepdims=True)
            back += dot(grad_up, wup[:, low : low + chunk], 1, 1)
    grad_mid = grad_ffn + back
    add_vec(1, grad_mid * unit1)
    add_vec(2, grad_mid)
    grad_attn = unit_back(grad_mid, unit1, inverse1, vec(1), width)
    add_vec(0, grad_attn)
    gattn_ref[...] = grad_attn
    grad_attn_low = grad_attn.astype(BF16)
    gattnb_ref[...] = grad_attn_low
    gctx_ref[...] = dot(grad_attn_low, wo_ref[...], 1, 1).astype(BF16)


def middle(ctx_same, ctx_cross, x, grad_out, vectors, b_up, w_out, w_up, w_down):
    rows, width = x.shape
    half = ctx_same.shape[1]
    part = w_up[0].shape[1]
    tile = 256
    chunk = part // 2

    def tiles(cols):
        return pl.BlockSpec((tile, cols), lambda i: (i, 0))

    def whole(array):
        return pl.BlockSpec(array.shape, lambda i: (0, 0), pipeline_mode=pl.Buffered(1))

    def shape(cols, kind):
        return jax.ShapeDtypeStruct((rows, cols), kind)

    outs = [
        (width, F32), (part, BF16), (part, BF16), (part, BF16), (part, BF16),
        (width, BF16), (width, BF16), (width, F32), (width, BF16), (width, BF16),
    ]
    sums = [jax.ShapeDtypeStruct(vectors.shape, F32), jax.ShapeDtypeStruct(b_up.shape, F32)]
    weights = [vectors, b_up, w_out, *w_up, *w_down]
    return pl.pallas_call(
        functools.partial(middle_kernel, chunk),
        grid=(rows // tile,),
        in_specs=[tiles(half), tiles(half), tiles(width), tiles(width)] + [whole(w) for w in weights],
        out_specs=[tiles(c) for c, _ in outs]
        + [pl.BlockSpec(s.shape, lambda i: (0, 0)) for s in sums],
        out_shape=[shape(c, k) for c, k in outs] + sums,
        scratch_shapes=[pltpu.VMEM((tile, 2 * part), F32)],
        compiler_params=pltpu.CompilerParams(vmem_limit_bytes=60 * MIB),
        name="middle",
    )(ctx_same, ctx_cross, x, grad_out, *weights)


LINES = 4


class Item:
    def __init__(self, at, source, first, cols, order):
        self.at, self.source, self.first, self.cols, self.order = at, source, first, cols, order


def plan_items(count, cols):
    step = cols // 3
    orders = {1: "ABA", 2: "ABABAC", 3: "ABABACBAB"}[count]
    axes = {"A": ("x", "y", "z"), "B": ("y", "x", "z"), "C": ("z", "x", "y")}
    return [
        Item(i, i // 3, (i % 3) * step, step, axes[o]) for i, o in enumerate(orders)
    ]


def reduce_rows(order, rows):
    sizes = []
    for axis in order:
        rows = rows // (LINES if axis == "z" else 2)
        sizes.append(rows)
    return sizes


def sum_kernel(count, groups, items, *refs):
    own = refs[:count]
    other = refs[count : 2 * count]
    small_own, small_other = refs[2 * count : 2 * count + 2]
    refs = refs[2 * count + 2 :]
    out = refs[:count]
    small_out = refs[count]
    total, landing, small_land, send_sem, recv_sem, small_send, small_recv = (
        refs[count + 1 : count + 1 + count],
        refs[count + 1 + count : count + 1 + count + 5 * len(items)],
        *refs[count + 1 + count + 5 * len(items) :],
    )
    rows = own[0].shape[0]
    head, blk, dp = lax.axis_index("head"), lax.axis_index("blk"), lax.axis_index("dp")
    low, line, group = dp % 2, (dp // 2) % LINES, dp // (2 * LINES)
    partner = {
        "head": {"head": 1 - head},
        "x": {"blk": 1 - blk},
        "y": {"dp": dp + 1 - 2 * low},
    }
    line_partner = [
        {"dp": group * (2 * LINES) + ((line + d) % LINES) * 2 + low} for d in range(1, LINES)
    ]
    group_partner = [
        {"dp": ((group + d) % groups) * (2 * LINES) + line * 2 + low} for d in range(1, groups)
    ]
    everyone = [partner["head"], partner["x"], partner["y"]] + line_partner + group_partner
    barrier = pltpu.get_barrier_semaphore()
    for device in everyone:
        pl.semaphore_signal(barrier, inc=1, device_id=device, device_id_type=pl.DeviceIdType.MESH)
    pl.semaphore_wait(barrier, len(everyone))

    started = []

    def remote(source, target, sends, recvs, at, slot, device):
        copy = pltpu.make_async_remote_copy(
            src_ref=source,
            dst_ref=target,
            send_sem=sends.at[at, slot],
            recv_sem=recvs.at[at, slot],
            device_id=device,
            device_id_type=pl.DeviceIdType.MESH,
        )
        copy.start()
        started.append(copy)
        return copy

    z_slot, g_slot = 3, 3 + LINES - 1
    back_slot = g_slot + groups - 1

    def bufs(item):
        return landing[5 * item.at : 5 * item.at + 5]

    def cols(item):
        return slice(item.first, item.first + item.cols)

    def part(ref, start, size, item):
        return ref.at[pl.ds(pl.multiple_of(start, 16), size), cols(item)]

    def stages(item):
        hbuf, *bufs3, gbuf = bufs(item)
        mine = total[item.source]
        result = out[item.source]
        core = remote(
            other[item.source].at[:, cols(item)], hbuf, send_sem, recv_sem, item.at, 0,
            partner["head"],
        )
        yield
        core.wait_recv()
        mine[:, cols(item)] = (
            own[item.source][:, cols(item)].astype(F32) + hbuf[...].astype(F32)
        ).astype(BF16)
        start, size = 0, rows
        trail = []
        for buf, axis in zip(bufs3, item.order):
            trail.append((axis, start, size))
            if axis == "z":
                size = size // LINES
                copies = [
                    remote(
                        part(mine, start + ((line + d) % LINES) * size, size, item),
                        buf.at[d - 1], send_sem, recv_sem, item.at, z_slot + d - 1,
                        line_partner[d - 1],
                    )
                    for d in range(1, LINES)
                ]
                start = start + line * size
            else:
                size = size // 2
                bit = blk if axis == "x" else low
                copies = [
                    remote(
                        part(mine, start + (1 - bit) * size, size, item), buf.at[0],
                        send_sem, recv_sem, item.at, 1 if axis == "x" else 2, partner[axis],
                    )
                ]
                start = start + bit * size
            yield
            here = part(mine, start, size, item)
            value = here[...].astype(F32)
            for d, copy in enumerate(copies):
                copy.wait_recv()
                value = value + buf[d].astype(F32)
            here[...] = value.astype(BF16)
        if groups > 1:
            copies = [
                remote(
                    part(mine, start, size, item), gbuf.at[d - 1], send_sem, recv_sem, item.at,
                    g_slot + d - 1, group_partner[d - 1],
                )
                for d in range(1, groups)
            ]
            yield
            value = part(mine, start, size, item)[...].astype(F32)
            for d, copy in enumerate(copies):
                copy.wait_recv()
                value = value + gbuf[d].astype(F32)
            part(result, start, size, item)[...] = value.astype(BF16)
        else:
            part(result, start, size, item)[...] = part(mine, start, size, item)[...]
        for axis, before, whole in reversed(trail):
            here = part(result, start, size, item)
            if axis == "z":
                copies = [
                    remote(
                        here, here, send_sem, recv_sem, item.at, back_slot + 1 + d,
                        line_partner[d - 1],
                    )
                    for d in range(1, LINES)
                ]
            else:
                copies = [
                    remote(
                        here, here, send_sem, recv_sem, item.at,
                        back_slot + (0 if axis == "x" else 1), partner[axis],
                    )
                ]
            yield
            for copy in copies:
                copy.wait_recv()
            start, size = before, whole

    def small_stages():
        small_out[...] = small_own[...]
        copy = remote(
            small_other, small_land.at[0], small_send, small_recv, 0, 0, partner["head"]
        )
        yield
        copy.wait_recv()
        slot = 1
        value = small_own[...] + small_land[0]
        for devices in ([partner["x"]], [partner["y"]], line_partner, group_partner):
            if not devices:
                continue
            at = slot
            small_stage = small_land.at[slot]
            small_stage[...] = value
            slot += 1
            copies = []
            for device in devices:
                copies.append(
                    remote(
                        small_stage, small_land.at[slot], small_send, small_recv, 0, slot, device
                    )
                )
                slot += 1
            yield
            for d, copy in enumerate(copies):
                copy.wait_recv()
                value = value + small_land[at + 1 + d]
        small_out[...] = value

    running = [stages(item) for item in items] + [small_stages()]
    waiting = list(running)
    active = []
    while waiting or active:
        if waiting:
            active.append(waiting.pop(0))
        for stage in list(active):
            try:
                next(stage)
            except StopIteration:
                active.remove(stage)
    for copy in started:
        copy.wait_send()


def sum_gradients(own, other, small_own, small_other, dp_size, collective_id):
    count = len(own)
    rows, cols = own[0].shape
    groups = dp_size // (2 * LINES)
    items = plan_items(count, cols)
    landing = []
    for item in items:
        sizes = reduce_rows(item.order, rows)
        landing.append(pltpu.VMEM((rows, item.cols), BF16))
        for axis, size in zip(item.order, sizes):
            slots = LINES - 1 if axis == "z" else 1
            landing.append(pltpu.VMEM((slots, size, item.cols), BF16))
        landing.append(pltpu.VMEM((max(groups - 1, 1), sizes[-1], item.cols), BF16))
    slots = 3 + (LINES - 1) + (groups - 1) + 2 + (LINES - 1) + 1
    small_slots = 1 + 2 + 2 + LINES + groups
    vmem = pl.BlockSpec(memory_space=pltpu.VMEM)
    return pl.pallas_call(
        functools.partial(sum_kernel, count, groups, items),
        out_shape=[jax.ShapeDtypeStruct((rows, cols), BF16)] * count
        + [jax.ShapeDtypeStruct(small_own.shape, F32)],
        in_specs=[vmem] * count + [pl.BlockSpec(memory_space=pl.ANY)] * count + [vmem] * 2,
        out_specs=[vmem] * (count + 1),
        scratch_shapes=[pltpu.VMEM((rows, cols), BF16)] * count
        + landing
        + [
            pltpu.VMEM((small_slots, *small_own.shape), F32),
            pltpu.SemaphoreType.DMA((len(items), slots)),
            pltpu.SemaphoreType.DMA((len(items), slots)),
            pltpu.SemaphoreType.DMA((1, small_slots)),
            pltpu.SemaphoreType.DMA((1, small_slots)),
        ],
        compiler_params=pltpu.CompilerParams(
            collective_id=collective_id, has_side_effects=True, vmem_limit_bytes=60 * MIB
        ),
        name="sum_gradients",
    )(*own, *other, small_own, small_other)


def on_device(
    layer_in, segments, block_perm, w_query, b_query, w_key, w_value, b_value, w_attn_out,
    b_attn_out, norm1_gain, norm1_bias, w_up, b_up, w_down, b_down, norm2_gain, norm2_bias,
    grad_out,
):
    seq_count, block_len, half = layer_in.shape
    width = w_query.shape[0]
    local_heads = block_perm.shape[0]
    heads = 2 * local_heads
    head_cols = w_query.shape[1]
    head_width = head_cols // local_heads
    seqs = seq_count // 2
    rows = seqs * block_len
    scale = head_width ** (-0.5)
    head = lax.axis_index("head")
    my_block = lax.axis_index("blk")
    first = head == 0
    dp_size = lax.axis_size("dp")

    def swap(array):
        return lax.ppermute(array, "head", [(0, 1), (1, 0)])

    def cross(array):
        return lax.ppermute(array, "blk", [(0, 1), (1, 0)])

    def joined(mine, received, axis=-1):
        return jnp.where(
            first,
            jnp.concatenate([mine, received], axis=axis),
            jnp.concatenate([received, mine], axis=axis),
        )

    def to_tokens(array):
        mine = lax.dynamic_slice_in_dim(array, head * seqs, seqs, 0)
        theirs = lax.dynamic_slice_in_dim(array, (1 - head) * seqs, seqs, 0)
        return joined(mine, swap(theirs)).reshape(rows, width)

    def to_features(array):
        array = array.reshape(seqs, block_len, width)
        mine = lax.dynamic_slice_in_dim(array, head * half, half, 2)
        theirs = lax.dynamic_slice_in_dim(array, (1 - head) * half, half, 2)
        return joined(mine, swap(theirs), 0)

    x = to_tokens(layer_in)
    x_cross = jnp.concatenate(
        [cross(x[s * block_len : (s + 1) * block_len]) for s in range(seqs)]
    )
    model_vecs = [b_attn_out, norm1_gain, norm1_bias, b_down, norm2_gain, norm2_bias]
    packed = jnp.concatenate(
        [*model_vecs, b_query, b_value, b_up, block_perm.astype(F32).reshape(-1)]
    )
    packed_other = swap(packed)

    def unpack(array):
        vecs = array[: 8 * half].reshape(8, half)
        ups = array[8 * half : 8 * half + b_up.shape[0]]
        perm = array[8 * half + b_up.shape[0] :].reshape(block_perm.shape)
        return vecs, ups, perm

    vecs_own, up_own, perm_own = unpack(packed)
    vecs_other, up_other, perm_other = unpack(packed_other)
    vectors = joined(vecs_own, vecs_other)
    b_up_all = jnp.concatenate([up_own, up_other])[None, :]
    b_heads = jnp.concatenate([vecs_own[6:8], vecs_other[6:8]], axis=1)

    perm = jnp.concatenate([perm_own, perm_other], axis=0)
    columns = jnp.arange(perm.shape[1])
    reads = jnp.sum(jnp.where(columns[None, :] == my_block, perm, 0.0), axis=1)
    crossed = (reads != my_block.astype(F32)).astype(jnp.int32)
    before = jnp.cumsum(crossed) - crossed
    place = jnp.where(crossed == 1, heads // 2 + before, jnp.arange(heads) - before)
    feature = jnp.arange(heads * head_width)
    target = jnp.repeat(place, head_width) * head_width + feature % head_width
    sorter = (target[:, None] == feature[None, :]).astype(BF16)

    def sort_cols(own, other):
        return dot(jnp.concatenate([own, other], axis=1), sorter).astype(BF16)

    wq = sort_cols(w_query, swap(w_query))
    wk = sort_cols(w_key, swap(w_key))
    wv = sort_cols(w_value, swap(w_value))
    wo = dot(sorter, jnp.concatenate([w_attn_out, swap(w_attn_out)], axis=0), 0, 0).astype(BF16)
    b_sorted = jnp.sum(b_heads[:, :, None] * sorter.astype(F32)[None], axis=1)
    bq, bv = b_sorted[0], b_sorted[1]
    w_up_pair = (w_up, swap(w_up))
    w_down_pair = (w_down, swap(w_down))

    same = heads // 2 * head_width
    queries = ((dot(x, wq) + bq) * scale).astype(BF16)
    keys_same = dot(x, wk[:, :same]).astype(BF16)
    values_same = (dot(x, wv[:, :same]) + bv[:same]).astype(BF16)

    my_segments = lax.dynamic_slice_in_dim(segments, head * seqs, seqs, 0)
    own_seg = lax.dynamic_slice_in_dim(my_segments, my_block * block_len, block_len, 1)
    cross_seg = lax.dynamic_slice_in_dim(my_segments, (1 - my_block) * block_len, block_len, 1)
    ctx_same, log_same = attend(
        queries, 0, keys_same, values_same, own_seg, own_seg, head_width
    )
    keys_cross = dot(x_cross, wk[:, same:]).astype(BF16)
    values_cross = (dot(x_cross, wv[:, same:]) + bv[same:]).astype(BF16)
    pairs = same // (2 * head_width)
    ctx_cross, log_cross = attend(
        queries, pairs, keys_cross, values_cross, own_seg, cross_seg, head_width
    )

    grad_rows = to_tokens(grad_out)
    (
        out_rows, act0, act1, gup0, gup1, normed, grad_ffn, grad_attn, grad_attn_low, grad_ctx,
        grad_vecs, grad_bup,
    ) = middle(
        ctx_same, ctx_cross, x, grad_rows, vectors, b_up_all, wo, w_up_pair, w_down_pair
    )
    layer_out = to_features(out_rows)

    def weight(left, right):
        return dot(left, right, 0, 0).astype(BF16)

    def down_grad(act):
        middle_col = act.shape[1] // 2
        return jnp.concatenate(
            [weight(act[:, :middle_col], grad_ffn), weight(act[:, middle_col:], grad_ffn)], axis=1
        )

    gup_own, gup_other = weight(normed, gup0), weight(normed, gup1)
    gdn_own, gdn_other = down_grad(act0), down_grad(act1)

    dq_cross, dk_cross, dv_cross = attend_back(
        queries, pairs, keys_cross, values_cross, grad_ctx, log_cross, own_seg, cross_seg,
        head_width, scale,
    )
    back_cross = (dot(dk_cross, wk[:, same:], 1, 1) + dot(dv_cross, wv[:, same:], 1, 1)).astype(
        BF16
    )
    returned = cross(back_cross)
    dq_same, dk_same, dv_same = attend_back(
        queries, 0, keys_same, values_same, grad_ctx, log_same, own_seg, own_seg, head_width, scale
    )

    grad_sorted = jnp.concatenate(
        [
            jnp.concatenate([weight(x, dq_same), weight(x, dq_cross)], axis=1),
            jnp.concatenate([weight(x, dk_same), weight(x_cross, dk_cross)], axis=1),
            jnp.concatenate([weight(x, dv_same), weight(x_cross, dv_cross)], axis=1),
        ],
        axis=0,
    )
    grad_natural = dot(grad_sorted, sorter, 1, 1).astype(BF16).reshape(3, width, 2, head_cols)
    grad_wo = jnp.concatenate(
        [weight(ctx_same, grad_attn_low), weight(ctx_cross, grad_attn_low)], axis=0
    )
    grad_wo = dot(sorter, grad_wo).astype(BF16).reshape(2, head_cols, 2, width // 2)

    def heads_part(at):
        out_rows_part = grad_wo[at].transpose(1, 0, 2).reshape(2 * head_cols, width // 2)
        return jnp.concatenate([*(grad_natural[i, :, at] for i in range(3)), out_rows_part], axis=1)

    dq = jnp.concatenate([dq_same, dq_cross], axis=1).astype(F32)
    dv = jnp.concatenate([dv_same, dv_cross], axis=1).astype(F32)
    grad_bq = jnp.sum(sorter.astype(F32) * jnp.sum(dq, axis=0)[None, :], axis=1)
    grad_bv = jnp.sum(sorter.astype(F32) * jnp.sum(dv, axis=0)[None, :], axis=1)
    up_cols = b_up.shape[0]

    def small_part(at, mine):
        vec_part = lax.dynamic_slice_in_dim(
            grad_vecs[:6], (head if mine else 1 - head) * half, half, 1
        )
        flat = jnp.concatenate(
            [
                vec_part.reshape(-1),
                grad_bq[at * head_cols : (at + 1) * head_cols],
                grad_bv[at * head_cols : (at + 1) * head_cols],
                grad_bup[0, at * up_cols : (at + 1) * up_cols],
            ]
        )
        return jnp.pad(flat, (0, 8 * up_cols - flat.shape[0])).reshape(8, up_cols)

    total_up, total_down, total_heads, small = sum_gradients(
        [gup_own, gdn_own, heads_part(0)],
        [gup_other, gdn_other, heads_part(1)],
        small_part(0, True),
        small_part(1, False),
        dp_size,
        1,
    )
    grad_in_rows = (
        grad_attn
        + dot(dq_same, wq[:, :same], 1, 1)
        + dot(dq_cross, wq[:, same:], 1, 1)
        + dot(dk_same, wk[:, :same], 1, 1)
        + dot(dv_same, wv[:, :same], 1, 1)
        + returned.astype(F32)
    )
    grad_in = to_features(grad_in_rows)

    small = small.reshape(-1)
    vec_totals = small[: 8 * half].reshape(8, half)
    heads_total = total_heads.astype(F32)
    down_total = total_down.astype(F32)
    out_total = heads_total[:, 3 * head_cols :]
    grad_w_attn_out = jnp.concatenate([out_total[:head_cols], out_total[head_cols:]], axis=1)
    grad_w_down = jnp.concatenate([down_total[:, :width], down_total[:, width:]], axis=0)
    return (
        layer_out,
        grad_in,
        heads_total[:, :head_cols],
        vec_totals[6],
        heads_total[:, head_cols : 2 * head_cols],
        heads_total[:, 2 * head_cols : 3 * head_cols],
        vec_totals[7],
        grad_w_attn_out,
        vec_totals[0],
        vec_totals[1],
        vec_totals[2],
        total_up.astype(F32),
        small[8 * half : 8 * half + up_cols],
        grad_w_down,
        vec_totals[3],
        vec_totals[4],
        vec_totals[5],
    )


def solution(mesh):
    rows, cols, vec = P("head", None), P(None, "head"), P("head")
    tokens = P("dp", "blk", "head")
    return jax.shard_map(
        on_device,
        mesh=mesh,
        in_specs=(
            tokens, P("dp", None), rows, cols, vec, cols, cols, vec, rows, vec, vec, vec, cols,
            vec, rows, vec, vec, vec, tokens,
        ),
        out_specs=(
            tokens, tokens, cols, vec, cols, cols, vec, rows, vec, vec, vec, cols, vec, rows, vec,
            vec, vec,
        ),
        check_vma=False,
    )
```

```python
import functools

import jax
import jax.numpy as jnp
from jax import lax
from jax.experimental import pallas as pl
from jax.experimental.pallas import tpu as pltpu
from jax.sharding import PartitionSpec as P

EPSILON = 1e-05
NEGATIVE = -1e30
ROOT_HALF = 0.7071067811865476
DENSITY_SCALE = 0.3989422804014327
F32 = jnp.float32
BF16 = jnp.bfloat16
MIB = 1 << 20


def dot(left, right, left_dim=1, right_dim=0):
    return lax.dot_general(
        left, right, (((left_dim,), (right_dim,)), ((), ())), preferred_element_type=F32
    )


def fill_bias(bias_ref, query_seg, keys_seg):
    same = keys_seg == query_seg
    covered = jnp.max(jnp.where(same, 1.0, 0.0), axis=0, keepdims=True)
    bias_ref[...] = jnp.where(same, 0.0, covered * NEGATIVE)


def attend_kernel(head_width, q_ref, k_ref, v_ref, qseg_ref, kseg_ref, ctx_ref, lse_ref, bias_ref):
    @pl.when(pl.program_id(1) == 0)
    def _():
        fill_bias(bias_ref, qseg_ref[0], kseg_ref[...])

    queries, keys = q_ref[...], k_ref[...]
    pair_width = queries.shape[1]
    value_cols = v_ref[...].astype(F32).T.astype(BF16)
    lane = lax.broadcasted_iota(jnp.int32, (1, pair_width), 1)
    parts, logs = [], []
    for low in range(0, pair_width, head_width):
        chosen = jnp.logical_and(lane >= low, lane < low + head_width)
        scores = dot(keys, jnp.where(chosen, queries, 0), 1, 1) + bias_ref[...]
        top = jnp.max(scores, axis=0, keepdims=True)
        shifted = jnp.exp(scores - top)
        total = jnp.sum(shifted, axis=0, keepdims=True)
        context = dot(value_cols[low : low + head_width], shifted.astype(BF16))
        parts.append(context * (1.0 / total))
        logs.append(top + jnp.log(total))
    ctx_ref[...] = jnp.concatenate(parts, axis=0).T.astype(BF16)
    lse_ref[0, 0] = jnp.concatenate(logs, axis=0)


def attend(queries, first_pair, keys, values, query_seg, keys_seg, head_width):
    seq_count, block_len = query_seg.shape
    pair = 2 * head_width
    pairs = keys.shape[1] // pair
    spec = pl.BlockSpec((block_len, pair), lambda s, p: (s, p))
    return pl.pallas_call(
        functools.partial(attend_kernel, head_width),
        grid=(seq_count, pairs),
        in_specs=[
            pl.BlockSpec((block_len, pair), lambda s, p: (s, p + first_pair)),
            spec,
            spec,
            pl.BlockSpec((1, 1, block_len), lambda s, p: (s, 0, 0)),
            pl.BlockSpec((block_len, 1), lambda s, p: (s, 0)),
        ],
        out_specs=[spec, pl.BlockSpec((1, 1, 2, block_len), lambda s, p: (s, p, 0, 0))],
        out_shape=[
            jax.ShapeDtypeStruct(keys.shape, BF16),
            jax.ShapeDtypeStruct((seq_count, pairs, 2, block_len), F32),
        ],
        scratch_shapes=[pltpu.VMEM((block_len, block_len), F32)],
        compiler_params=pltpu.CompilerParams(vmem_limit_bytes=48 * MIB),
        name="attend",
    )(queries, keys, values, query_seg[:, None, :], keys_seg.reshape(-1, 1))


def unit_rows(rows, width):
    mean = jnp.sum(rows, axis=1, keepdims=True) * (1.0 / width)
    centered = rows - mean
    variance = jnp.sum(centered * centered, axis=1, keepdims=True) * (1.0 / width)
    inverse = lax.rsqrt(variance + EPSILON)
    return centered * inverse, inverse


def unit_back(grad, unit, inverse, gain, width):
    scaled = grad * gain
    plain = jnp.sum(scaled, axis=1, keepdims=True) * (1.0 / width)
    along = jnp.sum(scaled * unit, axis=1, keepdims=True) * (1.0 / width)
    return (scaled - plain - unit * along) * inverse


def middle_kernel(
    chunk, ctxu_ref, ctxc_ref, x_ref, gout_ref, vec_ref, bup_ref, wo_ref,
    wup0_ref, wup1_ref, wdn0_ref, wdn1_ref,
    out_ref, act0_ref, act1_ref, gup0_ref, gup1_ref, normed_ref, gffn_ref, gattn_ref, gattnb_ref,
    gctx_ref, gvec_ref, gbup_ref, slope_ref,
):
    width = x_ref.shape[1]
    half = ctxu_ref.shape[1]
    part = wup0_ref.shape[1]

    @pl.when(pl.program_id(0) == 0)
    def _():
        gvec_ref[...] = jnp.zeros_like(gvec_ref)
        gbup_ref[...] = jnp.zeros_like(gbup_ref)

    def vec(i):
        return vec_ref[i : i + 1, :]

    def add_vec(i, rows):
        gvec_ref[i : i + 1, :] += jnp.sum(rows, axis=0, keepdims=True)

    attended = dot(ctxu_ref[...], wo_ref[:half]) + dot(ctxc_ref[...], wo_ref[half:])
    unit1, inverse1 = unit_rows(x_ref[...].astype(F32) + attended + vec(0), width)
    normed = unit1 * vec(1) + vec(2)
    normed_low = normed.astype(BF16)
    normed_ref[...] = normed_low
    pieces = ((wup0_ref, wdn0_ref, act0_ref, gup0_ref), (wup1_ref, wdn1_ref, act1_ref, gup1_ref))
    down = jnp.zeros_like(normed)
    for at, (wup, wdn, act_ref, _) in enumerate(pieces):
        for low in range(0, part, chunk):
            cols = slice(at * part + low, at * part + low + chunk)
            up = dot(normed_low, wup[:, low : low + chunk]) + bup_ref[:, cols]
            cumulative = 0.5 + 0.5 * lax.erf(up * ROOT_HALF)
            slope_ref[:, cols] = cumulative + up * (jnp.exp(-0.5 * up * up) * DENSITY_SCALE)
            activated = (up * cumulative).astype(BF16)
            act_ref[:, low : low + chunk] = activated
            down += dot(activated, wdn[low : low + chunk, :])
    unit2, inverse2 = unit_rows(normed + down + vec(3), width)
    out_ref[...] = unit2 * vec(4) + vec(5)
    grad_out = gout_ref[...]
    add_vec(4, grad_out * unit2)
    add_vec(5, grad_out)
    grad_ffn = unit_back(grad_out, unit2, inverse2, vec(4), width)
    add_vec(3, grad_ffn)
    grad_ffn_low = grad_ffn.astype(BF16)
    gffn_ref[...] = grad_ffn_low
    back = jnp.zeros_like(normed)
    for at, (wup, wdn, _, gup_ref) in enumerate(pieces):
        for low in range(0, part, chunk):
            cols = slice(at * part + low, at * part + low + chunk)
            grad_act = dot(grad_ffn_low, wdn[low : low + chunk, :], 1, 1)
            grad_up = (grad_act * slope_ref[:, cols]).astype(BF16)
            gup_ref[:, low : low + chunk] = grad_up
            gbup_ref[0:1, cols] += jnp.sum(grad_up.astype(F32), axis=0, keepdims=True)
            back += dot(grad_up, wup[:, low : low + chunk], 1, 1)
    grad_mid = grad_ffn + back
    add_vec(1, grad_mid * unit1)
    add_vec(2, grad_mid)
    grad_attn = unit_back(grad_mid, unit1, inverse1, vec(1), width)
    add_vec(0, grad_attn)
    gattn_ref[...] = grad_attn
    grad_attn_low = grad_attn.astype(BF16)
    gattnb_ref[...] = grad_attn_low
    gctx_ref[...] = dot(grad_attn_low, wo_ref[...], 1, 1).astype(BF16)


def middle(ctx_same, ctx_cross, x, grad_out, vectors, b_up, w_out, w_up, w_down):
    rows, width = x.shape
    half = ctx_same.shape[1]
    part = w_up[0].shape[1]
    tile = 256
    chunk = part // 2

    def tiles(cols):
        return pl.BlockSpec((tile, cols), lambda i: (i, 0))

    def whole(array):
        return pl.BlockSpec(array.shape, lambda i: (0, 0), pipeline_mode=pl.Buffered(1))

    def shape(cols, kind):
        return jax.ShapeDtypeStruct((rows, cols), kind)

    outs = [
        (width, F32), (part, BF16), (part, BF16), (part, BF16), (part, BF16),
        (width, BF16), (width, BF16), (width, F32), (width, BF16), (width, BF16),
    ]
    sums = [jax.ShapeDtypeStruct((8, width), F32), jax.ShapeDtypeStruct((8, b_up.shape[1]), F32)]
    weights = [vectors, b_up, w_out, *w_up, *w_down]
    return pl.pallas_call(
        functools.partial(middle_kernel, chunk),
        grid=(rows // tile,),
        in_specs=[tiles(half), tiles(half), tiles(width), tiles(width)] + [whole(w) for w in weights],
        out_specs=[tiles(c) for c, _ in outs]
        + [pl.BlockSpec(s.shape, lambda i: (0, 0)) for s in sums],
        out_shape=[shape(c, k) for c, k in outs] + sums,
        scratch_shapes=[pltpu.VMEM((tile, 2 * part), F32)],
        compiler_params=pltpu.CompilerParams(vmem_limit_bytes=60 * MIB),
        name="middle",
    )(ctx_same, ctx_cross, x, grad_out, *weights)


LINES = 4
RATES = {"head": 500e3, "x": 46e3, "y": 46e3, "z": 46e3, "group": 46e3}
DELAY = 4.0
ORDERS = {"A": ("x", "y", "z"), "B": ("y", "x", "z"), "C": ("z", "x", "y")}


class Item:
    def __init__(self, at, array, first, cols, rows, order, groups, stages):
        self.at, self.array, self.first, self.cols, self.rows = at, array, first, cols, rows
        self.groups = groups
        self.sums, self.results = [], []
        size = rows
        for axis in ORDERS[order] + (("group",) if groups > 1 else ()):
            before = size
            size = size // {"x": 2, "y": 2, "z": LINES, "group": 1}[axis]
            self.sums.append((axis, before, size))
        self.size = size
        self.results = [s for s in reversed(self.sums) if s[0] != "group"]
        self.stages = []
        if "head" in stages:
            self.stages.append(("head", "head", rows, rows))
        if "sum" in stages:
            self.stages += [("sum", *s) for s in self.sums]
        if "result" in stages:
            self.stages += [("result", *s) for s in self.results]

    def load(self, stage):
        kind, axis, before, size = self.stages[stage]
        moved = before if axis in ("head", "z") else size * (self.groups if axis == "group" else 1)
        return axis, moved * self.cols * 2


def plan(items, steps, ready):
    free = {axis: 0.0 for axis in RATES}
    due = [[at, 0] for at in ready]
    batches = []
    now = 0.0

    def run(index, batch):
        nonlocal now
        item, (_, stage) = items[index], due[index]
        batch.append((index, stage))
        now += 0.4
        if stage == len(item.stages):
            due[index] = None
            return
        axis, size = item.load(stage)
        start = max(free[axis], now)
        free[axis] = start + size / RATES[axis]
        due[index] = [free[axis] + DELAY, stage + 1]

    for time in [0.0] + steps:
        now += time
        batch = []
        while True:
            able = [i for i, d in enumerate(due) if d is not None and d[0] <= now]
            if not able:
                break
            run(min(able, key=lambda i: (due[i][0], -due[i][1])), batch)
        batches.append(batch)
    batch = []
    while any(d is not None for d in due):
        able = [i for i, d in enumerate(due) if d is not None]
        first = min(able, key=lambda i: (due[i][0], -due[i][1]))
        now = max(now, due[first][0])
        run(first, batch)
    batches.append(batch)
    return batches


class Places:
    def __init__(self, groups):
        head, blk, dp = lax.axis_index("head"), lax.axis_index("blk"), lax.axis_index("dp")
        low, line, group = dp % 2, (dp // 2) % LINES, dp // (2 * LINES)
        self.head, self.line = head, line
        self.bit = {"x": blk, "y": low}
        base = group * (2 * LINES) + low
        self.partners = {
            "head": [{"head": 1 - head}],
            "x": [{"blk": 1 - blk}],
            "y": [{"dp": dp + 1 - 2 * low}],
            "z": [{"dp": base + ((line + d) % LINES) * 2} for d in range(1, LINES)],
            "group": [
                {"dp": ((group + d) % groups) * (2 * LINES) + line * 2 + low}
                for d in range(1, groups)
            ],
        }

    def greet(self):
        barrier = pltpu.get_barrier_semaphore()
        everyone = [device for devices in self.partners.values() for device in devices]
        for device in everyone:
            pl.semaphore_signal(
                barrier, inc=1, device_id=device, device_id_type=pl.DeviceIdType.MESH
            )
        pl.semaphore_wait(barrier, len(everyone))


def remote(source, target, send, recv, device):
    return pltpu.make_async_remote_copy(
        src_ref=source,
        dst_ref=target,
        send_sem=send,
        recv_sem=recv,
        device_id=device,
        device_id_type=pl.DeviceIdType.MESH,
    )


def slot_count(groups):
    return 3 + 2 * (LINES - 1) + 2 + groups - 1


class Sums:
    def __init__(self, items, places, own, other, total, result, piece, landing, send, recv):
        self.items, self.places = items, places
        self.own, self.other, self.total, self.result = own, other, total, result
        self.piece, self.landing, self.send, self.recv = piece, landing, send, recv
        self.copies = {}
        self.sent = []

    def range_of(self, item, kind, axis):
        start, size = 0, item.rows
        for name, before, after in item.sums:
            if kind == "sum" and name == axis:
                return start, before, after
            if name == "z":
                start = start + self.places.line * after
            elif name != "group":
                start = start + self.places.bit[name] * after
        return start, None, None

    def part(self, ref, start, size, item):
        return ref.at[
            pl.ds(pl.multiple_of(start, 16), size), item.first : item.first + item.cols
        ]

    def copies_of(self, item, stage):
        kind, axis, before, after = item.stages[stage]
        devices = self.places.partners[axis]
        out = []

        def add(source, target, slot, device):
            out.append(
                remote(
                    source, target, self.send.at[item.at, slot], self.recv.at[item.at, slot], device
                )
            )

        if kind == "head":
            source = self.other[item.array].at[:, item.first : item.first + item.cols]
            add(source, self.landing[item.at]["head"], 0, devices[0])
            return out
        if kind == "sum":
            start, _, _ = self.range_of(item, kind, axis)
            ref = self.total[item.array]
            buf = self.landing[item.at][axis]
            for d, device in enumerate(devices):
                if axis == "z":
                    row = start + ((self.places.line + d + 1) % LINES) * after
                elif axis == "group":
                    row = start
                else:
                    row = start + (1 - self.places.bit[axis]) * after
                slot = {"x": 1, "y": 2, "z": 3, "group": 3 + 2 * (LINES - 1) + 2}[axis] + d
                add(self.part(ref, row, after, item), buf.at[d], slot, device)
            return out
        start, size = self.held(item, stage)
        here = self.part(self.result[item.array], start, size, item)
        for d, device in enumerate(devices):
            slot = 3 + (LINES - 1) + {"x": 0, "y": 1, "z": 2}[axis] + d
            add(here, here, slot, device)
        return out

    def held(self, item, stage):
        start, _, _ = self.range_of(item, "result", None)
        size = item.size
        for kind, axis, before, after in item.stages[:stage]:
            if kind == "result":
                start, _, _ = self.range_of(item, "sum", axis)
                size = before
        return start, size

    def op(self, index, stage):
        item = self.items[index]
        if stage > 0:
            kind, axis, before, after = item.stages[stage - 1]
            copies = self.copies_of(item, stage - 1)
            for copy in copies:
                copy.wait_recv()
            if kind == "head":
                cols = slice(item.first, item.first + item.cols)
                self.total[item.array][:, cols] = (
                    self.own[item.array][:, cols].astype(F32)
                    + self.landing[item.at]["head"][...].astype(F32)
                ).astype(BF16)
            elif kind == "sum":
                start, _, _ = self.range_of(item, kind, axis)
                if axis == "z":
                    start = start + self.places.line * after
                elif axis != "group":
                    start = start + self.places.bit[axis] * after
                here = self.part(self.total[item.array], start, after, item)
                value = here[...].astype(F32)
                for d in range(len(copies)):
                    value = value + self.landing[item.at][axis][d].astype(F32)
                last = stage == len(item.stages) or item.stages[stage][0] == "result"
                if not last:
                    here[...] = value.astype(BF16)
                elif self.piece[item.array] is not None:
                    self.piece[item.array][:, item.first : item.first + item.cols] = value.astype(
                        BF16
                    )
                else:
                    self.part(self.result[item.array], start, after, item)[...] = value.astype(BF16)
        elif item.stages[0][0] == "result":
            start, size = self.held(item, 0)
            self.part(self.result[item.array], start, size, item)[...] = self.piece[item.array][
                :, item.first : item.first + item.cols
            ]
        if stage < len(item.stages):
            for copy in self.copies_of(item, stage):
                copy.start()
            self.sent.append((item, stage))

    def finish(self):
        for item, stage in self.sent:
            for copy in self.copies_of(item, stage):
                copy.wait_send()


def landing_shapes(items):
    shapes = []
    for item in items:
        for kind, axis, before, after in item.stages:
            if kind == "head":
                shapes.append((item.at, "head", (item.rows, item.cols)))
            elif kind == "sum":
                slots = {"x": 1, "y": 1, "z": LINES - 1, "group": item.groups - 1}[axis]
                shapes.append((item.at, axis, (slots, after, item.cols)))
    return shapes


def make_items(arrays, rows, cols, step, orders, groups, stages, at=0):
    items = []
    for index in range(len(orders)):
        array, first = divmod(index * step, cols)
        items.append(
            Item(at + index, arrays[array], first, step, rows, orders[index], groups, stages)
        )
    return items


def run_batch(sums, batch):
    for index, stage in batch:
        sums.op(index, stage)


def back_kernel(
    plan_parts, head_width, scale, own_up, own_down, other_up, other_down, q_ref, k_ref, v_ref,
    g_ref, lse_ref, qseg_ref, kseg_ref, x_ref, xc_ref, ctx_ref, gattn_ref, gattnb_ref, wq_ref,
    wk_ref, wv_ref, sorter_ref,
    piece_up, piece_down, heads_own, heads_other, dx_ref, dxc_ref, bsum_ref,
    total_up, total_down, send, recv, dq_ref, dk_ref, dv_ref, bias_ref, gwo_ref, *landing_refs,
):
    items, batches, groups = plan_parts
    places = Places(groups)
    places.greet()
    landing = {}
    for (at, axis, _), ref in zip(landing_shapes(items), landing_refs):
        landing.setdefault(at, {})[axis] = ref
    sums = Sums(
        items, places, [own_up, own_down], [other_up, other_down], [total_up, total_down], None,
        [piece_up, piece_down], landing, send, recv,
    )
    rows, width = x_ref.shape
    seqs, _, block_len = qseg_ref.shape
    pair_width = 2 * head_width
    pairs = width // pair_width
    same = width // 2
    batches = list(batches)
    run_batch(sums, batches.pop(0))

    def steps(count, body):
        @pl.loop(0, count)
        def _(step):
            body(step)
            for at in range(count):
                if batches[at]:
                    @pl.when(step == at)
                    def _():
                        run_batch(sums, batches[at])

        del batches[:count]

    def attention(step):
        crossed = 1 - step // (pairs // 2 * seqs)
        seq = (step // (pairs // 2)) % seqs
        pair = crossed * (pairs // 2) + step % (pairs // 2)
        here = pl.ds(pl.multiple_of(seq * block_len, block_len), block_len)
        cols = pl.ds(pl.multiple_of(pair * pair_width, pair_width), pair_width)

        @pl.when(step % (pairs // 2) == 0)
        def _():
            fill_bias(bias_ref, qseg_ref[seq], kseg_ref[crossed, here, :])

        queries, keys = q_ref[here, cols], k_ref[here, cols]
        values, grads = v_ref[here, cols], g_ref[here, cols]
        logs = lse_ref[seq, pair]
        key_cols = keys.astype(F32).T.astype(BF16)
        lane = lax.broadcasted_iota(jnp.int32, (1, pair_width), 1)
        query_parts = []
        for at, low in enumerate(range(0, pair_width, head_width)):
            chosen = jnp.logical_and(lane >= low, lane < low + head_width)
            scores = dot(keys, jnp.where(chosen, queries, 0), 1, 1) + bias_ref[...]
            mixing = jnp.exp(scores - logs[at : at + 1, :])
            grad_mixing = dot(values, jnp.where(chosen, grads, 0), 1, 1)
            inner = jnp.sum(mixing * grad_mixing, axis=0, keepdims=True)
            grad_scores = (mixing * (grad_mixing - inner)).astype(BF16)
            grad_value = dot(mixing.astype(BF16), grads)
            grad_key = dot(grad_scores, queries)
            query_parts.append(dot(key_cols[low : low + head_width], grad_scores))
            if at == 0:
                all_value, all_key = grad_value, grad_key
            else:
                all_value = jnp.where(chosen, grad_value, all_value)
                all_key = jnp.where(chosen, grad_key, all_key)
        dq_ref[here, cols] = (jnp.concatenate(query_parts, axis=0).T.astype(BF16) * scale).astype(
            BF16
        )
        dk_ref[here, cols] = all_key.astype(BF16)
        dv_ref[here, cols] = all_value.astype(BF16)

    steps(seqs * pairs, attention)
    tile = 256
    sorter = sorter_ref[...]

    def tile_of(step):
        return pl.ds(pl.multiple_of(step * tile, tile), tile)

    def weights(step):
        mine = tile_of(step)
        left, left_cross = x_ref[:, mine].T, xc_ref[:, mine].T
        for at, ref in enumerate((dq_ref, dk_ref, dv_ref)):
            first = dot(left, ref[:, :same])
            second = dot(left if at == 0 else left_cross, ref[:, same:])
            found = jnp.concatenate([first, second], axis=1).astype(BF16)
            natural = dot(found, sorter, 1, 1).astype(BF16)
            heads_own[mine, at * same : (at + 1) * same] = natural[:, :same]
            heads_other[mine, at * same : (at + 1) * same] = natural[:, same:]
        gwo_ref[mine, :] = dot(ctx_ref[:, mine].T, gattnb_ref[...]).astype(BF16)

    steps(width // tile, weights)

    def last_weight(_):
        for ref, low in ((heads_own, 0), (heads_other, same)):
            natural = dot(sorter[low : low + same], gwo_ref[...]).astype(BF16)
            ref[:same, 3 * same :] = natural[:, :same]
            ref[same:, 3 * same :] = natural[:, same:]
        totals = []
        for ref in (dq_ref, dv_ref):
            totals.append(jnp.sum(ref[...].astype(F32), axis=0, keepdims=True))
        found = jnp.concatenate(totals + [jnp.zeros((6, width), F32)], axis=0)
        high = found.astype(BF16)
        rest = found - high.astype(F32)
        middle_part = rest.astype(BF16)
        rest = rest - middle_part.astype(F32)
        bsum_ref[...] = (
            dot(high, sorter, 1, 1)
            + dot(middle_part, sorter, 1, 1)
            + dot(rest.astype(BF16), sorter, 1, 1)
        )

    steps(1, last_weight)

    def inputs(step):
        here = tile_of(step)
        dq, dk, dv = dq_ref[here, :], dk_ref[here, :], dv_ref[here, :]
        dx_ref[here, :] = (
            gattn_ref[here, :]
            + dot(dq, wq_ref[...], 1, 1)
            + dot(dk[:, :same], wk_ref[:, :same], 1, 1)
            + dot(dv[:, :same], wv_ref[:, :same], 1, 1)
        )
        dxc_ref[here, :] = (
            dot(dk[:, same:], wk_ref[:, same:], 1, 1) + dot(dv[:, same:], wv_ref[:, same:], 1, 1)
        ).astype(BF16)

    steps(rows // tile, inputs)
    run_batch(sums, batches.pop(0))
    assert not batches
    sums.finish()


def attention_back(
    own, other, queries, keys, values, grads, logs, query_seg, keys_seg, x, x_cross, ctx, gattn,
    gattn_low, weights, sorter, head_width, scale, groups,
):
    rows, cols = own[0].shape
    width = x.shape[1]
    seqs, block_len = query_seg.shape
    items = make_items([0, 1], rows, cols, cols // 6, "ABABCABABABC", groups, ("head", "sum"))
    pair_steps = seqs * width // (2 * head_width)
    times = [2.3] * pair_steps + [4.0] * (width // 256) + [1.5] + [1.8] * (x.shape[0] // 256)
    batches = plan(items, times, [0.0] * len(items))
    landing = landing_shapes(items)
    vmem = pl.BlockSpec(memory_space=pltpu.VMEM)
    anywhere = pl.BlockSpec(memory_space=pl.ANY)
    size = items[0].size
    return pl.pallas_call(
        functools.partial(back_kernel, (items, batches, groups), head_width, scale),
        in_specs=[vmem] * 2 + [anywhere] * 2 + [vmem] * 16,
        out_specs=[vmem] * 7,
        out_shape=[jax.ShapeDtypeStruct((size, cols), BF16)] * 2
        + [jax.ShapeDtypeStruct((rows, cols), BF16)] * 2
        + [
            jax.ShapeDtypeStruct(x.shape, F32),
            jax.ShapeDtypeStruct(x.shape, BF16),
            jax.ShapeDtypeStruct((8, width), F32),
        ],
        scratch_shapes=[pltpu.VMEM((rows, cols), BF16)] * 2
        + [pltpu.SemaphoreType.DMA((len(items), slot_count(groups)))] * 2
        + [pltpu.VMEM(x.shape, BF16)] * 3
        + [pltpu.VMEM((block_len, block_len), F32), pltpu.VMEM((width, width), BF16)]
        + [pltpu.VMEM(shape, BF16) for _, _, shape in landing],
        compiler_params=pltpu.CompilerParams(
            collective_id=1, has_side_effects=True, vmem_limit_bytes=62 * MIB
        ),
        name="attention_back",
    )(
        *own, *other, queries, keys, values, grads, logs, query_seg[:, None, :],
        keys_seg[:, :, None], x, x_cross, ctx, gattn, gattn_low, *weights, sorter,
    )


def last_kernel(
    plan_parts, piece_up, piece_down, heads_own, heads_other, gvec_ref, gbup_ref, bsum_ref, dx_ref,
    dxc_ref,
    out_up, out_down, out_heads, small_ref, din_ref, din_other,
    total_heads, send, recv, small_land, small_stage, small_send, small_recv, cross_land, half_ref,
    move_send, move_recv, *landing_refs,
):
    items, batches, groups = plan_parts
    places = Places(groups)
    places.greet()
    landing = {}
    for (at, axis, _), ref in zip(landing_shapes(items), landing_refs):
        landing.setdefault(at, {})[axis] = ref
    sums = Sums(
        items, places, {2: heads_own}, {2: heads_other}, {2: total_heads},
        [out_up, out_down, out_heads], [piece_up, piece_down, None], landing, send, recv,
    )
    rows, width = dx_ref.shape
    half = width // 2
    part = gbup_ref.shape[1] // 2
    head = places.head
    moves = 4
    each = rows // moves

    def cross_copy(at):
        return remote(
            dxc_ref.at[at * each : (at + 1) * each], cross_land.at[at * each : (at + 1) * each],
            move_send.at[at], move_recv.at[at], places.partners["x"][0],
        )

    def head_copy(at):
        return remote(
            half_ref.at[at * each : (at + 1) * each], din_other.at[at * each : (at + 1) * each],
            move_send.at[moves + at], move_recv.at[moves + at], places.partners["head"][0],
        )

    def cross_start(at):
        cross_copy(at).start()

    def cross_end(at):
        here = slice(at * each, (at + 1) * each)
        cross_copy(at).wait_recv()
        mine = pl.ds(pl.multiple_of(head * half, half), half)
        theirs = pl.ds(pl.multiple_of((1 - head) * half, half), half)
        half_ref[here, :] = dx_ref[here, theirs] + cross_land[here, theirs].astype(F32)
        head_copy(at).start()
        din_ref[here, :] = dx_ref[here, mine] + cross_land[here, mine].astype(F32)

    def small_copies(stage):
        if stage == 0:
            theirs = pl.ds(pl.multiple_of((1 - head) * half, half), half)
            device = places.partners["head"][0]
            spans = (
                (gvec_ref.at[:, theirs], slice(0, half)),
                (bsum_ref.at[:, half:], slice(half, 2 * half)),
                (gbup_ref.at[:, part:], slice(2 * half, 2 * half + part)),
            )
            return [
                remote(
                    source, small_land.at[at, :, span], small_send.at[at], small_recv.at[at], device
                )
                for at, (source, span) in enumerate(spans)
            ]
        axis = ("x", "y", "z", "group")[stage - 1]
        first = 3 + {"x": 0, "y": 1, "z": 2, "group": 2 + LINES - 1}[axis]
        return [
            remote(small_stage.at[stage], small_land.at[first + d], small_send.at[first + d],
                   small_recv.at[first + d], device)
            for d, device in enumerate(places.partners[axis])
        ]

    small_stages = 4 + (1 if groups > 1 else 0)

    def small_op(stage):
        if stage == 1:
            for copy in small_copies(0):
                copy.wait_recv()
            mine = pl.ds(pl.multiple_of(head * half, half), half)
            small_stage[1, :, :half] = gvec_ref[:, mine] + small_land[0, :, :half]
            small_stage[1, :, half : 2 * half] = (
                bsum_ref[:, :half] + small_land[1, :, half : 2 * half]
            )
            small_stage[1, :, 2 * half :] = gbup_ref[:, :part] + small_land[2, :, 2 * half :]
        elif stage > 1:
            value = small_stage[stage - 1]
            axis = ("x", "y", "z", "group")[stage - 2]
            first = 3 + {"x": 0, "y": 1, "z": 2, "group": 2 + LINES - 1}[axis]
            for d, copy in enumerate(small_copies(stage - 1)):
                copy.wait_recv()
                value = value + small_land[first + d]
            if stage == small_stages:
                small_ref[...] = value
            else:
                small_stage[stage] = value
        if stage < small_stages:
            for copy in small_copies(stage):
                copy.start()

    batch = batches[-1]
    extra = []
    for at in range(moves):
        cross_start(at)
    small_op(0)
    count = len(batch)
    for at in range(1, small_stages + 1):
        extra.append((min(at * 5, count - 1), functools.partial(small_op, at)))
    for at in range(moves):
        extra.append((min(count // 3 + at * count // 12, count - 1), functools.partial(cross_end, at)))
    run_batch(sums, batches[0])
    for at, (index, stage) in enumerate(batch):
        for where, action in extra:
            if where == at:
                action()
        sums.op(index, stage)
    for at in range(moves):
        head_copy(at).wait_recv()
    sums.finish()
    for at in range(moves):
        cross_copy(at).wait_send()
        head_copy(at).wait_send()
    for stage in range(small_stages):
        for copy in small_copies(stage):
            copy.wait_send()


def last_sums(pieces, heads, grad_vecs, grad_bup, bsum, dx, dxc, groups):
    rows, cols = heads[0].shape
    step = cols // 6
    items = make_items([0, 1], rows, cols, step, "ABABCABABABC", groups, ("result",))
    items += make_items(
        [2], rows, cols, step, "ABCABB", groups, ("head", "sum", "result"), len(items)
    )
    ready = [0.0] * len(items)
    batches = plan(items, [], ready)
    landing = landing_shapes(items)
    vmem = pl.BlockSpec(memory_space=pltpu.VMEM)
    small = (8, bsum.shape[1] + cols)
    small_slots = 5 + LINES - 1 + groups - 1
    half = dx.shape[1] // 2
    moves = 8
    return pl.pallas_call(
        functools.partial(last_kernel, (items, batches, groups)),
        in_specs=[vmem] * 3 + [pl.BlockSpec(memory_space=pl.ANY)] + [vmem] * 5,
        out_specs=[vmem] * 6,
        out_shape=[jax.ShapeDtypeStruct((rows, cols), BF16)] * 3
        + [jax.ShapeDtypeStruct(small, F32)]
        + [jax.ShapeDtypeStruct((dx.shape[0], half), F32)] * 2,
        scratch_shapes=[pltpu.VMEM((rows, cols), BF16)]
        + [pltpu.SemaphoreType.DMA((len(items), slot_count(groups)))] * 2
        + [pltpu.VMEM((small_slots, *small), F32), pltpu.VMEM((6, *small), F32)]
        + [pltpu.SemaphoreType.DMA((small_slots,))] * 2
        + [pltpu.VMEM(dxc.shape, BF16), pltpu.VMEM((dx.shape[0], half), F32)]
        + [pltpu.SemaphoreType.DMA((moves,))] * 2
        + [pltpu.VMEM(shape, BF16) for _, _, shape in landing],
        compiler_params=pltpu.CompilerParams(
            collective_id=2, has_side_effects=True, vmem_limit_bytes=62 * MIB
        ),
        name="last_sums",
    )(*pieces, *heads, grad_vecs, grad_bup, bsum, dx, dxc)


def finish_kernel(up_ref, down_ref, heads_ref, gup_ref, gdown_ref, gq_ref, gk_ref, gv_ref, go_ref):
    width = gq_ref.shape[1]
    half = down_ref.shape[1] // 2
    gup_ref[...] = up_ref[...].astype(F32)
    gdown_ref[0] = down_ref[:, :half].astype(F32)
    gdown_ref[1] = down_ref[:, half:].astype(F32)
    for at, ref in enumerate((gq_ref, gk_ref, gv_ref, go_ref)):
        ref[...] = heads_ref[:, at * width : (at + 1) * width].astype(F32)


def finish(up, down, heads):
    rows, cols = up.shape
    tile = 96
    half, quarter = cols // 2, cols // 4
    steps = rows // tile
    spec = pl.BlockSpec((tile, cols), lambda i: (i, 0))
    third = pl.BlockSpec((tile, quarter), lambda i: (i, 0))
    return pl.pallas_call(
        finish_kernel,
        grid=(steps,),
        in_specs=[spec] * 3,
        out_specs=[
            spec,
            pl.BlockSpec((2, tile, half), lambda i: (0, i, 0)),
            third,
            third,
            third,
            pl.BlockSpec((tile, quarter), lambda i: (i % (steps // 2), i // (steps // 2))),
        ],
        out_shape=[
            jax.ShapeDtypeStruct((rows, cols), F32),
            jax.ShapeDtypeStruct((2, rows, half), F32),
            jax.ShapeDtypeStruct((rows, quarter), F32),
            jax.ShapeDtypeStruct((rows, quarter), F32),
            jax.ShapeDtypeStruct((rows, quarter), F32),
            jax.ShapeDtypeStruct((rows // 2, half), F32),
        ],
        compiler_params=pltpu.CompilerParams(vmem_limit_bytes=48 * MIB),
        name="finish",
    )(up, down, heads)


def on_device(
    layer_in, segments, block_perm, w_query, b_query, w_key, w_value, b_value, w_attn_out,
    b_attn_out, norm1_gain, norm1_bias, w_up, b_up, w_down, b_down, norm2_gain, norm2_bias,
    grad_out,
):
    seq_count, block_len, half = layer_in.shape
    width = w_query.shape[0]
    local_heads = block_perm.shape[0]
    heads = 2 * local_heads
    head_cols = w_query.shape[1]
    head_width = head_cols // local_heads
    seqs = seq_count // 2
    rows = seqs * block_len
    scale = head_width ** (-0.5)
    head = lax.axis_index("head")
    my_block = lax.axis_index("blk")
    first = head == 0
    dp_size = lax.axis_size("dp")

    def swap(array):
        return lax.ppermute(array, "head", [(0, 1), (1, 0)])

    def cross(array):
        return lax.ppermute(array, "blk", [(0, 1), (1, 0)])

    def joined(mine, received, axis=-1):
        return jnp.where(
            first,
            jnp.concatenate([mine, received], axis=axis),
            jnp.concatenate([received, mine], axis=axis),
        )

    def to_tokens(array):
        mine = lax.dynamic_slice_in_dim(array, head * seqs, seqs, 0)
        theirs = lax.dynamic_slice_in_dim(array, (1 - head) * seqs, seqs, 0)
        return joined(mine, swap(theirs)).reshape(rows, width)

    def to_features(array):
        array = array.reshape(seqs, block_len, width)
        mine = lax.dynamic_slice_in_dim(array, head * half, half, 2)
        theirs = lax.dynamic_slice_in_dim(array, (1 - head) * half, half, 2)
        return joined(mine, swap(theirs), 0)

    x = to_tokens(layer_in)
    x_cross = jnp.concatenate(
        [cross(x[s * block_len : (s + 1) * block_len]) for s in range(seqs)]
    )
    model_vecs = [b_attn_out, norm1_gain, norm1_bias, b_down, norm2_gain, norm2_bias]
    packed = jnp.concatenate(
        [*model_vecs, b_query, b_value, b_up, block_perm.astype(F32).reshape(-1)]
    )
    packed_other = swap(packed)

    def unpack(array):
        vecs = array[: 8 * half].reshape(8, half)
        ups = array[8 * half : 8 * half + b_up.shape[0]]
        perm = array[8 * half + b_up.shape[0] :].reshape(block_perm.shape)
        return vecs, ups, perm

    vecs_own, up_own, perm_own = unpack(packed)
    vecs_other, up_other, perm_other = unpack(packed_other)
    vectors = joined(vecs_own, vecs_other)
    b_up_all = jnp.concatenate([up_own, up_other])[None, :]
    b_heads = jnp.concatenate([vecs_own[6:8], vecs_other[6:8]], axis=1)

    perm = jnp.concatenate([perm_own, perm_other], axis=0)
    columns = jnp.arange(perm.shape[1])
    reads = jnp.sum(jnp.where(columns[None, :] == my_block, perm, 0.0), axis=1)
    crossed = (reads != my_block.astype(F32)).astype(jnp.int32)
    before = jnp.cumsum(crossed) - crossed
    place = jnp.where(crossed == 1, heads // 2 + before, jnp.arange(heads) - before)
    feature = jnp.arange(heads * head_width)
    target = jnp.repeat(place, head_width) * head_width + feature % head_width
    sorter = (target[:, None] == feature[None, :]).astype(BF16)

    def sort_cols(own, other):
        return dot(jnp.concatenate([own, other], axis=1), sorter).astype(BF16)

    wq = sort_cols(w_query, swap(w_query))
    wk = sort_cols(w_key, swap(w_key))
    wv = sort_cols(w_value, swap(w_value))
    wo = dot(sorter, jnp.concatenate([w_attn_out, swap(w_attn_out)], axis=0), 0, 0).astype(BF16)
    b_sorted = jnp.sum(b_heads[:, :, None] * sorter.astype(F32)[None], axis=1)
    bq, bv = b_sorted[0], b_sorted[1]
    w_up_pair = (w_up, swap(w_up))
    w_down_pair = (w_down, swap(w_down))

    same = heads // 2 * head_width
    queries = ((dot(x, wq) + bq) * scale).astype(BF16)
    keys_same = dot(x, wk[:, :same]).astype(BF16)
    values_same = (dot(x, wv[:, :same]) + bv[:same]).astype(BF16)

    my_segments = lax.dynamic_slice_in_dim(segments, head * seqs, seqs, 0)
    own_seg = lax.dynamic_slice_in_dim(my_segments, my_block * block_len, block_len, 1)
    cross_seg = lax.dynamic_slice_in_dim(my_segments, (1 - my_block) * block_len, block_len, 1)
    ctx_same, log_same = attend(
        queries, 0, keys_same, values_same, own_seg, own_seg, head_width
    )
    keys_cross = dot(x_cross, wk[:, same:]).astype(BF16)
    values_cross = (dot(x_cross, wv[:, same:]) + bv[same:]).astype(BF16)
    pairs = same // (2 * head_width)
    ctx_cross, log_cross = attend(
        queries, pairs, keys_cross, values_cross, own_seg, cross_seg, head_width
    )

    grad_rows = to_tokens(grad_out)
    (
        out_rows, act0, act1, gup0, gup1, normed, grad_ffn, grad_attn, grad_attn_low, grad_ctx,
        grad_vecs, grad_bup,
    ) = middle(
        ctx_same, ctx_cross, x, grad_rows, vectors, b_up_all, wo, w_up_pair, w_down_pair
    )
    layer_out = to_features(out_rows)

    def weight(left, right):
        return dot(left, right, 0, 0).astype(BF16)

    def down_grad(act):
        middle_col = act.shape[1] // 2
        return jnp.concatenate(
            [weight(act[:, :middle_col], grad_ffn), weight(act[:, middle_col:], grad_ffn)], axis=1
        )

    gup_own, gup_other = weight(normed, gup0), weight(normed, gup1)
    gdn_own, gdn_other = down_grad(act0), down_grad(act1)
    groups = dp_size // (2 * LINES)
    piece_up, piece_down, heads_own, heads_other, dx, dxc, bsum = attention_back(
        (gup_own, gdn_own),
        (gup_other, gdn_other),
        queries,
        jnp.concatenate([keys_same, keys_cross], axis=1),
        jnp.concatenate([values_same, values_cross], axis=1),
        grad_ctx,
        jnp.concatenate([log_same, log_cross], axis=1),
        own_seg,
        jnp.stack([own_seg.reshape(-1), cross_seg.reshape(-1)]),
        x,
        x_cross,
        jnp.concatenate([ctx_same, ctx_cross], axis=1),
        grad_attn,
        grad_attn_low,
        (wq, wk, wv),
        sorter,
        head_width,
        scale,
        groups,
    )
    total_up, total_down, total_heads, small, din_mine, din_other = last_sums(
        (piece_up, piece_down), (heads_own, heads_other), grad_vecs, grad_bup, bsum, dx, dxc, groups
    )
    din_mine = din_mine.reshape(seqs, block_len, half)
    din_other = din_other.reshape(seqs, block_len, half)
    grad_in = joined(din_mine, din_other, 0)
    grad_up, grad_down, grad_q, grad_k, grad_v, grad_o = finish(total_up, total_down, total_heads)
    return (
        layer_out,
        grad_in,
        grad_q,
        small[0, half : 2 * half],
        grad_k,
        grad_v,
        small[1, half : 2 * half],
        grad_o,
        small[0, :half],
        small[1, :half],
        small[2, :half],
        grad_up,
        small[0, 2 * half :],
        grad_down.reshape(w_down.shape),
        small[3, :half],
        small[4, :half],
        small[5, :half],
    )


def solution(mesh):
    rows, cols, vec = P("head", None), P(None, "head"), P("head")
    tokens = P("dp", "blk", "head")
    return jax.shard_map(
        on_device,
        mesh=mesh,
        in_specs=(
            tokens, P("dp", None), rows, cols, vec, cols, cols, vec, rows, vec, vec, vec, cols,
            vec, rows, vec, vec, vec, tokens,
        ),
        out_specs=(
            tokens, tokens, cols, vec, cols, cols, vec, rows, vec, vec, vec, cols, vec, rows, vec,
            vec, vec,
        ),
        check_vma=False,
    )
```

```python
import functools

import jax
import jax.numpy as jnp
from jax import lax
from jax.experimental import pallas as pl
from jax.experimental.pallas import tpu as pltpu
from jax.sharding import PartitionSpec as P

EPSILON = 1e-05
NEGATIVE = -1e30
ROOT_HALF = 0.7071067811865476
DENSITY_SCALE = 0.3989422804014327
F32 = jnp.float32
BF16 = jnp.bfloat16
MIB = 1 << 20


def dot(left, right, left_dim=1, right_dim=0):
    return lax.dot_general(
        left, right, (((left_dim,), (right_dim,)), ((), ())), preferred_element_type=F32
    )


def fill_bias(bias_ref, query_seg, keys_seg):
    same = keys_seg == query_seg
    covered = jnp.max(jnp.where(same, 1.0, 0.0), axis=0, keepdims=True)
    bias_ref[...] = jnp.where(same, 0.0, covered * NEGATIVE)


def attend_kernel(head_width, q_ref, k_ref, v_ref, qseg_ref, kseg_ref, ctx_ref, lse_ref, bias_ref):
    @pl.when(pl.program_id(1) == 0)
    def _():
        fill_bias(bias_ref, qseg_ref[0], kseg_ref[...])

    queries, keys = q_ref[...], k_ref[...]
    pair_width = queries.shape[1]
    value_cols = v_ref[...].astype(F32).T.astype(BF16)
    lane = lax.broadcasted_iota(jnp.int32, (1, pair_width), 1)
    parts, logs = [], []
    for low in range(0, pair_width, head_width):
        chosen = jnp.logical_and(lane >= low, lane < low + head_width)
        scores = dot(keys, jnp.where(chosen, queries, 0), 1, 1) + bias_ref[...]
        top = jnp.max(scores, axis=0, keepdims=True)
        shifted = jnp.exp(scores - top)
        total = jnp.sum(shifted, axis=0, keepdims=True)
        context = dot(value_cols[low : low + head_width], shifted.astype(BF16))
        parts.append(context * (1.0 / total))
        logs.append(top + jnp.log(total))
    ctx_ref[...] = jnp.concatenate(parts, axis=0).T.astype(BF16)
    lse_ref[0, 0] = jnp.concatenate(logs, axis=0)


def attend(queries, first_pair, keys, values, query_seg, keys_seg, head_width):
    seq_count, block_len = query_seg.shape
    pair = 2 * head_width
    pairs = keys.shape[1] // pair
    spec = pl.BlockSpec((block_len, pair), lambda s, p: (s, p))
    return pl.pallas_call(
        functools.partial(attend_kernel, head_width),
        grid=(seq_count, pairs),
        in_specs=[
            pl.BlockSpec((block_len, pair), lambda s, p: (s, p + first_pair)),
            spec,
            spec,
            pl.BlockSpec((1, 1, block_len), lambda s, p: (s, 0, 0)),
            pl.BlockSpec((block_len, 1), lambda s, p: (s, 0)),
        ],
        out_specs=[spec, pl.BlockSpec((1, 1, 2, block_len), lambda s, p: (s, p, 0, 0))],
        out_shape=[
            jax.ShapeDtypeStruct(keys.shape, BF16),
            jax.ShapeDtypeStruct((seq_count, pairs, 2, block_len), F32),
        ],
        scratch_shapes=[pltpu.VMEM((block_len, block_len), F32)],
        compiler_params=pltpu.CompilerParams(vmem_limit_bytes=48 * MIB),
        name="attend",
    )(queries, keys, values, query_seg[:, None, :], keys_seg.reshape(-1, 1))


def unit_rows(rows, width):
    mean = jnp.sum(rows, axis=1, keepdims=True) * (1.0 / width)
    centered = rows - mean
    variance = jnp.sum(centered * centered, axis=1, keepdims=True) * (1.0 / width)
    inverse = lax.rsqrt(variance + EPSILON)
    return centered * inverse, inverse


def unit_back(grad, unit, inverse, gain, width):
    scaled = grad * gain
    plain = jnp.sum(scaled, axis=1, keepdims=True) * (1.0 / width)
    along = jnp.sum(scaled * unit, axis=1, keepdims=True) * (1.0 / width)
    return (scaled - plain - unit * along) * inverse


def middle_kernel(
    chunk, tiles, ctxu_ref, ctxc_ref, x_ref, gout_ref, vec_ref, bup_ref, wo_ref,
    wup0_ref, wup1_ref, wdn0_ref, wdn1_ref,
    out_ref, gattn_ref, gattnb_ref, gctx_ref, gvec_ref, gbup_ref, gwup_ref, gwdn_ref,
    slope_ref, act_ref, gup_ref, normed_t, gffn_t,
):
    tile, width = x_ref.shape
    half = ctxu_ref.shape[1]
    part = wup0_ref.shape[1]
    at_step = pl.program_id(0)

    @pl.when(at_step == 0)
    def _():
        gvec_ref[...] = jnp.zeros_like(gvec_ref)
        gbup_ref[...] = jnp.zeros_like(gbup_ref)

    def vec(i):
        return vec_ref[i : i + 1, :]

    def add_vec(i, rows):
        gvec_ref[i : i + 1, :] += jnp.sum(rows, axis=0, keepdims=True)

    @pl.when(at_step < tiles)
    def _():
        here = pl.ds(pl.multiple_of(at_step * tile, tile), tile)
        attended = dot(ctxu_ref[...], wo_ref[:half]) + dot(ctxc_ref[...], wo_ref[half:])
        unit1, inverse1 = unit_rows(x_ref[...].astype(F32) + attended + vec(0), width)
        normed = unit1 * vec(1) + vec(2)
        normed_low = normed.astype(BF16)
        normed_t[:, here] = normed_low.T
        pieces = ((wup0_ref, wdn0_ref), (wup1_ref, wdn1_ref))
        down = jnp.zeros_like(normed)
        for at, (wup, wdn) in enumerate(pieces):
            for low in range(0, part, chunk):
                cols = slice(at * part + low, at * part + low + chunk)
                up = dot(normed_low, wup[:, low : low + chunk]) + bup_ref[:, cols]
                cumulative = 0.5 + 0.5 * lax.erf(up * ROOT_HALF)
                slope_ref[:, cols] = cumulative + up * (jnp.exp(-0.5 * up * up) * DENSITY_SCALE)
                activated = (up * cumulative).astype(BF16)
                act_ref[here, cols] = activated
                down += dot(activated, wdn[low : low + chunk, :])
        unit2, inverse2 = unit_rows(normed + down + vec(3), width)
        out_ref[...] = unit2 * vec(4) + vec(5)
        grad_out = gout_ref[...]
        add_vec(4, grad_out * unit2)
        add_vec(5, grad_out)
        grad_ffn = unit_back(grad_out, unit2, inverse2, vec(4), width)
        add_vec(3, grad_ffn)
        grad_ffn_low = grad_ffn.astype(BF16)
        gffn_t[:, here] = grad_ffn_low.T
        back = jnp.zeros_like(normed)
        for at, (wup, wdn) in enumerate(pieces):
            for low in range(0, part, chunk):
                cols = slice(at * part + low, at * part + low + chunk)
                grad_act = dot(grad_ffn_low, wdn[low : low + chunk, :], 1, 1)
                grad_up = (grad_act * slope_ref[:, cols]).astype(BF16)
                gup_ref[here, cols] = grad_up
                gbup_ref[0:1, cols] += jnp.sum(grad_up.astype(F32), axis=0, keepdims=True)
                back += dot(grad_up, wup[:, low : low + chunk], 1, 1)
        grad_mid = grad_ffn + back
        add_vec(1, grad_mid * unit1)
        add_vec(2, grad_mid)
        grad_attn = unit_back(grad_mid, unit1, inverse1, vec(1), width)
        add_vec(0, grad_attn)
        gattn_ref[...] = grad_attn
        grad_attn_low = grad_attn.astype(BF16)
        gattnb_ref[...] = grad_attn_low
        gctx_ref[...] = dot(grad_attn_low, wo_ref[...], 1, 1).astype(BF16)

    @pl.when(at_step >= tiles)
    def _():
        cols_step = gwup_ref.shape[1]
        cols = pl.ds(pl.multiple_of((at_step - tiles) * cols_step, cols_step), cols_step)
        gwup_ref[...] = dot(normed_t[...], gup_ref[:, cols]).astype(BF16)
        gwdn_ref[...] = dot(gffn_t[...], act_ref[:, cols]).astype(BF16)


def middle(ctx_same, ctx_cross, x, grad_out, vectors, b_up, w_out, w_up, w_down):
    rows, width = x.shape
    half = ctx_same.shape[1]
    part = w_up[0].shape[1]
    tile = 256
    tiles = rows // tile
    chunk = part // 2
    cols_step = part // 3

    def tiled(cols):
        return pl.BlockSpec((tile, cols), lambda i: (jnp.minimum(i, tiles - 1), 0))

    def whole(array):
        return pl.BlockSpec(array.shape, lambda i: (0, 0), pipeline_mode=pl.Buffered(1))

    def shape(cols, kind):
        return jax.ShapeDtypeStruct((rows, cols), kind)

    outs = [(width, F32), (width, F32), (width, BF16), (width, BF16)]
    sums = [jax.ShapeDtypeStruct((8, width), F32), jax.ShapeDtypeStruct((8, b_up.shape[1]), F32)]
    grads = [jax.ShapeDtypeStruct((width, 2 * part), BF16)] * 2
    grad_spec = pl.BlockSpec((width, cols_step), lambda i: (0, jnp.maximum(i - tiles, 0)))
    weights = [vectors, b_up, w_out, *w_up, *w_down]
    return pl.pallas_call(
        functools.partial(middle_kernel, chunk, tiles),
        grid=(tiles + 2 * part // cols_step,),
        in_specs=[tiled(half), tiled(half), tiled(width), tiled(width)]
        + [whole(w) for w in weights],
        out_specs=[tiled(c) for c, _ in outs]
        + [pl.BlockSpec(s.shape, lambda i: (0, 0)) for s in sums]
        + [grad_spec] * 2,
        out_shape=[shape(c, k) for c, k in outs] + sums + grads,
        scratch_shapes=[
            pltpu.VMEM((tile, 2 * part), F32),
            pltpu.VMEM((rows, 2 * part), BF16),
            pltpu.VMEM((rows, 2 * part), BF16),
            pltpu.VMEM((width, rows), BF16),
            pltpu.VMEM((width, rows), BF16),
        ],
        compiler_params=pltpu.CompilerParams(vmem_limit_bytes=60 * MIB),
        name="middle",
    )(ctx_same, ctx_cross, x, grad_out, *weights)


LINES = 4
RATES = {"head": 500e3, "x": 46e3, "y": 46e3, "z": 46e3, "group": 46e3}
DELAY = 8.0
ORDERS = {"A": ("x", "y", "z"), "B": ("y", "x", "z"), "C": ("z", "x", "y")}


class Item:
    action = None

    def __init__(self, at, array, first, cols, rows, order, groups):
        self.at, self.array, self.first, self.cols, self.rows = at, array, first, cols, rows
        self.groups = groups
        self.sums = []
        size = rows
        for axis in ORDERS[order] + (("group",) if groups > 1 else ()):
            before = size
            size = size // {"x": 2, "y": 2, "z": LINES, "group": 1}[axis]
            self.sums.append((axis, before, size))
        self.size = size
        self.stages = (
            [("head", "head", rows, rows)]
            + [("sum", *s) for s in self.sums]
            + [("result", *s) for s in reversed(self.sums) if s[0] != "group"]
        )

    def load(self, stage):
        kind, axis, before, size = self.stages[stage]
        moved = before if axis in ("head", "z") else size * (self.groups if axis == "group" else 1)
        return axis, moved * self.cols * 2


def plan(items, steps, ready):
    free = {axis: 0.0 for axis in RATES}
    due = [[0.0, 0] for _ in items]
    batches = []
    now = 0.0

    def run(index, batch):
        nonlocal now
        item, (_, stage) = items[index], due[index]
        batch.append((index, stage))
        now += 0.5
        if stage == len(item.stages):
            due[index] = None
            return
        axis, size = item.load(stage)
        start = max(free[axis], now)
        free[axis] = start + size / RATES[axis]
        due[index] = [free[axis] + DELAY, stage + 1]

    for at, time in enumerate([0.0] + steps):
        now += time
        batch = []
        while True:
            able = [
                i for i, d in enumerate(due) if d is not None and d[0] <= now and ready[i] <= at
            ]
            if not able:
                break
            run(min(able, key=lambda i: (due[i][0], -due[i][1])), batch)
        batches.append(batch)
    batch = batches[-1]
    while any(d is not None for d in due):
        able = [i for i, d in enumerate(due) if d is not None]
        first = min(able, key=lambda i: (due[i][0], -due[i][1]))
        now = max(now, due[first][0])
        run(first, batch)
    return batches


class Places:
    def __init__(self, groups):
        head, blk, dp = lax.axis_index("head"), lax.axis_index("blk"), lax.axis_index("dp")
        low, line, group = dp % 2, (dp // 2) % LINES, dp // (2 * LINES)
        self.head, self.line = head, line
        self.bit = {"x": blk, "y": low}
        base = group * (2 * LINES) + low
        self.partners = {
            "head": [{"head": 1 - head}],
            "x": [{"blk": 1 - blk}],
            "y": [{"dp": dp + 1 - 2 * low}],
            "z": [{"dp": base + ((line + d) % LINES) * 2} for d in range(1, LINES)],
            "group": [
                {"dp": ((group + d) % groups) * (2 * LINES) + line * 2 + low}
                for d in range(1, groups)
            ],
        }

    def greet(self):
        barrier = pltpu.get_barrier_semaphore()
        everyone = [device for devices in self.partners.values() for device in devices]
        for device in everyone:
            pl.semaphore_signal(
                barrier, inc=1, device_id=device, device_id_type=pl.DeviceIdType.MESH
            )
        pl.semaphore_wait(barrier, len(everyone))


def remote(source, target, send, recv, device):
    return pltpu.make_async_remote_copy(
        src_ref=source,
        dst_ref=target,
        send_sem=send,
        recv_sem=recv,
        device_id=device,
        device_id_type=pl.DeviceIdType.MESH,
    )


def slot_count(groups):
    return 3 + 2 * (LINES - 1) + 2 + groups - 1


class Sums:
    def __init__(self, items, places, own, other, total, result, landing, send, recv):
        self.items, self.places = items, places
        self.own, self.other, self.total, self.result = own, other, total, result
        self.landing, self.send, self.recv = landing, send, recv
        self.sent = []

    def start_of(self, item, stop):
        start = 0
        for name, before, after in item.sums:
            if name == stop:
                return start
            start = self.within(start, name, after)
        return start

    def within(self, start, axis, after):
        if axis == "z":
            return start + self.places.line * after
        if axis == "group":
            return start
        return start + self.places.bit[axis] * after

    def part(self, ref, start, size, item):
        return ref.at[
            pl.ds(pl.multiple_of(start, 16), size), item.first : item.first + item.cols
        ]

    def copies_of(self, item, stage):
        kind, axis, before, after = item.stages[stage]
        devices = self.places.partners[axis]
        out = []

        def add(source, target, slot, device):
            out.append(
                remote(
                    source, target, self.send.at[item.at, slot], self.recv.at[item.at, slot], device
                )
            )

        if kind == "head":
            cols = slice(item.first, item.first + item.cols)
            add(self.other[item.array](cols), self.total[item.array].at[:, cols], 0, devices[0])
            return out
        if kind == "sum":
            start = self.start_of(item, axis)
            ref = self.total[item.array]
            buf = self.landing[item.at][axis]
            for d, device in enumerate(devices):
                if axis == "z":
                    row = start + ((self.places.line + d + 1) % LINES) * after
                elif axis == "group":
                    row = start
                else:
                    row = start + (1 - self.places.bit[axis]) * after
                slot = {"x": 1, "y": 2, "z": 3, "group": 3 + 2 * (LINES - 1) + 2}[axis] + d
                add(self.part(ref, row, after, item), buf.at[d], slot, device)
            return out
        start, size = self.held(item, stage)
        here = self.part(self.result[item.array], start, size, item)
        for d, device in enumerate(devices):
            slot = 3 + (LINES - 1) + {"x": 0, "y": 1, "z": 2}[axis] + d
            add(here, here, slot, device)
        return out

    def held(self, item, stage):
        start, size = self.start_of(item, None), item.size
        for kind, axis, before, after in item.stages[:stage]:
            if kind == "result":
                start, size = self.start_of(item, axis), before
        return start, size

    def op(self, index, stage):
        item = self.items[index]
        if item.action is not None:
            item.action(stage)
            if stage < len(item.stages):
                self.sent.append((item, stage))
            return
        if stage > 0:
            kind, axis, before, after = item.stages[stage - 1]
            copies = self.copies_of(item, stage - 1)
            for copy in copies:
                copy.wait_recv()
            if kind == "head":
                cols = slice(item.first, item.first + item.cols)
                total = self.total[item.array]
                total[:, cols] = (
                    self.own[item.array][:, cols].astype(F32) + total[:, cols].astype(F32)
                ).astype(BF16)
            elif kind == "sum":
                start = self.within(self.start_of(item, axis), axis, after)
                here = self.part(self.total[item.array], start, after, item)
                value = here[...].astype(F32)
                for d in range(len(copies)):
                    value = value + self.landing[item.at][axis][d].astype(F32)
                if item.stages[stage][0] != "result":
                    here[...] = value.astype(BF16)
                else:
                    self.part(self.result[item.array], start, after, item)[...] = value.astype(BF16)
        if stage < len(item.stages):
            for copy in self.copies_of(item, stage):
                copy.start()
            self.sent.append((item, stage))

    def finish(self):
        for item, stage in self.sent:
            copies = self.copies_of(item, stage) if item.action is None else item.copies(stage)
            for copy in copies:
                copy.wait_send()


class Other:
    def __init__(self, loads):
        self.stages, self.action, self.copies = loads, None, None

    def load(self, stage):
        return self.stages[stage]


def landing_shapes(items):
    shapes = []
    for item in items:
        if isinstance(item, Other):
            continue
        for kind, axis, before, after in item.stages:
            if kind == "sum":
                slots = {"x": 1, "y": 1, "z": LINES - 1, "group": item.groups - 1}[axis]
                shapes.append((item.at, axis, (slots, after, item.cols)))
    return shapes


def make_items(arrays, rows, cols, step, orders, groups, at=0):
    items = []
    for index in range(len(orders)):
        array, first = divmod(index * step, cols)
        items.append(Item(at + index, arrays[array], first, step, rows, orders[index], groups))
    return items


def run_batch(sums, batch):
    for index, stage in batch:
        sums.op(index, stage)


FFN_ORDERS = "ABABCABABABC"
HEAD_ORDERS = "BCBABB"
MOVES = 4


def small_axes(groups):
    return ("x", "y", "z") + (("group",) if groups > 1 else ())


def small_slot(axis):
    return 3 + {"x": 0, "y": 1, "z": 2, "group": 2 + LINES - 1}[axis]


def back_kernel(
    items, batches, groups, head_width, scale,
    up_hbm, down_hbm, q_hbm, k_hbm, v_hbm, g_hbm, x_hbm, xc_hbm, ctx_hbm, gattnb_hbm, gattn_hbm,
    wq_hbm, wk_hbm, wv_hbm, sorter_hbm, lse_ref, qseg_ref, kseg_ref, gvec_ref, gbup_ref,
    out_up, out_down, out_heads, small_ref, din_mine, din_other,
    own_up, own_down, total_up, total_down, total_heads, heads_own, heads_other,
    q_ref, k_ref, v_ref, g_ref, x_ref, xc_ref, ctx_ref, gattnb_ref, dx_ref, wq_ref, wk_ref, wv_ref,
    sorter_ref, bias_ref, gwo_ref, bsum_ref, dxc_ref, cross_land, small_land, small_stage,
    send, recv, small_send, small_recv, move_send, move_recv, local, *landing_refs,
):
    places = Places(groups)
    rows, cols_own = own_up.shape
    tokens, width = x_ref.shape
    seqs, _, block_len = qseg_ref.shape
    half = width // 2
    part = gbup_ref.shape[1] // 2
    head = places.head
    mine_cols = pl.ds(pl.multiple_of(head * half, half), half)
    their_cols = pl.ds(pl.multiple_of((1 - head) * half, half), half)

    pairs_in = [
        (q_hbm, q_ref), (k_hbm, k_ref), (v_hbm, v_ref), (g_hbm, g_ref),
        (up_hbm.at[:, :cols_own], own_up), (down_hbm.at[:, :cols_own], own_down),
        (x_hbm, x_ref), (xc_hbm, xc_ref), (ctx_hbm, ctx_ref), (gattnb_hbm, gattnb_ref),
        (sorter_hbm, sorter_ref), (gattn_hbm, dx_ref), (wq_hbm, wq_ref), (wk_hbm, wk_ref),
        (wv_hbm, wv_ref),
    ]
    loads = [
        pltpu.make_async_copy(source, target, local.at[at])
        for at, (source, target) in enumerate(pairs_in)
    ]
    for load in loads:
        load.start()
    places.greet()
    landing = {}
    for (at, axis, _), ref in zip(landing_shapes(items), landing_refs):
        landing.setdefault(at, {})[axis] = ref
    sums = Sums(
        items, places, [own_up, own_down, heads_own],
        [
            lambda cols: up_hbm.at[:, cols_own + cols.start : cols_own + cols.stop],
            lambda cols: down_hbm.at[:, cols_own + cols.start : cols_own + cols.stop],
            lambda cols: heads_other.at[:, cols],
        ],
        [total_up, total_down, total_heads], [out_up, out_down, out_heads], landing, send, recv,
    )

    each = tokens // MOVES

    def cross_copy(at):
        here = slice(at * each, (at + 1) * each)
        return remote(
            dxc_ref.at[here], cross_land.at[here], move_send.at[at], move_recv.at[at],
            places.partners["x"][0],
        )

    def head_copy(at):
        here = slice(at * each, (at + 1) * each)
        return remote(
            dx_ref.at[here, their_cols], din_other.at[here], move_send.at[MOVES + at],
            move_recv.at[MOVES + at], places.partners["head"][0],
        )

    def keep_copy(at):
        here = slice(at * each, (at + 1) * each)
        return pltpu.make_async_copy(
            dx_ref.at[here, mine_cols], din_mine.at[here], local.at[len(pairs_in) + at]
        )

    def move_copies(at, stage):
        return [cross_copy(at) if stage == 0 else head_copy(at)]

    def move(at, stage):
        here = slice(at * each, (at + 1) * each)
        if stage == 0:
            cross_copy(at).start()
        elif stage == 1:
            cross_copy(at).wait_recv()
            dx_ref[here, :] = dx_ref[here, :] + cross_land[here, :].astype(F32)
            head_copy(at).start()
            keep_copy(at).start()
        else:
            head_copy(at).wait_recv()
            keep_copy(at).wait()

    axes = small_axes(groups)

    def small_copies(stage):
        if stage == 0:
            device = places.partners["head"][0]
            spans = (
                (gvec_ref.at[:, their_cols], slice(0, half)),
                (bsum_ref.at[:, half:], slice(half, 2 * half)),
                (gbup_ref.at[:, part:], slice(2 * half, 2 * half + part)),
            )
            return [
                remote(
                    source, small_land.at[at, :, span], small_send.at[at], small_recv.at[at], device
                )
                for at, (source, span) in enumerate(spans)
            ]
        first = small_slot(axes[stage - 1])
        return [
            remote(
                small_stage.at[stage], small_land.at[first + d], small_send.at[first + d],
                small_recv.at[first + d], device,
            )
            for d, device in enumerate(places.partners[axes[stage - 1]])
        ]

    def small(stage):
        if stage == 1:
            for copy in small_copies(0):
                copy.wait_recv()
            small_stage[1, :, :half] = gvec_ref[:, mine_cols] + small_land[0, :, :half]
            small_stage[1, :, half : 2 * half] = (
                bsum_ref[:, :half] + small_land[1, :, half : 2 * half]
            )
            small_stage[1, :, 2 * half :] = gbup_ref[:, :part] + small_land[2, :, 2 * half :]
        elif stage > 1:
            value = small_stage[stage - 1]
            first = small_slot(axes[stage - 2])
            for d, copy in enumerate(small_copies(stage - 1)):
                copy.wait_recv()
                value = value + small_land[first + d]
            if stage <= len(axes):
                small_stage[stage] = value
            else:
                small_ref[...] = value
        if stage <= len(axes):
            for copy in small_copies(stage):
                copy.start()

    others = [item for item in items if isinstance(item, Other)]
    others[0].action, others[0].copies = small, small_copies
    for at, item in enumerate(others[1:]):
        item.action = functools.partial(move, at)
        item.copies = functools.partial(move_copies, at)

    pair_width = 2 * head_width
    pairs = width // pair_width
    batches = list(batches)
    for at in (4, 5):
        loads[at].wait()
    run_batch(sums, batches.pop(0))

    def steps(count, body):
        last = len(batches) == count

        @pl.loop(0, count)
        def _(step):
            body(step)
            for at in range(count - 1 if last else count):
                if batches[at]:
                    @pl.when(step == at)
                    def _():
                        run_batch(sums, batches[at])

        if last:
            run_batch(sums, batches[-1])
        del batches[:count]

    def attention(step):
        crossed = 1 - step // (pairs // 2 * seqs)
        seq = (step // (pairs // 2)) % seqs
        pair = crossed * (pairs // 2) + step % (pairs // 2)
        here = pl.ds(pl.multiple_of(seq * block_len, block_len), block_len)
        cols = pl.ds(pl.multiple_of(pair * pair_width, pair_width), pair_width)

        @pl.when(step % (pairs // 2) == 0)
        def _():
            fill_bias(bias_ref, qseg_ref[seq], kseg_ref[crossed, here, :])

        queries, keys = q_ref[here, cols], k_ref[here, cols]
        values, grads = v_ref[here, cols], g_ref[here, cols]
        logs = lse_ref[seq, pair]
        key_cols = keys.astype(F32).T.astype(BF16)
        lane = lax.broadcasted_iota(jnp.int32, (1, pair_width), 1)
        query_parts = []
        for at, low in enumerate(range(0, pair_width, head_width)):
            chosen = jnp.logical_and(lane >= low, lane < low + head_width)
            scores = dot(keys, jnp.where(chosen, queries, 0), 1, 1) + bias_ref[...]
            mixing = jnp.exp(scores - logs[at : at + 1, :])
            grad_mixing = dot(values, jnp.where(chosen, grads, 0), 1, 1)
            inner = jnp.sum(mixing * grad_mixing, axis=0, keepdims=True)
            grad_scores = (mixing * (grad_mixing - inner)).astype(BF16)
            grad_value = dot(mixing.astype(BF16), grads)
            grad_key = dot(grad_scores, queries)
            query_parts.append(dot(key_cols[low : low + head_width], grad_scores))
            if at == 0:
                all_value, all_key = grad_value, grad_key
            else:
                all_value = jnp.where(chosen, grad_value, all_value)
                all_key = jnp.where(chosen, grad_key, all_key)
        q_ref[here, cols] = (jnp.concatenate(query_parts, axis=0).T.astype(BF16) * scale).astype(
            BF16
        )
        k_ref[here, cols] = all_key.astype(BF16)
        v_ref[here, cols] = all_value.astype(BF16)

    for at in range(4):
        loads[at].wait()
    steps(seqs * pairs, attention)
    tile = 256
    for at in range(6, 11):
        loads[at].wait()

    def tile_of(step):
        return pl.ds(pl.multiple_of(step * tile, tile), tile)

    def weights(step):
        mine = tile_of(step)
        left, left_cross = x_ref[:, mine].T, xc_ref[:, mine].T
        for at, ref in enumerate((q_ref, k_ref, v_ref)):
            first = dot(left, ref[:, :half])
            second = dot(left if at == 0 else left_cross, ref[:, half:])
            found = jnp.concatenate([first, second], axis=1).astype(BF16)
            natural = dot(found, sorter_ref[...], 1, 1).astype(BF16)
            heads_own[mine, at * half : (at + 1) * half] = natural[:, :half]
            heads_other[mine, at * half : (at + 1) * half] = natural[:, half:]
        gwo_ref[mine, :] = dot(ctx_ref[:, mine].T, gattnb_ref[...]).astype(BF16)

    steps(width // tile, weights)

    def last_weight(_):
        for ref, low in ((heads_own, 0), (heads_other, half)):
            natural = dot(sorter_ref[low : low + half], gwo_ref[...]).astype(BF16)
            ref[:half, 3 * half :] = natural[:, :half]
            ref[half:, 3 * half :] = natural[:, half:]
        totals = []
        for ref in (q_ref, v_ref):
            totals.append(jnp.sum(ref[...].astype(F32), axis=0, keepdims=True))
        found = jnp.concatenate(totals + [jnp.zeros((6, width), F32)], axis=0)
        high = found.astype(BF16)
        rest = found - high.astype(F32)
        middle_part = rest.astype(BF16)
        rest = rest - middle_part.astype(F32)
        bsum_ref[...] = (
            dot(high, sorter_ref[...], 1, 1)
            + dot(middle_part, sorter_ref[...], 1, 1)
            + dot(rest.astype(BF16), sorter_ref[...], 1, 1)
        )

    steps(1, last_weight)
    for at in range(11, 15):
        loads[at].wait()

    def inputs(step):
        here = tile_of(step)
        dq, dk, dv = q_ref[here, :], k_ref[here, :], v_ref[here, :]
        dx_ref[here, :] = (
            dx_ref[here, :]
            + dot(dq, wq_ref[...], 1, 1)
            + dot(dk[:, :half], wk_ref[:, :half], 1, 1)
            + dot(dv[:, :half], wv_ref[:, :half], 1, 1)
        )
        dxc_ref[here, :] = (
            dot(dk[:, half:], wk_ref[:, half:], 1, 1) + dot(dv[:, half:], wv_ref[:, half:], 1, 1)
        ).astype(BF16)

    steps(tokens // tile, inputs)
    assert not batches
    sums.finish()


def attention_back(
    grads, tokens, weights, logs, query_seg, keys_seg, grad_vecs, grad_bup, head_width, scale,
    groups,
):
    rows, cols = grads[0].shape[0], grads[0].shape[1] // 2
    count, width = tokens[0].shape
    seqs, block_len = query_seg.shape
    step = cols // 6
    items = make_items([0, 1], rows, cols, step, FFN_ORDERS, groups)
    items += make_items([2], rows, cols, step, HEAD_ORDERS, groups, len(items))
    pair_steps = seqs * width // (2 * head_width)
    tiles, weight_steps = count // 256, width // 256
    times = [2.3] * pair_steps + [4.0] * weight_steps + [1.5] + [1.8] * tiles
    ready = [0] * len(FFN_ORDERS) + [pair_steps + weight_steps + 1] * len(HEAD_ORDERS)
    small = (8, width + cols)
    items.append(Other([("head", 1e4)] + [(axis, 7e4) for axis in small_axes(groups)]))
    ready.append(pair_steps + weight_steps + 1)
    for at in range(MOVES):
        items.append(Other([("x", count // MOVES * width * 2), ("head", count // MOVES * width * 2)]))
        ready.append(pair_steps + weight_steps + 1 + (at + 1) * tiles // MOVES)
    batches = plan(items, times, ready)
    landing = landing_shapes(items)
    vmem = pl.BlockSpec(memory_space=pltpu.VMEM)
    anywhere = pl.BlockSpec(memory_space=pl.ANY)
    slots = len(FFN_ORDERS) + len(HEAD_ORDERS)
    small_slots = 5 + LINES - 1 + groups - 1
    big = pltpu.VMEM((rows, cols), BF16)
    rows_low = pltpu.VMEM((count, width), BF16)
    square = pltpu.VMEM((width, width), BF16)
    large = [*grads, *tokens, *weights]
    return pl.pallas_call(
        functools.partial(back_kernel, items, batches, groups, head_width, scale),
        in_specs=[anywhere] * len(large) + [vmem] * 5,
        out_specs=[vmem] * 4 + [anywhere] * 2,
        out_shape=[jax.ShapeDtypeStruct((rows, cols), BF16)] * 3
        + [jax.ShapeDtypeStruct(small, F32)]
        + [jax.ShapeDtypeStruct((count, width // 2), F32)] * 2,
        scratch_shapes=[big] * 7
        + [rows_low] * 8
        + [pltpu.VMEM((count, width), F32)]
        + [square] * 4
        + [pltpu.VMEM((block_len, block_len), F32), square, pltpu.VMEM((8, width), F32)]
        + [rows_low] * 2
        + [pltpu.VMEM((small_slots, *small), F32), pltpu.VMEM((6, *small), F32)]
        + [pltpu.SemaphoreType.DMA((slots, slot_count(groups)))] * 2
        + [pltpu.SemaphoreType.DMA((small_slots,))] * 2
        + [pltpu.SemaphoreType.DMA((2 * MOVES,))] * 2
        + [pltpu.SemaphoreType.DMA((len(large) + MOVES,))]
        + [pltpu.VMEM(shape, BF16) for _, _, shape in landing],
        compiler_params=pltpu.CompilerParams(
            collective_id=1, has_side_effects=True, vmem_limit_bytes=63 * MIB
        ),
        name="attention_back",
    )(
        *large, logs, query_seg[:, None, :], keys_seg[:, :, None], grad_vecs, grad_bup
    )


def finish_kernel(up_ref, down_ref, heads_ref, gup_ref, gdown_ref, gq_ref, gk_ref, gv_ref, go_ref):
    width = gq_ref.shape[1]
    gup_ref[...] = up_ref[...].astype(F32)
    gdown_ref[...] = down_ref[...].astype(F32).T
    for at, ref in enumerate((gq_ref, gk_ref, gv_ref, go_ref)):
        ref[...] = heads_ref[:, at * width : (at + 1) * width].astype(F32)


def finish(up, down, heads):
    rows, cols = up.shape
    steps = 6
    tile = rows // steps
    half, quarter = cols // 2, cols // 4
    spec = pl.BlockSpec((tile, cols), lambda i: (i, 0))
    third = pl.BlockSpec((tile, quarter), lambda i: (i, 0))
    return pl.pallas_call(
        finish_kernel,
        grid=(steps,),
        in_specs=[spec, pl.BlockSpec((rows, cols // steps), lambda i: (0, i)), spec],
        out_specs=[
            spec,
            pl.BlockSpec((cols // steps, rows), lambda i: (i, 0)),
            third,
            third,
            third,
            pl.BlockSpec((tile, quarter), lambda i: (i % (steps // 2), i // (steps // 2))),
        ],
        out_shape=[
            jax.ShapeDtypeStruct((rows, cols), F32),
            jax.ShapeDtypeStruct((cols, rows), F32),
            jax.ShapeDtypeStruct((rows, quarter), F32),
            jax.ShapeDtypeStruct((rows, quarter), F32),
            jax.ShapeDtypeStruct((rows, quarter), F32),
            jax.ShapeDtypeStruct((rows // 2, half), F32),
        ],
        compiler_params=pltpu.CompilerParams(vmem_limit_bytes=48 * MIB),
        name="finish",
    )(up, down, heads)


def on_device(
    layer_in, segments, block_perm, w_query, b_query, w_key, w_value, b_value, w_attn_out,
    b_attn_out, norm1_gain, norm1_bias, w_up, b_up, w_down, b_down, norm2_gain, norm2_bias,
    grad_out,
):
    seq_count, block_len, half = layer_in.shape
    width = w_query.shape[0]
    local_heads = block_perm.shape[0]
    heads = 2 * local_heads
    head_cols = w_query.shape[1]
    head_width = head_cols // local_heads
    seqs = seq_count // 2
    rows = seqs * block_len
    scale = head_width ** (-0.5)
    head = lax.axis_index("head")
    my_block = lax.axis_index("blk")
    first = head == 0
    dp_size = lax.axis_size("dp")

    def swap(array):
        return lax.ppermute(array, "head", [(0, 1), (1, 0)])

    def cross(array):
        return lax.ppermute(array, "blk", [(0, 1), (1, 0)])

    def joined(mine, received, axis=-1):
        return jnp.where(
            first,
            jnp.concatenate([mine, received], axis=axis),
            jnp.concatenate([received, mine], axis=axis),
        )

    def to_tokens(array):
        mine = lax.dynamic_slice_in_dim(array, head * seqs, seqs, 0)
        theirs = lax.dynamic_slice_in_dim(array, (1 - head) * seqs, seqs, 0)
        return joined(mine, swap(theirs)).reshape(rows, width)

    def to_features(array):
        array = array.reshape(seqs, block_len, width)
        mine = lax.dynamic_slice_in_dim(array, head * half, half, 2)
        theirs = lax.dynamic_slice_in_dim(array, (1 - head) * half, half, 2)
        return joined(mine, swap(theirs), 0)

    x = to_tokens(layer_in)
    x_cross = jnp.concatenate(
        [cross(x[s * block_len : (s + 1) * block_len]) for s in range(seqs)]
    )
    model_vecs = [b_attn_out, norm1_gain, norm1_bias, b_down, norm2_gain, norm2_bias]
    packed = jnp.concatenate(
        [*model_vecs, b_query, b_value, b_up, block_perm.astype(F32).reshape(-1)]
    )
    packed_other = swap(packed)

    def unpack(array):
        vecs = array[: 8 * half].reshape(8, half)
        ups = array[8 * half : 8 * half + b_up.shape[0]]
        perm = array[8 * half + b_up.shape[0] :].reshape(block_perm.shape)
        return vecs, ups, perm

    vecs_own, up_own, perm_own = unpack(packed)
    vecs_other, up_other, perm_other = unpack(packed_other)
    vectors = joined(vecs_own, vecs_other)
    b_up_all = jnp.concatenate([up_own, up_other])[None, :]
    b_heads = jnp.concatenate([vecs_own[6:8], vecs_other[6:8]], axis=1)

    perm = jnp.concatenate([perm_own, perm_other], axis=0)
    columns = jnp.arange(perm.shape[1])
    reads = jnp.sum(jnp.where(columns[None, :] == my_block, perm, 0.0), axis=1)
    crossed = (reads != my_block.astype(F32)).astype(jnp.int32)
    before = jnp.cumsum(crossed) - crossed
    place = jnp.where(crossed == 1, heads // 2 + before, jnp.arange(heads) - before)
    feature = jnp.arange(heads * head_width)
    target = jnp.repeat(place, head_width) * head_width + feature % head_width
    sorter = (target[:, None] == feature[None, :]).astype(BF16)

    def sort_cols(own, other):
        return dot(jnp.concatenate([own, other], axis=1), sorter).astype(BF16)

    wq = sort_cols(w_query, swap(w_query))
    wk = sort_cols(w_key, swap(w_key))
    wv = sort_cols(w_value, swap(w_value))
    wo = dot(sorter, jnp.concatenate([w_attn_out, swap(w_attn_out)], axis=0), 0, 0).astype(BF16)
    b_sorted = jnp.sum(b_heads[:, :, None] * sorter.astype(F32)[None], axis=1)
    bq, bv = b_sorted[0], b_sorted[1]
    w_up_pair = (w_up, swap(w_up))
    w_down_pair = (w_down, swap(w_down))

    same = heads // 2 * head_width
    queries = ((dot(x, wq) + bq) * scale).astype(BF16)
    keys_same = dot(x, wk[:, :same]).astype(BF16)
    values_same = (dot(x, wv[:, :same]) + bv[:same]).astype(BF16)

    my_segments = lax.dynamic_slice_in_dim(segments, head * seqs, seqs, 0)
    own_seg = lax.dynamic_slice_in_dim(my_segments, my_block * block_len, block_len, 1)
    cross_seg = lax.dynamic_slice_in_dim(my_segments, (1 - my_block) * block_len, block_len, 1)
    ctx_same, log_same = attend(
        queries, 0, keys_same, values_same, own_seg, own_seg, head_width
    )
    keys_cross = dot(x_cross, wk[:, same:]).astype(BF16)
    values_cross = (dot(x_cross, wv[:, same:]) + bv[same:]).astype(BF16)
    pairs = same // (2 * head_width)
    ctx_cross, log_cross = attend(
        queries, pairs, keys_cross, values_cross, own_seg, cross_seg, head_width
    )

    grad_rows = to_tokens(grad_out)
    (
        out_rows, grad_attn, grad_attn_low, grad_ctx, grad_vecs, grad_bup, grad_up_all,
        grad_down_all,
    ) = middle(ctx_same, ctx_cross, x, grad_rows, vectors, b_up_all, wo, w_up_pair, w_down_pair)
    layer_out = to_features(out_rows)

    total_up, total_down, total_heads, small, din_mine, din_other = attention_back(
        (grad_up_all, grad_down_all),
        (
            queries,
            jnp.concatenate([keys_same, keys_cross], axis=1),
            jnp.concatenate([values_same, values_cross], axis=1),
            grad_ctx,
            x,
            x_cross,
            jnp.concatenate([ctx_same, ctx_cross], axis=1),
            grad_attn_low,
            grad_attn,
        ),
        (wq, wk, wv, sorter),
        jnp.concatenate([log_same, log_cross], axis=1),
        own_seg,
        jnp.stack([own_seg.reshape(-1), cross_seg.reshape(-1)]),
        grad_vecs,
        grad_bup,
        head_width,
        scale,
        dp_size // (2 * LINES),
    )
    din_mine = din_mine.reshape(seqs, block_len, half)
    din_other = din_other.reshape(seqs, block_len, half)
    grad_in = joined(din_mine, din_other, 0)
    grad_up, grad_down, grad_q, grad_k, grad_v, grad_o = finish(total_up, total_down, total_heads)
    return (
        layer_out,
        grad_in,
        grad_q,
        small[0, half : 2 * half],
        grad_k,
        grad_v,
        small[1, half : 2 * half],
        grad_o,
        small[0, :half],
        small[1, :half],
        small[2, :half],
        grad_up,
        small[0, 2 * half :],
        grad_down,
        small[3, :half],
        small[4, :half],
        small[5, :half],
    )


def solution(mesh):
    rows, cols, vec = P("head", None), P(None, "head"), P("head")
    tokens = P("dp", "blk", "head")
    return jax.shard_map(
        on_device,
        mesh=mesh,
        in_specs=(
            tokens, P("dp", None), rows, cols, vec, cols, cols, vec, rows, vec, vec, vec, cols,
            vec, rows, vec, vec, vec, tokens,
        ),
        out_specs=(
            tokens, tokens, cols, vec, cols, cols, vec, rows, vec, vec, vec, cols, vec, rows, vec,
            vec, vec,
        ),
        check_vma=False,
    )
```

```python
import functools

import jax
import jax.numpy as jnp
from jax import lax
from jax.experimental import pallas as pl
from jax.experimental.pallas import tpu as pltpu
from jax.sharding import PartitionSpec as P

EPSILON = 1e-05
NEGATIVE = -1e30
ROOT_HALF = 0.7071067811865476
DENSITY_SCALE = 0.3989422804014327
F32 = jnp.float32
BF16 = jnp.bfloat16
MIB = 1 << 20


def dot(left, right, left_dim=1, right_dim=0):
    return lax.dot_general(
        left, right, (((left_dim,), (right_dim,)), ((), ())), preferred_element_type=F32
    )


def fill_bias(bias_ref, query_seg, keys_seg):
    same = keys_seg == query_seg
    covered = jnp.max(jnp.where(same, 1.0, 0.0), axis=0, keepdims=True)
    bias_ref[...] = jnp.where(same, 0.0, covered * NEGATIVE)


def attend_pair(queries, keys, values, bias, head_width):
    pair_width = queries.shape[1]
    value_cols = values.astype(F32).T.astype(BF16)
    lane = lax.broadcasted_iota(jnp.int32, (1, pair_width), 1)
    parts, logs = [], []
    for low in range(0, pair_width, head_width):
        chosen = jnp.logical_and(lane >= low, lane < low + head_width)
        scores = dot(keys, jnp.where(chosen, queries, 0), 1, 1) + bias[...]
        top = jnp.max(scores, axis=0, keepdims=True)
        shifted = jnp.exp(scores - top)
        total = jnp.sum(shifted, axis=0, keepdims=True)
        context = dot(value_cols[low : low + head_width], shifted.astype(BF16))
        parts.append(context * (1.0 / total))
        logs.append(top + jnp.log(total))
    return jnp.concatenate(parts, axis=0).T.astype(BF16), jnp.concatenate(logs, axis=0)


def split_dot(left, right, left_dim=1, right_dim=0):
    high = left.astype(BF16)
    rest = left - high.astype(F32)
    mid = rest.astype(BF16)
    low = (rest - mid.astype(F32)).astype(BF16)
    return sum(dot(x, right, left_dim, right_dim) for x in (high, mid, low))


def front_kernel(
    head_width, scale, seqs,
    layer_hbm, gout_hbm, wq_hbm, wk_hbm, wv_hbm, wo_hbm, wup_hbm, wdn_hbm, vec_own, qseg_ref,
    kseg_ref,
    x_hbm, xc_hbm, q_hbm, k_hbm, v_hbm, ctx_hbm, wqs_hbm, wks_hbm, wvs_hbm, wos_hbm, sorter_hbm,
    wup_other, wdn_other, grad_hbm, vec_all, bup_all, lse_ref,
    x_ref, xc_ref, q_ref, k_ref, v_ref, ctx_ref, wn_q, wn_k, wn_v, wn_o, ws_q, ws_k, ws_v, ws_o,
    sorter_ref, sorter_t, vec_land, bias_ref, local, send, recv,
):
    head, blk = lax.axis_index("head"), lax.axis_index("blk")
    to_head, to_cross = {"head": 1 - head}, {"blk": 1 - blk}
    rows, width = x_ref.shape
    half = width // 2
    block_len = rows // seqs
    my_rows = pl.ds(pl.multiple_of(head * rows, rows), rows)
    their_rows = pl.ds(pl.multiple_of((1 - head) * rows, rows), rows)
    mine = pl.ds(pl.multiple_of(head * half, half), half)
    theirs = pl.ds(pl.multiple_of((1 - head) * half, half), half)

    started = []

    def bring(at, source, target):
        copy = pltpu.make_async_copy(source, target, local.at[at])
        copy.start()
        return copy

    def give(at, source, target, device):
        copy = remote(source, target, send.at[at], recv.at[at], device)
        copy.start()
        started.append(copy)
        return copy

    barrier = pltpu.get_barrier_semaphore()
    for device in (to_head, to_cross):
        pl.semaphore_signal(barrier, inc=1, device_id=device, device_id_type=pl.DeviceIdType.MESH)
    own_x = bring(0, layer_hbm.at[my_rows], x_ref.at[:, mine])
    own_w = [
        bring(1, wq_hbm, wn_q.at[:, :half]),
        bring(2, wk_hbm, wn_k.at[:, :half]),
        bring(3, wv_hbm, wn_v.at[:, :half]),
        bring(4, wo_hbm, wn_o.at[:half]),
    ]
    own_grad = bring(5, gout_hbm.at[my_rows], grad_hbm.at[:, mine])
    pl.semaphore_wait(barrier, 2)

    def seq_rows(seq):
        return slice(seq * block_len, (seq + 1) * block_len)

    def block_of(seq):
        return pl.ds(pl.multiple_of(head * rows + seq * block_len, block_len), block_len)

    vecs = give(0, vec_own, vec_land, to_head)
    features = give(1, layer_hbm.at[their_rows], x_ref.at[:, mine], to_head)
    cross = [[give(2, layer_hbm.at[block_of(0)], xc_ref.at[seq_rows(0), mine], to_cross)]]
    other_w = [
        give(3, wq_hbm, wn_q.at[:, half:], to_head),
        give(4, wk_hbm, wn_k.at[:, half:], to_head),
        give(5, wv_hbm, wn_v.at[:, half:], to_head),
        give(6, wo_hbm, wn_o.at[half:], to_head),
    ]
    features.wait_recv()
    base = 7
    for seq in range(seqs):
        if seq > 0:
            cross.append(
                [give(base, layer_hbm.at[block_of(seq)], xc_ref.at[seq_rows(seq), mine], to_cross)]
            )
            base += 1
        here = seq_rows(seq)
        cross[seq].append(give(base, x_ref.at[here, theirs], xc_ref.at[here, theirs], to_cross))
        base += 1
    later = [
        give(base, wup_hbm, wup_other, to_head),
        give(base + 1, wdn_hbm, wdn_other, to_head),
        give(base + 2, gout_hbm.at[their_rows], grad_hbm.at[:, mine], to_head),
    ]

    vecs.wait_recv()
    crossed = jnp.concatenate([vec_own[12:13, :], vec_land[12:13, :]], axis=1)
    row = lax.broadcasted_iota(jnp.int32, (width, width), 0)
    col = lax.broadcasted_iota(jnp.int32, (width, width), 1)
    earlier = jnp.where(row // head_width < col // head_width, 1.0, 0.0).astype(BF16)
    before = dot(jnp.broadcast_to(crossed, (8, width)).astype(BF16), earlier)[0:1]
    lane = lax.broadcasted_iota(jnp.int32, (1, width), 1)
    place = jnp.where(
        crossed > 0.5, half + before + (lane % head_width).astype(F32), lane.astype(F32) - before
    )
    found = jnp.where(row.astype(F32) == place, 1.0, 0.0)
    sorter_t[...] = found.astype(BF16)
    sorter_ref[...] = found.T.astype(BF16)
    vec_all[:, mine] = vec_own[0:8, :]
    vec_all[:, theirs] = vec_land[0:8, :]
    for at in range(bup_all.shape[1] // half):
        source = vec_own if at < 4 else vec_land
        bup_all[:, at * half : (at + 1) * half] = source[8 + at % 4 : 9 + at % 4, :]
    b_local = jnp.concatenate([vec_own[0:8, :], vec_land[0:8, :]], axis=1)
    b_sorted = split_dot(b_local, sorter_ref[...])
    bq, bv = b_sorted[6:7], b_sorted[7:8]

    out = []
    pairs_w = ((wn_q, ws_q, wqs_hbm), (wn_k, ws_k, wks_hbm), (wn_v, ws_v, wvs_hbm))
    for at, (natural, ordered, target) in enumerate(pairs_w):
        own_w[at].wait()
        other_w[at].wait_recv()
        ordered[...] = dot(natural[...], sorter_ref[...]).astype(BF16)
        out.append(bring(6 + at, ordered, target))
    out.append(bring(9, sorter_ref, sorter_hbm))
    own_x.wait()
    out.append(bring(10, x_ref, x_hbm))
    x = x_ref[...]
    q_ref[...] = ((dot(x, ws_q[...]) + bq) * scale).astype(BF16)
    out.append(bring(11, q_ref, q_hbm))
    k_ref[:, :half] = dot(x, ws_k[:, :half]).astype(BF16)
    v_ref[:, :half] = (dot(x, ws_v[:, :half]) + bv[:, :half]).astype(BF16)

    pair_width = 2 * head_width
    pairs = half // pair_width

    def attention(seq, first_pair, kind):
        here = pl.ds(pl.multiple_of(seq * block_len, block_len), block_len)
        fill_bias(bias_ref, qseg_ref[seq], kseg_ref[kind, here, :])

        @pl.loop(0, pairs)
        def _(at):
            pair = first_pair + at
            cols = pl.ds(pl.multiple_of(pair * pair_width, pair_width), pair_width)
            context, logs = attend_pair(
                q_ref[here, cols], k_ref[here, cols], v_ref[here, cols], bias_ref, head_width
            )
            ctx_ref[here, cols] = context
            lse_ref[seq, pair] = logs

    @pl.loop(0, seqs)
    def _(seq):
        attention(seq, 0, 0)

    own_w[3].wait()
    other_w[3].wait_recv()
    ws_o[...] = dot(sorter_t[...], wn_o[...]).astype(BF16)
    out.append(bring(12, ws_o, wos_hbm))
    for seq in range(seqs):
        here = seq_rows(seq)
        for copy in cross[seq]:
            copy.wait_recv()
        x_cross = xc_ref[here, :]
        k_ref[here, half:] = dot(x_cross, ws_k[:, half:]).astype(BF16)
        v_ref[here, half:] = (dot(x_cross, ws_v[:, half:]) + bv[:, half:]).astype(BF16)
        attention(seq, pairs, 1)
    out.append(bring(13, xc_ref, xc_hbm))
    out.append(bring(14, k_ref, k_hbm))
    out.append(bring(15, v_ref, v_hbm))
    out.append(bring(16, ctx_ref, ctx_hbm))
    own_grad.wait()
    for copy in later:
        copy.wait_recv()
    for copy in out:
        copy.wait()
    for copy in started:
        copy.wait_send()


def front(layer_in, grad_out, weights, vecs, query_seg, keys_seg, head_width, scale):
    width = weights[0].shape[0]
    half = width // 2
    seqs, block_len = query_seg.shape
    rows = seqs * block_len
    part = weights[4].shape[1]
    anywhere = pl.BlockSpec(memory_space=pl.ANY)
    vmem = pl.BlockSpec(memory_space=pltpu.VMEM)
    tokens = jax.ShapeDtypeStruct((rows, width), BF16)
    square = jax.ShapeDtypeStruct((width, width), BF16)
    low_rows, low_square = pltpu.VMEM((rows, width), BF16), pltpu.VMEM((width, width), BF16)
    copies = 7 + 2 * seqs - 1 + 3
    return pl.pallas_call(
        functools.partial(front_kernel, head_width, scale, seqs),
        in_specs=[anywhere] * 8 + [vmem] * 3,
        out_specs=[anywhere] * 14 + [vmem] * 3,
        out_shape=[tokens] * 6
        + [square] * 5
        + [
            jax.ShapeDtypeStruct(weights[4].shape, BF16),
            jax.ShapeDtypeStruct(weights[5].shape, BF16),
            jax.ShapeDtypeStruct((rows, width), F32),
            jax.ShapeDtypeStruct((8, width), F32),
            jax.ShapeDtypeStruct((1, 2 * part), F32),
            jax.ShapeDtypeStruct((seqs, width // (2 * head_width), 2, block_len), F32),
        ],
        scratch_shapes=[low_rows] * 6
        + [low_square] * 10
        + [
            pltpu.VMEM((16, half), F32),
            pltpu.VMEM((block_len, block_len), F32),
            pltpu.SemaphoreType.DMA((17,)),
            pltpu.SemaphoreType.DMA((copies,)),
            pltpu.SemaphoreType.DMA((copies,)),
        ],
        compiler_params=pltpu.CompilerParams(
            collective_id=3, has_side_effects=True, vmem_limit_bytes=60 * MIB
        ),
        name="front",
    )(
        layer_in, grad_out, *weights, vecs, query_seg[:, None, :], keys_seg[:, :, None]
    )


def unit_rows(rows, width):
    mean = jnp.sum(rows, axis=1, keepdims=True) * (1.0 / width)
    centered = rows - mean
    variance = jnp.sum(centered * centered, axis=1, keepdims=True) * (1.0 / width)
    inverse = lax.rsqrt(variance + EPSILON)
    return centered * inverse, inverse


def unit_back(grad, unit, inverse, gain, width):
    scaled = grad * gain
    plain = jnp.sum(scaled, axis=1, keepdims=True) * (1.0 / width)
    along = jnp.sum(scaled * unit, axis=1, keepdims=True) * (1.0 / width)
    return (scaled - plain - unit * along) * inverse


def middle_kernel(
    chunk, tiles, ctx_ref, x_ref, gout_ref, vec_ref, bup_ref, wo_ref,
    wup0_ref, wup1_ref, wdn0_ref, wdn1_ref,
    out_ref, gattn_ref, gattnb_ref, gctx_ref, gvec_ref, gbup_ref, gwup_ref, gwdn_ref,
    slope_ref, act_ref, gup_ref, normed_t, gffn_t,
):
    tile, width = x_ref.shape
    part = wup0_ref.shape[1]
    at_step = pl.program_id(0)

    @pl.when(at_step == 0)
    def _():
        gvec_ref[...] = jnp.zeros_like(gvec_ref)
        gbup_ref[...] = jnp.zeros_like(gbup_ref)

    def vec(i):
        return vec_ref[i : i + 1, :]

    def add_vec(i, rows):
        gvec_ref[i : i + 1, :] += jnp.sum(rows, axis=0, keepdims=True)

    @pl.when(at_step < tiles)
    def _():
        here = pl.ds(pl.multiple_of(at_step * tile, tile), tile)
        attended = dot(ctx_ref[...], wo_ref[...])
        unit1, inverse1 = unit_rows(x_ref[...].astype(F32) + attended + vec(0), width)
        normed = unit1 * vec(1) + vec(2)
        normed_low = normed.astype(BF16)
        normed_t[:, here] = normed_low.T
        pieces = ((wup0_ref, wdn0_ref), (wup1_ref, wdn1_ref))
        down = jnp.zeros_like(normed)
        for at, (wup, wdn) in enumerate(pieces):
            for low in range(0, part, chunk):
                cols = slice(at * part + low, at * part + low + chunk)
                up = dot(normed_low, wup[:, low : low + chunk]) + bup_ref[:, cols]
                cumulative = 0.5 + 0.5 * lax.erf(up * ROOT_HALF)
                slope_ref[:, cols] = cumulative + up * (jnp.exp(-0.5 * up * up) * DENSITY_SCALE)
                activated = (up * cumulative).astype(BF16)
                act_ref[here, cols] = activated
                down += dot(activated, wdn[low : low + chunk, :])
        unit2, inverse2 = unit_rows(normed + down + vec(3), width)
        out_ref[...] = unit2 * vec(4) + vec(5)
        grad_out = gout_ref[...]
        add_vec(4, grad_out * unit2)
        add_vec(5, grad_out)
        grad_ffn = unit_back(grad_out, unit2, inverse2, vec(4), width)
        add_vec(3, grad_ffn)
        grad_ffn_low = grad_ffn.astype(BF16)
        gffn_t[:, here] = grad_ffn_low.T
        back = jnp.zeros_like(normed)
        for at, (wup, wdn) in enumerate(pieces):
            for low in range(0, part, chunk):
                cols = slice(at * part + low, at * part + low + chunk)
                grad_act = dot(grad_ffn_low, wdn[low : low + chunk, :], 1, 1)
                grad_up = (grad_act * slope_ref[:, cols]).astype(BF16)
                gup_ref[here, cols] = grad_up
                gbup_ref[0:1, cols] += jnp.sum(grad_up.astype(F32), axis=0, keepdims=True)
                back += dot(grad_up, wup[:, low : low + chunk], 1, 1)
        grad_mid = grad_ffn + back
        add_vec(1, grad_mid * unit1)
        add_vec(2, grad_mid)
        grad_attn = unit_back(grad_mid, unit1, inverse1, vec(1), width)
        add_vec(0, grad_attn)
        gattn_ref[...] = grad_attn
        grad_attn_low = grad_attn.astype(BF16)
        gattnb_ref[...] = grad_attn_low
        gctx_ref[...] = dot(grad_attn_low, wo_ref[...], 1, 1).astype(BF16)

    @pl.when(at_step >= tiles)
    def _():
        cols_step = gwup_ref.shape[1]
        cols = pl.ds(pl.multiple_of((at_step - tiles) * cols_step, cols_step), cols_step)
        gwup_ref[...] = dot(normed_t[...], gup_ref[:, cols]).astype(BF16)
        gwdn_ref[...] = dot(gffn_t[...], act_ref[:, cols]).astype(BF16)


def middle(ctx, x, grad_out, vectors, b_up, w_out, w_up, w_down):
    rows, width = x.shape
    part = w_up[0].shape[1]
    tile = 256
    tiles = rows // tile
    chunk = part // 2
    cols_step = part // 3

    def tiled(cols):
        return pl.BlockSpec((tile, cols), lambda i: (jnp.minimum(i, tiles - 1), 0))

    def whole(array):
        return pl.BlockSpec(array.shape, lambda i: (0, 0), pipeline_mode=pl.Buffered(1))

    def shape(cols, kind):
        return jax.ShapeDtypeStruct((rows, cols), kind)

    outs = [(width, F32), (width, F32), (width, BF16), (width, BF16)]
    sums = [jax.ShapeDtypeStruct((8, width), F32), jax.ShapeDtypeStruct((8, b_up.shape[1]), F32)]
    grads = [jax.ShapeDtypeStruct((width, 2 * part), BF16)] * 2
    grad_spec = pl.BlockSpec((width, cols_step), lambda i: (0, jnp.maximum(i - tiles, 0)))
    weights = [vectors, b_up, w_out, *w_up, *w_down]
    return pl.pallas_call(
        functools.partial(middle_kernel, chunk, tiles),
        grid=(tiles + 2 * part // cols_step,),
        in_specs=[tiled(width), tiled(width), tiled(width)]
        + [whole(w) for w in weights],
        out_specs=[tiled(c) for c, _ in outs]
        + [pl.BlockSpec(s.shape, lambda i: (0, 0)) for s in sums]
        + [grad_spec] * 2,
        out_shape=[shape(c, k) for c, k in outs] + sums + grads,
        scratch_shapes=[
            pltpu.VMEM((tile, 2 * part), F32),
            pltpu.VMEM((rows, 2 * part), BF16),
            pltpu.VMEM((rows, 2 * part), BF16),
            pltpu.VMEM((width, rows), BF16),
            pltpu.VMEM((width, rows), BF16),
        ],
        compiler_params=pltpu.CompilerParams(vmem_limit_bytes=60 * MIB),
        name="middle",
    )(ctx, x, grad_out, *weights)


LINES = 4
RATES = {"head": 500e3, "x": 46e3, "y": 46e3, "z": 46e3, "group": 46e3}
DELAY = 8.0
ORDERS = {"A": ("x", "y", "z"), "B": ("y", "x", "z"), "C": ("z", "x", "y")}


class Item:
    action = None

    def __init__(self, at, array, first, cols, rows, order, groups):
        self.at, self.array, self.first, self.cols, self.rows = at, array, first, cols, rows
        self.groups = groups
        self.sums = []
        size = rows
        for axis in ORDERS[order] + (("group",) if groups > 1 else ()):
            before = size
            size = size // {"x": 2, "y": 2, "z": LINES, "group": 1}[axis]
            self.sums.append((axis, before, size))
        self.size = size
        self.stages = (
            [("head", "head", rows, rows)]
            + [("sum", *s) for s in self.sums]
            + [("result", *s) for s in reversed(self.sums) if s[0] != "group"]
        )

    def load(self, stage):
        kind, axis, before, size = self.stages[stage]
        moved = before if axis in ("head", "z") else size * (self.groups if axis == "group" else 1)
        return axis, moved * self.cols * 2


def plan(items, steps, ready):
    free = {axis: 0.0 for axis in RATES}
    due = [[0.0, 0] for _ in items]
    batches = []
    now = 0.0

    def run(index, batch):
        nonlocal now
        item, (_, stage) = items[index], due[index]
        batch.append((index, stage))
        now += 0.5
        if stage == len(item.stages):
            due[index] = None
            return
        axis, size = item.load(stage)
        start = max(free[axis], now)
        free[axis] = start + size / RATES[axis]
        due[index] = [free[axis] + DELAY, stage + 1]

    for at, time in enumerate([0.0] + steps):
        now += time
        batch = []
        while True:
            able = [
                i for i, d in enumerate(due) if d is not None and d[0] <= now and ready[i] <= at
            ]
            if not able:
                break
            run(min(able, key=lambda i: (due[i][0], -due[i][1])), batch)
        batches.append(batch)
    batch = batches[-1]
    while any(d is not None for d in due):
        able = [i for i, d in enumerate(due) if d is not None]
        first = min(able, key=lambda i: (due[i][0], -due[i][1]))
        now = max(now, due[first][0])
        run(first, batch)
    return batches


class Places:
    def __init__(self, groups):
        head, blk, dp = lax.axis_index("head"), lax.axis_index("blk"), lax.axis_index("dp")
        low, line, group = dp % 2, (dp // 2) % LINES, dp // (2 * LINES)
        self.head, self.line = head, line
        self.bit = {"x": blk, "y": low}
        base = group * (2 * LINES) + low
        self.partners = {
            "head": [{"head": 1 - head}],
            "x": [{"blk": 1 - blk}],
            "y": [{"dp": dp + 1 - 2 * low}],
            "z": [{"dp": base + ((line + d) % LINES) * 2} for d in range(1, LINES)],
            "group": [
                {"dp": ((group + d) % groups) * (2 * LINES) + line * 2 + low}
                for d in range(1, groups)
            ],
        }

    def greet(self):
        barrier = pltpu.get_barrier_semaphore()
        everyone = [device for devices in self.partners.values() for device in devices]
        for device in everyone:
            pl.semaphore_signal(
                barrier, inc=1, device_id=device, device_id_type=pl.DeviceIdType.MESH
            )
        pl.semaphore_wait(barrier, len(everyone))


def remote(source, target, send, recv, device):
    return pltpu.make_async_remote_copy(
        src_ref=source,
        dst_ref=target,
        send_sem=send,
        recv_sem=recv,
        device_id=device,
        device_id_type=pl.DeviceIdType.MESH,
    )


def slot_count(groups):
    return 3 + 2 * (LINES - 1) + 2 + groups - 1


class Sums:
    def __init__(self, items, places, own, other, total, result, landing, send, recv):
        self.items, self.places = items, places
        self.own, self.other, self.total, self.result = own, other, total, result
        self.landing, self.send, self.recv = landing, send, recv
        self.sent = []

    def start_of(self, item, stop):
        start = 0
        for name, before, after in item.sums:
            if name == stop:
                return start
            start = self.within(start, name, after)
        return start

    def within(self, start, axis, after):
        if axis == "z":
            return start + self.places.line * after
        if axis == "group":
            return start
        return start + self.places.bit[axis] * after

    def part(self, ref, start, size, item):
        return ref.at[
            pl.ds(pl.multiple_of(start, 16), size), item.first : item.first + item.cols
        ]

    def copies_of(self, item, stage):
        kind, axis, before, after = item.stages[stage]
        devices = self.places.partners[axis]
        out = []

        def add(source, target, slot, device):
            out.append(
                remote(
                    source, target, self.send.at[item.at, slot], self.recv.at[item.at, slot], device
                )
            )

        if kind == "head":
            cols = slice(item.first, item.first + item.cols)
            add(self.other[item.array](cols), self.total[item.array].at[:, cols], 0, devices[0])
            return out
        if kind == "sum":
            start = self.start_of(item, axis)
            ref = self.total[item.array]
            buf = self.landing[item.at][axis]
            for d, device in enumerate(devices):
                if axis == "z":
                    row = start + ((self.places.line + d + 1) % LINES) * after
                elif axis == "group":
                    row = start
                else:
                    row = start + (1 - self.places.bit[axis]) * after
                slot = {"x": 1, "y": 2, "z": 3, "group": 3 + 2 * (LINES - 1) + 2}[axis] + d
                add(self.part(ref, row, after, item), buf.at[d], slot, device)
            return out
        start, size = self.held(item, stage)
        here = self.part(self.result[item.array], start, size, item)
        for d, device in enumerate(devices):
            slot = 3 + (LINES - 1) + {"x": 0, "y": 1, "z": 2}[axis] + d
            add(here, here, slot, device)
        return out

    def held(self, item, stage):
        start, size = self.start_of(item, None), item.size
        for kind, axis, before, after in item.stages[:stage]:
            if kind == "result":
                start, size = self.start_of(item, axis), before
        return start, size

    def op(self, index, stage):
        item = self.items[index]
        if item.action is not None:
            item.action(stage)
            if stage < len(item.stages):
                self.sent.append((item, stage))
            return
        if stage > 0:
            kind, axis, before, after = item.stages[stage - 1]
            copies = self.copies_of(item, stage - 1)
            for copy in copies:
                copy.wait_recv()
            if kind == "head":
                cols = slice(item.first, item.first + item.cols)
                total = self.total[item.array]
                total[:, cols] = (
                    self.own[item.array][:, cols].astype(F32) + total[:, cols].astype(F32)
                ).astype(BF16)
            elif kind == "sum":
                start = self.within(self.start_of(item, axis), axis, after)
                here = self.part(self.total[item.array], start, after, item)
                value = here[...].astype(F32)
                for d in range(len(copies)):
                    value = value + self.landing[item.at][axis][d].astype(F32)
                if item.stages[stage][0] != "result":
                    here[...] = value.astype(BF16)
                else:
                    self.part(self.result[item.array], start, after, item)[...] = value.astype(BF16)
        if stage < len(item.stages):
            for copy in self.copies_of(item, stage):
                copy.start()
            self.sent.append((item, stage))

    def finish(self):
        for item, stage in self.sent:
            copies = self.copies_of(item, stage) if item.action is None else item.copies(stage)
            for copy in copies:
                copy.wait_send()


class Other:
    def __init__(self, loads):
        self.stages, self.action, self.copies = loads, None, None

    def load(self, stage):
        return self.stages[stage]


def landing_shapes(items):
    shapes = []
    for item in items:
        if isinstance(item, Other):
            continue
        for kind, axis, before, after in item.stages:
            if kind == "sum":
                slots = {"x": 1, "y": 1, "z": LINES - 1, "group": item.groups - 1}[axis]
                shapes.append((item.at, axis, (slots, after, item.cols)))
    return shapes


def make_items(arrays, rows, cols, step, orders, groups, at=0):
    items = []
    for index in range(len(orders)):
        array, first = divmod(index * step, cols)
        items.append(Item(at + index, arrays[array], first, step, rows, orders[index], groups))
    return items


def run_batch(sums, batch):
    for index, stage in batch:
        sums.op(index, stage)


FFN_ORDERS = "ABABCABABABC"
HEAD_ORDERS = "BCBABB"
MOVES = 4


def small_axes(groups):
    return ("x", "y", "z") + (("group",) if groups > 1 else ())


def small_slot(axis):
    return 3 + {"x": 0, "y": 1, "z": 2, "group": 2 + LINES - 1}[axis]


def back_kernel(
    items, batches, groups, head_width, scale,
    up_hbm, down_hbm, q_hbm, k_hbm, v_hbm, g_hbm, x_hbm, xc_hbm, ctx_hbm, gattnb_hbm, gattn_hbm,
    wq_hbm, wk_hbm, wv_hbm, sorter_hbm, rows_hbm, lse_ref, qseg_ref, kseg_ref, gvec_ref, gbup_ref,
    out_up, out_down, out_heads, small_ref, din_all, rows_all,
    own_up, own_down, total_up, total_down, total_heads, heads_own, heads_other,
    q_ref, k_ref, v_ref, g_ref, x_ref, xc_ref, ctx_ref, gattnb_ref, dx_ref, wq_ref, wk_ref, wv_ref,
    sorter_ref, bias_ref, gwo_ref, bsum_ref, dxc_ref, cross_land, small_land, small_stage,
    send, recv, small_send, small_recv, move_send, move_recv, local, *landing_refs,
):
    places = Places(groups)
    rows, cols_own = own_up.shape
    tokens, width = x_ref.shape
    seqs, _, block_len = qseg_ref.shape
    half = width // 2
    part = gbup_ref.shape[1] // 2
    head = places.head
    mine_cols = pl.ds(pl.multiple_of(head * half, half), half)
    their_cols = pl.ds(pl.multiple_of((1 - head) * half, half), half)

    pairs_in = [
        (q_hbm, q_ref), (k_hbm, k_ref), (v_hbm, v_ref), (g_hbm, g_ref),
        (up_hbm.at[:, :cols_own], own_up), (down_hbm.at[:, :cols_own], own_down),
        (x_hbm, x_ref), (xc_hbm, xc_ref), (ctx_hbm, ctx_ref), (gattnb_hbm, gattnb_ref),
        (sorter_hbm, sorter_ref), (gattn_hbm, dx_ref), (wq_hbm, wq_ref), (wk_hbm, wk_ref),
        (wv_hbm, wv_ref),
    ]
    loads = [
        pltpu.make_async_copy(source, target, local.at[at])
        for at, (source, target) in enumerate(pairs_in)
    ]
    for load in loads:
        load.start()
    places.greet()
    landing = {}
    for (at, axis, _), ref in zip(landing_shapes(items), landing_refs):
        landing.setdefault(at, {})[axis] = ref
    sums = Sums(
        items, places, [own_up, own_down, heads_own],
        [
            lambda cols: up_hbm.at[:, cols_own + cols.start : cols_own + cols.stop],
            lambda cols: down_hbm.at[:, cols_own + cols.start : cols_own + cols.stop],
            lambda cols: heads_other.at[:, cols],
        ],
        [total_up, total_down, total_heads], [out_up, out_down, out_heads], landing, send, recv,
    )

    each = tokens // MOVES

    def kept(at):
        return pl.ds(pl.multiple_of(head * tokens + at * each, each), each)

    my_rows = pl.ds(pl.multiple_of(head * tokens, tokens), tokens)

    def rows_copy():
        return remote(
            rows_hbm.at[:, their_cols], rows_all.at[my_rows], move_send.at[2 * MOVES],
            move_recv.at[2 * MOVES], places.partners["head"][0],
        )

    rows_keep = pltpu.make_async_copy(
        rows_hbm.at[:, mine_cols], rows_all.at[my_rows], local.at[len(pairs_in) + MOVES]
    )
    rows_keep.start()

    def cross_copy(at):
        here = slice(at * each, (at + 1) * each)
        return remote(
            dxc_ref.at[here], cross_land.at[here], move_send.at[at], move_recv.at[at],
            places.partners["x"][0],
        )

    def head_copy(at):
        here = slice(at * each, (at + 1) * each)
        return remote(
            dx_ref.at[here, their_cols], din_all.at[kept(at)], move_send.at[MOVES + at],
            move_recv.at[MOVES + at], places.partners["head"][0],
        )

    def keep_copy(at):
        here = slice(at * each, (at + 1) * each)
        return pltpu.make_async_copy(
            dx_ref.at[here, mine_cols], din_all.at[kept(at)], local.at[len(pairs_in) + at]
        )

    def move_copies(at, stage):
        return [cross_copy(at) if stage == 0 else head_copy(at)]

    def move(at, stage):
        here = slice(at * each, (at + 1) * each)
        if stage == 0:
            cross_copy(at).start()
        elif stage == 1:
            cross_copy(at).wait_recv()
            dx_ref[here, :] = dx_ref[here, :] + cross_land[here, :].astype(F32)
            head_copy(at).start()
            keep_copy(at).start()
        else:
            head_copy(at).wait_recv()
            keep_copy(at).wait()

    axes = small_axes(groups)

    def small_copies(stage):
        if stage == 0:
            device = places.partners["head"][0]
            spans = (
                (gvec_ref.at[:, their_cols], slice(0, half)),
                (bsum_ref.at[:, half:], slice(half, 2 * half)),
                (gbup_ref.at[:, part:], slice(2 * half, 2 * half + part)),
            )
            return [
                remote(
                    source, small_land.at[at, :, span], small_send.at[at], small_recv.at[at], device
                )
                for at, (source, span) in enumerate(spans)
            ]
        first = small_slot(axes[stage - 1])
        return [
            remote(
                small_stage.at[stage], small_land.at[first + d], small_send.at[first + d],
                small_recv.at[first + d], device,
            )
            for d, device in enumerate(places.partners[axes[stage - 1]])
        ]

    def small(stage):
        if stage == 1:
            for copy in small_copies(0):
                copy.wait_recv()
            small_stage[1, :, :half] = gvec_ref[:, mine_cols] + small_land[0, :, :half]
            small_stage[1, :, half : 2 * half] = (
                bsum_ref[:, :half] + small_land[1, :, half : 2 * half]
            )
            small_stage[1, :, 2 * half :] = gbup_ref[:, :part] + small_land[2, :, 2 * half :]
        elif stage > 1:
            value = small_stage[stage - 1]
            first = small_slot(axes[stage - 2])
            for d, copy in enumerate(small_copies(stage - 1)):
                copy.wait_recv()
                value = value + small_land[first + d]
            if stage <= len(axes):
                small_stage[stage] = value
            else:
                small_ref[...] = value
        if stage <= len(axes):
            for copy in small_copies(stage):
                copy.start()

    others = [item for item in items if isinstance(item, Other)]
    others[0].action, others[0].copies = small, small_copies
    for at, item in enumerate(others[1:]):
        item.action = functools.partial(move, at)
        item.copies = functools.partial(move_copies, at)

    pair_width = 2 * head_width
    pairs = width // pair_width
    batches = list(batches)
    for at in (4, 5):
        loads[at].wait()
    run_batch(sums, batches.pop(0))

    def steps(count, body):
        last = len(batches) == count

        @pl.loop(0, count)
        def _(step):
            body(step)
            for at in range(count - 1 if last else count):
                if batches[at]:
                    @pl.when(step == at)
                    def _():
                        run_batch(sums, batches[at])

        if last:
            run_batch(sums, batches[-1])
        del batches[:count]

    def attention(step):
        crossed = 1 - step // (pairs // 2 * seqs)
        seq = (step // (pairs // 2)) % seqs
        pair = crossed * (pairs // 2) + step % (pairs // 2)
        here = pl.ds(pl.multiple_of(seq * block_len, block_len), block_len)
        cols = pl.ds(pl.multiple_of(pair * pair_width, pair_width), pair_width)

        @pl.when(step % (pairs // 2) == 0)
        def _():
            fill_bias(bias_ref, qseg_ref[seq], kseg_ref[crossed, here, :])

        queries, keys = q_ref[here, cols], k_ref[here, cols]
        values, grads = v_ref[here, cols], g_ref[here, cols]
        logs = lse_ref[seq, pair]
        key_cols = keys.astype(F32).T.astype(BF16)
        lane = lax.broadcasted_iota(jnp.int32, (1, pair_width), 1)
        query_parts = []
        for at, low in enumerate(range(0, pair_width, head_width)):
            chosen = jnp.logical_and(lane >= low, lane < low + head_width)
            scores = dot(keys, jnp.where(chosen, queries, 0), 1, 1) + bias_ref[...]
            mixing = jnp.exp(scores - logs[at : at + 1, :])
            grad_mixing = dot(values, jnp.where(chosen, grads, 0), 1, 1)
            inner = jnp.sum(mixing * grad_mixing, axis=0, keepdims=True)
            grad_scores = (mixing * (grad_mixing - inner)).astype(BF16)
            grad_value = dot(mixing.astype(BF16), grads)
            grad_key = dot(grad_scores, queries)
            query_parts.append(dot(key_cols[low : low + head_width], grad_scores))
            if at == 0:
                all_value, all_key = grad_value, grad_key
            else:
                all_value = jnp.where(chosen, grad_value, all_value)
                all_key = jnp.where(chosen, grad_key, all_key)
        q_ref[here, cols] = (jnp.concatenate(query_parts, axis=0).T.astype(BF16) * scale).astype(
            BF16
        )
        k_ref[here, cols] = all_key.astype(BF16)
        v_ref[here, cols] = all_value.astype(BF16)

    for at in range(4):
        loads[at].wait()
    steps(seqs * pairs, attention)
    tile = 256
    for at in range(6, 11):
        loads[at].wait()

    def tile_of(step):
        return pl.ds(pl.multiple_of(step * tile, tile), tile)

    def weights(step):
        mine = tile_of(step)
        left, left_cross = x_ref[:, mine].T, xc_ref[:, mine].T
        for at, ref in enumerate((q_ref, k_ref, v_ref)):
            first = dot(left, ref[:, :half])
            second = dot(left if at == 0 else left_cross, ref[:, half:])
            found = jnp.concatenate([first, second], axis=1).astype(BF16)
            natural = dot(found, sorter_ref[...], 1, 1).astype(BF16)
            heads_own[mine, at * half : (at + 1) * half] = natural[:, :half]
            heads_other[mine, at * half : (at + 1) * half] = natural[:, half:]
        gwo_ref[mine, :] = dot(ctx_ref[:, mine].T, gattnb_ref[...]).astype(BF16)

    steps(width // tile, weights)

    def last_weight(_):
        for ref, low in ((heads_own, 0), (heads_other, half)):
            natural = dot(sorter_ref[low : low + half], gwo_ref[...]).astype(BF16)
            ref[:half, 3 * half :] = natural[:, :half]
            ref[half:, 3 * half :] = natural[:, half:]
        totals = []
        for ref in (q_ref, v_ref):
            totals.append(jnp.sum(ref[...].astype(F32), axis=0, keepdims=True))
        found = jnp.concatenate(totals + [jnp.zeros((6, width), F32)], axis=0)
        high = found.astype(BF16)
        rest = found - high.astype(F32)
        middle_part = rest.astype(BF16)
        rest = rest - middle_part.astype(F32)
        bsum_ref[...] = (
            dot(high, sorter_ref[...], 1, 1)
            + dot(middle_part, sorter_ref[...], 1, 1)
            + dot(rest.astype(BF16), sorter_ref[...], 1, 1)
        )

    steps(1, last_weight)
    rows_copy().start()
    for at in range(11, 15):
        loads[at].wait()

    def inputs(step):
        here = tile_of(step)
        dq, dk, dv = q_ref[here, :], k_ref[here, :], v_ref[here, :]
        dx_ref[here, :] = (
            dx_ref[here, :]
            + dot(dq, wq_ref[...], 1, 1)
            + dot(dk[:, :half], wk_ref[:, :half], 1, 1)
            + dot(dv[:, :half], wv_ref[:, :half], 1, 1)
        )
        dxc_ref[here, :] = (
            dot(dk[:, half:], wk_ref[:, half:], 1, 1) + dot(dv[:, half:], wv_ref[:, half:], 1, 1)
        ).astype(BF16)

    steps(tokens // tile, inputs)
    assert not batches
    rows_keep.wait()
    rows_copy().wait()
    sums.finish()


def attention_back(
    grads, tokens, weights, out_rows, logs, query_seg, keys_seg, grad_vecs, grad_bup, head_width,
    scale, groups,
):
    rows, cols = grads[0].shape[0], grads[0].shape[1] // 2
    count, width = tokens[0].shape
    seqs, block_len = query_seg.shape
    step = cols // 6
    items = make_items([0, 1], rows, cols, step, FFN_ORDERS, groups)
    items += make_items([2], rows, cols, step, HEAD_ORDERS, groups, len(items))
    pair_steps = seqs * width // (2 * head_width)
    tiles, weight_steps = count // 256, width // 256
    times = [2.3] * pair_steps + [4.0] * weight_steps + [1.5] + [1.8] * tiles
    ready = [0] * len(FFN_ORDERS) + [pair_steps + weight_steps + 1] * len(HEAD_ORDERS)
    small = (8, width + cols)
    items.append(Other([("head", 1e4)] + [(axis, 7e4) for axis in small_axes(groups)]))
    ready.append(pair_steps + weight_steps + 1)
    for at in range(MOVES):
        items.append(Other([("x", count // MOVES * width * 2), ("head", count // MOVES * width * 2)]))
        ready.append(pair_steps + weight_steps + 1 + (at + 1) * tiles // MOVES)
    batches = plan(items, times, ready)
    landing = landing_shapes(items)
    vmem = pl.BlockSpec(memory_space=pltpu.VMEM)
    anywhere = pl.BlockSpec(memory_space=pl.ANY)
    slots = len(FFN_ORDERS) + len(HEAD_ORDERS)
    small_slots = 5 + LINES - 1 + groups - 1
    big = pltpu.VMEM((rows, cols), BF16)
    rows_low = pltpu.VMEM((count, width), BF16)
    square = pltpu.VMEM((width, width), BF16)
    large = [*grads, *tokens, *weights, out_rows]
    return pl.pallas_call(
        functools.partial(back_kernel, items, batches, groups, head_width, scale),
        in_specs=[anywhere] * len(large) + [vmem] * 5,
        out_specs=[vmem] * 4 + [anywhere] * 2,
        out_shape=[jax.ShapeDtypeStruct((rows, cols), BF16)] * 3
        + [jax.ShapeDtypeStruct(small, F32)]
        + [jax.ShapeDtypeStruct((2 * count, width // 2), F32)] * 2,
        scratch_shapes=[big] * 7
        + [rows_low] * 8
        + [pltpu.VMEM((count, width), F32)]
        + [square] * 4
        + [pltpu.VMEM((block_len, block_len), F32), square, pltpu.VMEM((8, width), F32)]
        + [rows_low] * 2
        + [pltpu.VMEM((small_slots, *small), F32), pltpu.VMEM((6, *small), F32)]
        + [pltpu.SemaphoreType.DMA((slots, slot_count(groups)))] * 2
        + [pltpu.SemaphoreType.DMA((small_slots,))] * 2
        + [pltpu.SemaphoreType.DMA((2 * MOVES + 1,))] * 2
        + [pltpu.SemaphoreType.DMA((len(large) + MOVES + 1,))]
        + [pltpu.VMEM(shape, BF16) for _, _, shape in landing],
        compiler_params=pltpu.CompilerParams(
            collective_id=1, has_side_effects=True, vmem_limit_bytes=63 * MIB
        ),
        name="attention_back",
    )(
        *large, logs, query_seg[:, None, :], keys_seg[:, :, None], grad_vecs, grad_bup
    )


def finish_kernel(up_ref, down_ref, heads_ref, gup_ref, gdown_ref, gq_ref, gk_ref, gv_ref, go_ref):
    width = gq_ref.shape[1]
    gup_ref[...] = up_ref[...].astype(F32)
    gdown_ref[...] = down_ref[...].astype(F32).T
    for at, ref in enumerate((gq_ref, gk_ref, gv_ref, go_ref)):
        ref[...] = heads_ref[:, at * width : (at + 1) * width].astype(F32)


def finish(up, down, heads):
    rows, cols = up.shape
    steps = 6
    tile = rows // steps
    half, quarter = cols // 2, cols // 4
    spec = pl.BlockSpec((tile, cols), lambda i: (i, 0))
    third = pl.BlockSpec((tile, quarter), lambda i: (i, 0))
    return pl.pallas_call(
        finish_kernel,
        grid=(steps,),
        in_specs=[spec, pl.BlockSpec((rows, cols // steps), lambda i: (0, i)), spec],
        out_specs=[
            spec,
            pl.BlockSpec((cols // steps, rows), lambda i: (i, 0)),
            third,
            third,
            third,
            pl.BlockSpec((tile, quarter), lambda i: (i % (steps // 2), i // (steps // 2))),
        ],
        out_shape=[
            jax.ShapeDtypeStruct((rows, cols), F32),
            jax.ShapeDtypeStruct((cols, rows), F32),
            jax.ShapeDtypeStruct((rows, quarter), F32),
            jax.ShapeDtypeStruct((rows, quarter), F32),
            jax.ShapeDtypeStruct((rows, quarter), F32),
            jax.ShapeDtypeStruct((rows // 2, half), F32),
        ],
        compiler_params=pltpu.CompilerParams(vmem_limit_bytes=48 * MIB),
        name="finish",
    )(up, down, heads)


def on_device(
    layer_in, segments, block_perm, w_query, b_query, w_key, w_value, b_value, w_attn_out,
    b_attn_out, norm1_gain, norm1_bias, w_up, b_up, w_down, b_down, norm2_gain, norm2_bias,
    grad_out,
):
    seq_count, block_len, half = layer_in.shape
    local_heads, block_count = block_perm.shape
    head_width = w_query.shape[1] // local_heads
    seqs = seq_count // 2
    scale = head_width ** (-0.5)
    head = lax.axis_index("head")
    my_block = lax.axis_index("blk")

    own_place = jnp.where(jnp.arange(block_count)[None, :] == my_block, block_perm, 0)
    crossed = jnp.repeat((jnp.sum(own_place, axis=1) != my_block).astype(F32), head_width)
    row = lax.broadcasted_iota(jnp.int32, (16, half), 0)
    vecs = jnp.pad(b_up.reshape(-1, half), ((8, 16 - 8 - b_up.shape[0] // half), (0, 0)))
    listed = [
        b_attn_out, norm1_gain, norm1_bias, b_down, norm2_gain, norm2_bias, b_query, b_value,
    ]
    for at, vec in [*enumerate(listed), (12, crossed)]:
        vecs = jnp.where(row == at, vec[None, :], vecs)

    my_segments = lax.dynamic_slice_in_dim(segments, head * seqs, seqs, 0)
    own_seg = lax.dynamic_slice_in_dim(my_segments, my_block * block_len, block_len, 1)
    cross_seg = lax.dynamic_slice_in_dim(my_segments, (1 - my_block) * block_len, block_len, 1)
    keys_seg = jnp.stack([own_seg.reshape(-1), cross_seg.reshape(-1)])
    (
        x, x_cross, queries, keys, values, ctx, wq, wk, wv, wo, sorter, up_other, down_other,
        grad_rows, vectors, b_up_all, logs,
    ) = front(
        layer_in.reshape(-1, half),
        grad_out.reshape(-1, half),
        (w_query, w_key, w_value, w_attn_out, w_up, w_down),
        vecs,
        own_seg,
        keys_seg,
        head_width,
        scale,
    )
    (
        out_rows, grad_attn, grad_attn_low, grad_ctx, grad_vecs, grad_bup, grad_up_all,
        grad_down_all,
    ) = middle(
        ctx, x, grad_rows, vectors, b_up_all, wo, (w_up, up_other), (w_down, down_other)
    )
    total_up, total_down, total_heads, small, grad_in, layer_out = attention_back(
        (grad_up_all, grad_down_all),
        (queries, keys, values, grad_ctx, x, x_cross, ctx, grad_attn_low, grad_attn),
        (wq, wk, wv, sorter),
        out_rows,
        logs,
        own_seg,
        keys_seg,
        grad_vecs,
        grad_bup,
        head_width,
        scale,
        lax.axis_size("dp") // (2 * LINES),
    )
    grad_up, grad_down, grad_q, grad_k, grad_v, grad_o = finish(total_up, total_down, total_heads)
    return (
        layer_out.reshape(layer_in.shape),
        grad_in.reshape(layer_in.shape),
        grad_q,
        small[0, half : 2 * half],
        grad_k,
        grad_v,
        small[1, half : 2 * half],
        grad_o,
        small[0, :half],
        small[1, :half],
        small[2, :half],
        grad_up,
        small[0, 2 * half :],
        grad_down,
        small[3, :half],
        small[4, :half],
        small[5, :half],
    )


def solution(mesh):
    rows, cols, vec = P("head", None), P(None, "head"), P("head")
    tokens = P("dp", "blk", "head")
    return jax.shard_map(
        on_device,
        mesh=mesh,
        in_specs=(
            tokens, P("dp", None), rows, cols, vec, cols, cols, vec, rows, vec, vec, vec, cols,
            vec, rows, vec, vec, vec, tokens,
        ),
        out_specs=(
            tokens, tokens, cols, vec, cols, cols, vec, rows, vec, vec, vec, cols, vec, rows, vec,
            vec, vec,
        ),
        check_vma=False,
    )
```

```python
import functools

import jax
import jax.numpy as jnp
from jax import lax
from jax.experimental import pallas as pl
from jax.experimental.pallas import tpu as pltpu
from jax.sharding import PartitionSpec as P

EPSILON = 1e-05
NEGATIVE = -1e30
ROOT_HALF = 0.7071067811865476
DENSITY_SCALE = 0.3989422804014327
F32 = jnp.float32
BF16 = jnp.bfloat16
MIB = 1 << 20


def dot(left, right, left_dim=1, right_dim=0):
    return lax.dot_general(
        left, right, (((left_dim,), (right_dim,)), ((), ())), preferred_element_type=F32
    )


def fill_bias(bias_ref, query_seg, keys_seg):
    same = keys_seg == query_seg
    covered = jnp.max(jnp.where(same, 1.0, 0.0), axis=0, keepdims=True)
    bias_ref[...] = jnp.where(same, 0.0, covered * NEGATIVE)


def attend_pair(queries, keys, values, bias, head_width):
    pair_width = queries.shape[1]
    value_cols = values.astype(F32).T.astype(BF16)
    lane = lax.broadcasted_iota(jnp.int32, (1, pair_width), 1)
    parts, logs = [], []
    for low in range(0, pair_width, head_width):
        chosen = jnp.logical_and(lane >= low, lane < low + head_width)
        scores = dot(keys, jnp.where(chosen, queries, 0), 1, 1) + bias[...]
        top = jnp.max(scores, axis=0, keepdims=True)
        shifted = jnp.exp(scores - top)
        total = jnp.sum(shifted, axis=0, keepdims=True)
        context = dot(value_cols[low : low + head_width], shifted.astype(BF16))
        parts.append(context * (1.0 / total))
        logs.append(top + jnp.log(total))
    return jnp.concatenate(parts, axis=0).T.astype(BF16), jnp.concatenate(logs, axis=0)


def split_dot(left, right, left_dim=1, right_dim=0):
    high = left.astype(BF16)
    rest = left - high.astype(F32)
    mid = rest.astype(BF16)
    low = (rest - mid.astype(F32)).astype(BF16)
    return sum(dot(x, right, left_dim, right_dim) for x in (high, mid, low))


def front_kernel(
    head_width, scale, seqs,
    layer_hbm, gout_hbm, wq_hbm, wk_hbm, wv_hbm, wo_hbm, wup_hbm, wdn_hbm, vec_own, qseg_ref,
    kseg_ref,
    x_hbm, xc_hbm, q_hbm, k_hbm, v_hbm, ctx_hbm, wqs_hbm, wks_hbm, wvs_hbm, wos_hbm, sorter_hbm,
    wup_other, wdn_other, grad_hbm, vec_all, bup_all, lse_ref,
    x_ref, xc_ref, q_ref, k_ref, v_ref, ctx_ref, wn_q, wn_k, wn_v, wn_o, ws_q, ws_k, ws_v, ws_o,
    sorter_ref, sorter_t, vec_land, bias_ref, local, send, recv,
):
    head, blk = lax.axis_index("head"), lax.axis_index("blk")
    to_head, to_cross = {"head": 1 - head}, {"blk": 1 - blk}
    rows, width = x_ref.shape
    half = width // 2
    block_len = rows // seqs
    my_rows = pl.ds(pl.multiple_of(head * rows, rows), rows)
    their_rows = pl.ds(pl.multiple_of((1 - head) * rows, rows), rows)
    mine = pl.ds(pl.multiple_of(head * half, half), half)
    theirs = pl.ds(pl.multiple_of((1 - head) * half, half), half)

    started = []

    def bring(at, source, target):
        copy = pltpu.make_async_copy(source, target, local.at[at])
        copy.start()
        return copy

    def give(at, source, target, device):
        copy = remote(source, target, send.at[at], recv.at[at], device)
        copy.start()
        started.append(copy)
        return copy

    barrier = pltpu.get_barrier_semaphore()
    for device in (to_head, to_cross):
        pl.semaphore_signal(barrier, inc=1, device_id=device, device_id_type=pl.DeviceIdType.MESH)
    own_x = bring(0, layer_hbm.at[my_rows], x_ref.at[:, mine])
    own_w = [
        bring(1, wq_hbm, wn_q.at[:, :half]),
        bring(2, wk_hbm, wn_k.at[:, :half]),
        bring(3, wv_hbm, wn_v.at[:, :half]),
        bring(4, wo_hbm, wn_o.at[:half]),
    ]
    own_grad = bring(5, gout_hbm.at[my_rows], grad_hbm.at[:, mine])
    pl.semaphore_wait(barrier, 2)

    def seq_rows(seq):
        return slice(seq * block_len, (seq + 1) * block_len)

    def block_of(seq):
        return pl.ds(pl.multiple_of(head * rows + seq * block_len, block_len), block_len)

    vecs = give(0, vec_own, vec_land, to_head)
    features = give(1, layer_hbm.at[their_rows], x_ref.at[:, mine], to_head)
    cross = [[give(2, layer_hbm.at[block_of(0)], xc_ref.at[seq_rows(0), mine], to_cross)]]
    other_w = [
        give(3, wq_hbm, wn_q.at[:, half:], to_head),
        give(4, wk_hbm, wn_k.at[:, half:], to_head),
        give(5, wv_hbm, wn_v.at[:, half:], to_head),
        give(6, wo_hbm, wn_o.at[half:], to_head),
    ]
    features.wait_recv()
    base = 7
    for seq in range(seqs):
        if seq > 0:
            cross.append(
                [give(base, layer_hbm.at[block_of(seq)], xc_ref.at[seq_rows(seq), mine], to_cross)]
            )
            base += 1
        here = seq_rows(seq)
        cross[seq].append(give(base, x_ref.at[here, theirs], xc_ref.at[here, theirs], to_cross))
        base += 1
    later = [
        give(base, wup_hbm, wup_other, to_head),
        give(base + 1, wdn_hbm, wdn_other, to_head),
        give(base + 2, gout_hbm.at[their_rows], grad_hbm.at[:, mine], to_head),
    ]

    vecs.wait_recv()
    crossed = jnp.concatenate([vec_own[12:13, :], vec_land[12:13, :]], axis=1)
    row = lax.broadcasted_iota(jnp.int32, (width, width), 0)
    col = lax.broadcasted_iota(jnp.int32, (width, width), 1)
    earlier = jnp.where(row // head_width < col // head_width, 1.0, 0.0).astype(BF16)
    before = dot(jnp.broadcast_to(crossed, (8, width)).astype(BF16), earlier)[0:1]
    lane = lax.broadcasted_iota(jnp.int32, (1, width), 1)
    place = jnp.where(
        crossed > 0.5, half + before + (lane % head_width).astype(F32), lane.astype(F32) - before
    )
    found = jnp.where(row.astype(F32) == place, 1.0, 0.0)
    sorter_t[...] = found.astype(BF16)
    sorter_ref[...] = found.T.astype(BF16)
    vec_all[:, mine] = vec_own[0:8, :]
    vec_all[:, theirs] = vec_land[0:8, :]
    for at in range(bup_all.shape[1] // half):
        source = vec_own if at < 4 else vec_land
        bup_all[:, at * half : (at + 1) * half] = source[8 + at % 4 : 9 + at % 4, :]
    b_local = jnp.concatenate([vec_own[0:8, :], vec_land[0:8, :]], axis=1)
    b_sorted = split_dot(b_local, sorter_ref[...])
    bq, bv = b_sorted[6:7], b_sorted[7:8]

    out = []
    pairs_w = ((wn_q, ws_q, wqs_hbm), (wn_k, ws_k, wks_hbm), (wn_v, ws_v, wvs_hbm))
    for at, (natural, ordered, target) in enumerate(pairs_w):
        own_w[at].wait()
        other_w[at].wait_recv()
        ordered[...] = dot(natural[...], sorter_ref[...]).astype(BF16)
        out.append(bring(6 + at, ordered, target))
    out.append(bring(9, sorter_ref, sorter_hbm))
    own_x.wait()
    out.append(bring(10, x_ref, x_hbm))
    x = x_ref[...]
    q_ref[...] = ((dot(x, ws_q[...]) + bq) * scale).astype(BF16)
    out.append(bring(11, q_ref, q_hbm))
    k_ref[:, :half] = dot(x, ws_k[:, :half]).astype(BF16)
    v_ref[:, :half] = (dot(x, ws_v[:, :half]) + bv[:, :half]).astype(BF16)

    pair_width = 2 * head_width
    pairs = half // pair_width

    def attention(seq, first_pair, kind):
        here = pl.ds(pl.multiple_of(seq * block_len, block_len), block_len)
        fill_bias(bias_ref, qseg_ref[seq], kseg_ref[kind, here, :])

        @pl.loop(0, pairs)
        def _(at):
            pair = first_pair + at
            cols = pl.ds(pl.multiple_of(pair * pair_width, pair_width), pair_width)
            context, logs = attend_pair(
                q_ref[here, cols], k_ref[here, cols], v_ref[here, cols], bias_ref, head_width
            )
            ctx_ref[here, cols] = context
            lse_ref[seq, pair] = logs

    @pl.loop(0, seqs)
    def _(seq):
        attention(seq, 0, 0)

    own_w[3].wait()
    other_w[3].wait_recv()
    ws_o[...] = dot(sorter_t[...], wn_o[...]).astype(BF16)
    out.append(bring(12, ws_o, wos_hbm))
    for seq in range(seqs):
        here = seq_rows(seq)
        for copy in cross[seq]:
            copy.wait_recv()
        x_cross = xc_ref[here, :]
        k_ref[here, half:] = dot(x_cross, ws_k[:, half:]).astype(BF16)
        v_ref[here, half:] = (dot(x_cross, ws_v[:, half:]) + bv[:, half:]).astype(BF16)
        attention(seq, pairs, 1)
    out.append(bring(13, xc_ref, xc_hbm))
    out.append(bring(14, k_ref, k_hbm))
    out.append(bring(15, v_ref, v_hbm))
    out.append(bring(16, ctx_ref, ctx_hbm))
    own_grad.wait()
    for copy in later:
        copy.wait_recv()
    for copy in out:
        copy.wait()
    for copy in started:
        copy.wait_send()


def front(layer_in, grad_out, weights, vecs, query_seg, keys_seg, head_width, scale):
    width = weights[0].shape[0]
    half = width // 2
    seqs, block_len = query_seg.shape
    rows = seqs * block_len
    part = weights[4].shape[1]
    anywhere = pl.BlockSpec(memory_space=pl.ANY)
    vmem = pl.BlockSpec(memory_space=pltpu.VMEM)
    tokens = jax.ShapeDtypeStruct((rows, width), BF16)
    square = jax.ShapeDtypeStruct((width, width), BF16)
    low_rows, low_square = pltpu.VMEM((rows, width), BF16), pltpu.VMEM((width, width), BF16)
    copies = 7 + 2 * seqs - 1 + 3
    return pl.pallas_call(
        functools.partial(front_kernel, head_width, scale, seqs),
        in_specs=[anywhere] * 8 + [vmem] * 3,
        out_specs=[anywhere] * 14 + [vmem] * 3,
        out_shape=[tokens] * 6
        + [square] * 5
        + [
            jax.ShapeDtypeStruct(weights[4].shape, BF16),
            jax.ShapeDtypeStruct(weights[5].shape, BF16),
            jax.ShapeDtypeStruct((rows, width), F32),
            jax.ShapeDtypeStruct((8, width), F32),
            jax.ShapeDtypeStruct((1, 2 * part), F32),
            jax.ShapeDtypeStruct((seqs, width // (2 * head_width), 2, block_len), F32),
        ],
        scratch_shapes=[low_rows] * 6
        + [low_square] * 10
        + [
            pltpu.VMEM((16, half), F32),
            pltpu.VMEM((block_len, block_len), F32),
            pltpu.SemaphoreType.DMA((17,)),
            pltpu.SemaphoreType.DMA((copies,)),
            pltpu.SemaphoreType.DMA((copies,)),
        ],
        compiler_params=pltpu.CompilerParams(
            collective_id=3, has_side_effects=True, vmem_limit_bytes=60 * MIB
        ),
        name="front",
    )(
        layer_in, grad_out, *weights, vecs, query_seg[:, None, :], keys_seg[:, :, None]
    )


def unit_rows(rows, width):
    mean = jnp.sum(rows, axis=1, keepdims=True) * (1.0 / width)
    centered = rows - mean
    variance = jnp.sum(centered * centered, axis=1, keepdims=True) * (1.0 / width)
    inverse = lax.rsqrt(variance + EPSILON)
    return centered * inverse, inverse


def unit_back(grad, unit, inverse, gain, width):
    scaled = grad * gain
    plain = jnp.sum(scaled, axis=1, keepdims=True) * (1.0 / width)
    along = jnp.sum(scaled * unit, axis=1, keepdims=True) * (1.0 / width)
    return (scaled - plain - unit * along) * inverse


def middle_kernel(
    chunk, tiles, ctx_ref, x_ref, gout_ref, vec_ref, bup_ref, wo_ref,
    wup0_ref, wup1_ref, wdn0_ref, wdn1_ref,
    out_ref, gattn_ref, gattnb_ref, gctx_ref, gvec_ref, gbup_ref, gwup_ref, gwdn_ref,
    slope_ref, act_ref, gup_ref, normed_t, gffn_t,
):
    tile, width = x_ref.shape
    part = wup0_ref.shape[1]
    at_step = pl.program_id(0)

    @pl.when(at_step == 0)
    def _():
        gvec_ref[...] = jnp.zeros_like(gvec_ref)
        gbup_ref[...] = jnp.zeros_like(gbup_ref)

    def vec(i):
        return vec_ref[i : i + 1, :]

    def add_vec(i, rows):
        gvec_ref[i : i + 1, :] += jnp.sum(rows, axis=0, keepdims=True)

    @pl.when(at_step < tiles)
    def _():
        here = pl.ds(pl.multiple_of(at_step * tile, tile), tile)
        attended = dot(ctx_ref[...], wo_ref[...])
        unit1, inverse1 = unit_rows(x_ref[...].astype(F32) + attended + vec(0), width)
        normed = unit1 * vec(1) + vec(2)
        normed_low = normed.astype(BF16)
        normed_t[:, here] = normed_low.T
        pieces = ((wup0_ref, wdn0_ref), (wup1_ref, wdn1_ref))
        down = jnp.zeros_like(normed)
        for at, (wup, wdn) in enumerate(pieces):
            for low in range(0, part, chunk):
                cols = slice(at * part + low, at * part + low + chunk)
                up = dot(normed_low, wup[:, low : low + chunk]) + bup_ref[:, cols]
                cumulative = 0.5 + 0.5 * lax.erf(up * ROOT_HALF)
                slope_ref[:, cols] = cumulative + up * (jnp.exp(-0.5 * up * up) * DENSITY_SCALE)
                activated = (up * cumulative).astype(BF16)
                act_ref[here, cols] = activated
                down += dot(activated, wdn[low : low + chunk, :])
        unit2, inverse2 = unit_rows(normed + down + vec(3), width)
        out_ref[...] = unit2 * vec(4) + vec(5)
        grad_out = gout_ref[...]
        add_vec(4, grad_out * unit2)
        add_vec(5, grad_out)
        grad_ffn = unit_back(grad_out, unit2, inverse2, vec(4), width)
        add_vec(3, grad_ffn)
        grad_ffn_low = grad_ffn.astype(BF16)
        gffn_t[:, here] = grad_ffn_low.T
        back = jnp.zeros_like(normed)
        for at, (wup, wdn) in enumerate(pieces):
            for low in range(0, part, chunk):
                cols = slice(at * part + low, at * part + low + chunk)
                grad_act = dot(grad_ffn_low, wdn[low : low + chunk, :], 1, 1)
                grad_up = (grad_act * slope_ref[:, cols]).astype(BF16)
                gup_ref[here, cols] = grad_up
                gbup_ref[0:1, cols] += jnp.sum(grad_up.astype(F32), axis=0, keepdims=True)
                back += dot(grad_up, wup[:, low : low + chunk], 1, 1)
        grad_mid = grad_ffn + back
        add_vec(1, grad_mid * unit1)
        add_vec(2, grad_mid)
        grad_attn = unit_back(grad_mid, unit1, inverse1, vec(1), width)
        add_vec(0, grad_attn)
        gattn_ref[...] = grad_attn
        grad_attn_low = grad_attn.astype(BF16)
        gattnb_ref[...] = grad_attn_low
        gctx_ref[...] = dot(grad_attn_low, wo_ref[...], 1, 1).astype(BF16)

    @pl.when(at_step >= tiles)
    def _():
        cols_step = gwup_ref.shape[1]
        cols = pl.ds(pl.multiple_of((at_step - tiles) * cols_step, cols_step), cols_step)
        gwup_ref[...] = dot(normed_t[...], gup_ref[:, cols]).astype(BF16)
        gwdn_ref[...] = dot(gffn_t[...], act_ref[:, cols]).astype(BF16)


def middle(ctx, x, grad_out, vectors, b_up, w_out, w_up, w_down):
    rows, width = x.shape
    part = w_up[0].shape[1]
    tile = 256
    tiles = rows // tile
    chunk = part // 2
    cols_step = part // 3

    def tiled(cols):
        return pl.BlockSpec((tile, cols), lambda i: (jnp.minimum(i, tiles - 1), 0))

    def whole(array):
        return pl.BlockSpec(array.shape, lambda i: (0, 0), pipeline_mode=pl.Buffered(1))

    def shape(cols, kind):
        return jax.ShapeDtypeStruct((rows, cols), kind)

    outs = [(width, F32), (width, F32), (width, BF16), (width, BF16)]
    sums = [jax.ShapeDtypeStruct((8, width), F32), jax.ShapeDtypeStruct((8, b_up.shape[1]), F32)]
    grads = [jax.ShapeDtypeStruct((width, 2 * part), BF16)] * 2
    grad_spec = pl.BlockSpec((width, cols_step), lambda i: (0, jnp.maximum(i - tiles, 0)))
    weights = [vectors, b_up, w_out, *w_up, *w_down]
    return pl.pallas_call(
        functools.partial(middle_kernel, chunk, tiles),
        grid=(tiles + 2 * part // cols_step,),
        in_specs=[tiled(width), tiled(width), tiled(width)]
        + [whole(w) for w in weights],
        out_specs=[tiled(c) for c, _ in outs]
        + [pl.BlockSpec(s.shape, lambda i: (0, 0)) for s in sums]
        + [grad_spec] * 2,
        out_shape=[shape(c, k) for c, k in outs] + sums + grads,
        scratch_shapes=[
            pltpu.VMEM((tile, 2 * part), F32),
            pltpu.VMEM((rows, 2 * part), BF16),
            pltpu.VMEM((rows, 2 * part), BF16),
            pltpu.VMEM((width, rows), BF16),
            pltpu.VMEM((width, rows), BF16),
        ],
        compiler_params=pltpu.CompilerParams(vmem_limit_bytes=60 * MIB),
        name="middle",
    )(ctx, x, grad_out, *weights)


LINKS = {
    "head": (("core", 1),),
    "x": (("x", 1),),
    "y": (("y", 1),),
    "u": (("outer", 1),),
    "w": (("outer", 1), ("inner", 2)),
    "group": (("group", 1),),
}
RATES = {"core": 500e3, "x": 46e3, "y": 46e3, "outer": 46e3, "inner": 46e3, "group": 46e3}
DELAY = 4.5
OP_TIME = 0.3
ORDERS = {
    "A": "xyuw", "B": "yxuw", "C": "uwxy", "D": "uxyw", "E": "xuyw", "F": "yuxw", "G": "uyxw",
    "H": "uwyx",
}


class Item:
    action = None
    later = 0

    def __init__(self, at, array, first, cols, rows, order, groups):
        self.at, self.array, self.first, self.cols, self.rows = at, array, first, cols, rows
        self.groups = groups
        self.sums = []
        size = rows
        for axis in [*ORDERS[order]] + (["group"] if groups > 1 else []):
            before = size
            size = size if axis == "group" else size // 2
            self.sums.append((axis, before, size))
        self.size = size
        self.stages = (
            [("head", "head", rows, rows)]
            + [("sum", *s) for s in self.sums]
            + [("result", *s) for s in reversed(self.sums) if s[0] != "group"]
        )

    def load(self, stage):
        kind, axis, before, size = self.stages[stage]
        moved = size * (self.groups - 1 if axis == "group" else 1)
        return axis, moved * self.cols * 2


def plan(items, steps, ready):
    free = {link: 0.0 for link in RATES}
    due = [[0.0, 0] for _ in items]
    batches = []
    now = 0.0

    def rank(i):
        return (due[i][0], -due[i][1])

    def run(index, batch):
        nonlocal now
        item, (_, stage) = items[index], due[index]
        batch.append((index, stage))
        now += OP_TIME
        if stage == len(item.stages):
            due[index] = None
            return
        axis, size = item.load(stage)
        end = now
        for link, times in LINKS[axis]:
            free[link] = max(free[link], now) + times * size / RATES[link]
            end = max(end, free[link])
        due[index] = [end + DELAY, stage + 1]

    for at, time in enumerate([0.0] + steps):
        now += time
        batch = []
        while True:
            able = [
                i
                for i, d in enumerate(due)
                if d is not None
                and d[0] <= now
                and at >= (items[i].later if d[1] else ready[i])
            ]
            if not able:
                break
            run(min(able, key=rank), batch)
        batches.append(batch)
    batch = batches[-1]
    while any(d is not None for d in due):
        able = [i for i, d in enumerate(due) if d is not None]
        here = [i for i in able if due[i][0] <= now]
        first = min(here, key=rank) if here else min(able, key=lambda i: due[i][0])
        now = max(now, due[first][0])
        run(first, batch)
    return batches


class Places:
    def __init__(self, groups):
        head, blk, dp = lax.axis_index("head"), lax.axis_index("blk"), lax.axis_index("dp")
        group = dp // 8
        self.head = head
        self.bit = {"x": blk, "y": dp % 2, "u": (dp // 2) % 2, "w": (dp // 4) % 2}
        self.partners = {
            "head": [{"head": 1 - head}],
            "x": [{"blk": 1 - blk}],
            "y": [{"dp": dp + 1 - 2 * self.bit["y"]}],
            "u": [{"dp": dp + 2 - 4 * self.bit["u"]}],
            "w": [{"dp": dp + 4 - 8 * self.bit["w"]}],
            "group": [{"dp": (group + d) % groups * 8 + dp % 8} for d in range(1, groups)],
        }

    def greet(self):
        barrier = pltpu.get_barrier_semaphore()
        everyone = [device for devices in self.partners.values() for device in devices]
        for device in everyone:
            pl.semaphore_signal(
                barrier, inc=1, device_id=device, device_id_type=pl.DeviceIdType.MESH
            )
        pl.semaphore_wait(barrier, len(everyone))


def remote(source, target, send, recv, device):
    return pltpu.make_async_remote_copy(
        src_ref=source,
        dst_ref=target,
        send_sem=send,
        recv_sem=recv,
        device_id=device,
        device_id_type=pl.DeviceIdType.MESH,
    )


SUM_SLOT = {"x": 1, "y": 2, "u": 3, "w": 4, "group": 9}
RESULT_SLOT = {"x": 5, "y": 6, "u": 7, "w": 8}


def slot_count(groups):
    return 9 + groups - 1


class Sums:
    def __init__(self, items, places, own, other, total, result, landing, send, recv):
        self.items, self.places = items, places
        self.own, self.other, self.total, self.result = own, other, total, result
        self.landing, self.send, self.recv = landing, send, recv
        self.sent = []

    def start_of(self, item, stop):
        start = 0
        for name, before, after in item.sums:
            if name == stop:
                return start
            start = self.within(start, name, after)
        return start

    def within(self, start, axis, after):
        if axis == "group":
            return start
        return start + self.places.bit[axis] * after

    def part(self, ref, start, size, item):
        return ref.at[
            pl.ds(pl.multiple_of(start, 16), size), item.first : item.first + item.cols
        ]

    def copies_of(self, item, stage):
        kind, axis, before, after = item.stages[stage]
        devices = self.places.partners[axis]
        out = []

        def add(source, target, slot, device):
            out.append(
                remote(
                    source, target, self.send.at[item.at, slot], self.recv.at[item.at, slot], device
                )
            )

        if kind == "head":
            cols = slice(item.first, item.first + item.cols)
            add(self.other[item.array](cols), self.total[item.array].at[:, cols], 0, devices[0])
            return out
        if kind == "sum":
            start = self.start_of(item, axis)
            ref = self.total[item.array]
            buf = self.landing[item.at][axis]
            for d, device in enumerate(devices):
                if axis == "group":
                    row = start
                else:
                    row = start + (1 - self.places.bit[axis]) * after
                add(self.part(ref, row, after, item), buf.at[d], SUM_SLOT[axis] + d, device)
            return out
        start, size = self.held(item, stage)
        here = self.part(self.result[item.array], start, size, item)
        for device in devices:
            add(here, here, RESULT_SLOT[axis], device)
        return out

    def held(self, item, stage):
        start, size = self.start_of(item, None), item.size
        for kind, axis, before, after in item.stages[:stage]:
            if kind == "result":
                start, size = self.start_of(item, axis), before
        return start, size

    def op(self, index, stage):
        item = self.items[index]
        if item.action is not None:
            item.action(stage)
            if stage < len(item.stages):
                self.sent.append((item, stage))
            return
        if stage > 0:
            kind, axis, before, after = item.stages[stage - 1]
            copies = self.copies_of(item, stage - 1)
            for copy in copies:
                copy.wait_recv()
            if kind == "head":
                cols = slice(item.first, item.first + item.cols)
                total = self.total[item.array]
                total[:, cols] = (
                    self.own[item.array][:, cols].astype(F32) + total[:, cols].astype(F32)
                ).astype(BF16)
            elif kind == "sum":
                start = self.within(self.start_of(item, axis), axis, after)
                here = self.part(self.total[item.array], start, after, item)
                value = here[...].astype(F32)
                for d in range(len(copies)):
                    value = value + self.landing[item.at][axis][d].astype(F32)
                if item.stages[stage][0] != "result":
                    here[...] = value.astype(BF16)
                else:
                    self.part(self.result[item.array], start, after, item)[...] = value.astype(BF16)
        if stage < len(item.stages):
            for copy in self.copies_of(item, stage):
                copy.start()
            self.sent.append((item, stage))

    def finish(self):
        for item, stage in self.sent:
            copies = self.copies_of(item, stage) if item.action is None else item.copies(stage)
            for copy in copies:
                copy.wait_send()


class Other:
    def __init__(self, loads):
        self.stages, self.action, self.copies = loads, None, None
        self.later = 0

    def load(self, stage):
        return self.stages[stage]


def landing_shapes(items):
    shapes = []
    for item in items:
        if isinstance(item, Other):
            continue
        for kind, axis, before, after in item.stages:
            if kind == "sum":
                slots = item.groups - 1 if axis == "group" else 1
                shapes.append((item.at, axis, (slots, after, item.cols)))
    return shapes


def make_items(arrays, rows, cols, orders, groups, at=0):
    items = []
    step = len(arrays) * cols // len(orders)
    for index in range(len(orders)):
        array, first = divmod(index * step, cols)
        items.append(Item(at + index, arrays[array], first, step, rows, orders[index], groups))
    return items


def run_batch(sums, batch):
    for index, stage in batch:
        sums.op(index, stage)


FFN_ORDERS = "AABFFFCG"
HEAD_ORDERS = "DBEBBE"
MOVES = 4


def small_axes(groups):
    return ("x", "y", "u", "w") + (("group",) if groups > 1 else ())


def small_slot(axis):
    return 3 + {"x": 0, "y": 1, "u": 2, "w": 3, "group": 4}[axis]


def back_kernel(
    items, batches, groups, head_width, scale,
    up_hbm, down_hbm, q_hbm, k_hbm, v_hbm, g_hbm, x_hbm, xc_hbm, ctx_hbm, gattnb_hbm, gattn_hbm,
    wq_hbm, wk_hbm, wv_hbm, sorter_hbm, rows_hbm, lse_ref, qseg_ref, kseg_ref, gvec_ref, gbup_ref,
    out_up, out_down, out_heads, small_ref, din_all, rows_all,
    own_up, own_down, total_up, total_down, total_heads, heads_own, heads_other,
    q_ref, k_ref, v_ref, g_ref, x_ref, xc_ref, ctx_ref, gattnb_ref, dx_ref, wq_ref, wk_ref, wv_ref,
    sorter_ref, bias_ref, gwo_ref, bsum_ref, dxc_ref, cross_land, small_land, small_stage,
    send, recv, small_send, small_recv, move_send, move_recv, local, *landing_refs,
):
    places = Places(groups)
    rows, cols_own = own_up.shape
    tokens, width = x_ref.shape
    seqs, _, block_len = qseg_ref.shape
    half = width // 2
    part = gbup_ref.shape[1] // 2
    head = places.head
    mine_cols = pl.ds(pl.multiple_of(head * half, half), half)
    their_cols = pl.ds(pl.multiple_of((1 - head) * half, half), half)

    pairs_in = [
        (q_hbm, q_ref), (k_hbm, k_ref), (v_hbm, v_ref), (g_hbm, g_ref),
        (up_hbm.at[:, :cols_own], own_up), (down_hbm.at[:, :cols_own], own_down),
        (wk_hbm, wk_ref), (wv_hbm, wv_ref), (x_hbm, x_ref), (xc_hbm, xc_ref), (ctx_hbm, ctx_ref),
        (gattnb_hbm, gattnb_ref), (sorter_hbm, sorter_ref), (gattn_hbm, dx_ref), (wq_hbm, wq_ref),
    ]
    loads = [
        pltpu.make_async_copy(source, target, local.at[at])
        for at, (source, target) in enumerate(pairs_in)
    ]
    for load in loads:
        load.start()
    places.greet()
    landing = {}
    for (at, axis, _), ref in zip(landing_shapes(items), landing_refs):
        landing.setdefault(at, {})[axis] = ref
    sums = Sums(
        items, places, [own_up, own_down, heads_own],
        [
            lambda cols: up_hbm.at[:, cols_own + cols.start : cols_own + cols.stop],
            lambda cols: down_hbm.at[:, cols_own + cols.start : cols_own + cols.stop],
            lambda cols: heads_other.at[:, cols],
        ],
        [total_up, total_down, total_heads], [out_up, out_down, out_heads], landing, send, recv,
    )

    each = tokens // MOVES

    def kept(at):
        return pl.ds(pl.multiple_of(head * tokens + at * each, each), each)

    my_rows = pl.ds(pl.multiple_of(head * tokens, tokens), tokens)

    def rows_copy():
        return remote(
            rows_hbm.at[:, their_cols], rows_all.at[my_rows], move_send.at[2 * MOVES],
            move_recv.at[2 * MOVES], places.partners["head"][0],
        )

    rows_keep = pltpu.make_async_copy(
        rows_hbm.at[:, mine_cols], rows_all.at[my_rows], local.at[len(pairs_in) + MOVES]
    )
    rows_keep.start()

    def cross_copy(at):
        here = slice(at * each, (at + 1) * each)
        return remote(
            dxc_ref.at[here], cross_land.at[here], move_send.at[at], move_recv.at[at],
            places.partners["x"][0],
        )

    def head_copy(at):
        here = slice(at * each, (at + 1) * each)
        return remote(
            dx_ref.at[here, their_cols], din_all.at[kept(at)], move_send.at[MOVES + at],
            move_recv.at[MOVES + at], places.partners["head"][0],
        )

    def keep_copy(at):
        here = slice(at * each, (at + 1) * each)
        return pltpu.make_async_copy(
            dx_ref.at[here, mine_cols], din_all.at[kept(at)], local.at[len(pairs_in) + at]
        )

    def move_copies(at, stage):
        return [cross_copy(at) if stage == 0 else head_copy(at)]

    def move(at, stage):
        here = slice(at * each, (at + 1) * each)
        if stage == 0:
            cross_copy(at).start()
        elif stage == 1:
            cross_copy(at).wait_recv()
            dx_ref[here, :] = dx_ref[here, :] + cross_land[here, :].astype(F32)
            head_copy(at).start()
            keep_copy(at).start()
        else:
            head_copy(at).wait_recv()
            keep_copy(at).wait()

    axes = small_axes(groups)

    def small_copies(stage):
        if stage == 0:
            device = places.partners["head"][0]
            spans = (
                (gvec_ref.at[:, their_cols], slice(0, half)),
                (bsum_ref.at[:, half:], slice(half, 2 * half)),
                (gbup_ref.at[:, part:], slice(2 * half, 2 * half + part)),
            )
            return [
                remote(
                    source, small_land.at[at, :, span], small_send.at[at], small_recv.at[at], device
                )
                for at, (source, span) in enumerate(spans)
            ]
        first = small_slot(axes[stage - 1])
        return [
            remote(
                small_stage.at[stage], small_land.at[first + d], small_send.at[first + d],
                small_recv.at[first + d], device,
            )
            for d, device in enumerate(places.partners[axes[stage - 1]])
        ]

    def small(stage):
        if stage == 1:
            for copy in small_copies(0):
                copy.wait_recv()
            small_stage[1, :, :half] = gvec_ref[:, mine_cols] + small_land[0, :, :half]
            small_stage[1, :, half : 2 * half] = (
                bsum_ref[:, :half] + small_land[1, :, half : 2 * half]
            )
            small_stage[1, :, 2 * half :] = gbup_ref[:, :part] + small_land[2, :, 2 * half :]
        elif stage > 1:
            value = small_stage[stage - 1]
            first = small_slot(axes[stage - 2])
            for d, copy in enumerate(small_copies(stage - 1)):
                copy.wait_recv()
                value = value + small_land[first + d]
            if stage <= len(axes):
                small_stage[stage] = value
            else:
                small_ref[...] = value
        if stage <= len(axes):
            for copy in small_copies(stage):
                copy.start()

    others = [item for item in items if isinstance(item, Other)]
    others[0].action, others[0].copies = small, small_copies
    for at, item in enumerate(others[1:]):
        item.action = functools.partial(move, at)
        item.copies = functools.partial(move_copies, at)

    pair_width = 2 * head_width
    pairs = width // pair_width
    batches = list(batches)
    for at in (4, 5):
        loads[at].wait()
    run_batch(sums, batches.pop(0))

    def steps(count, body):
        last = len(batches) == count

        @pl.loop(0, count)
        def _(step):
            body(step)
            for at in range(count - 1 if last else count):
                if batches[at]:
                    @pl.when(step == at)
                    def _():
                        run_batch(sums, batches[at])

        if last:
            run_batch(sums, batches[-1])
        del batches[:count]

    def attention(crossed, step):
        seq = step // (pairs // 2)
        pair = crossed * (pairs // 2) + step % (pairs // 2)
        here = pl.ds(pl.multiple_of(seq * block_len, block_len), block_len)
        cols = pl.ds(pl.multiple_of(pair * pair_width, pair_width), pair_width)

        @pl.when(step % (pairs // 2) == 0)
        def _():
            fill_bias(bias_ref, qseg_ref[seq], kseg_ref[crossed, here, :])

        queries, keys = q_ref[here, cols], k_ref[here, cols]
        values, grads = v_ref[here, cols], g_ref[here, cols]
        logs = lse_ref[seq, pair]
        key_cols = keys.astype(F32).T.astype(BF16)
        lane = lax.broadcasted_iota(jnp.int32, (1, pair_width), 1)
        query_parts = []
        for at, low in enumerate(range(0, pair_width, head_width)):
            chosen = jnp.logical_and(lane >= low, lane < low + head_width)
            scores = dot(keys, jnp.where(chosen, queries, 0), 1, 1) + bias_ref[...]
            mixing = jnp.exp(scores - logs[at : at + 1, :])
            grad_mixing = dot(values, jnp.where(chosen, grads, 0), 1, 1)
            inner = jnp.sum(mixing * grad_mixing, axis=0, keepdims=True)
            grad_scores = (mixing * (grad_mixing - inner)).astype(BF16)
            grad_value = dot(mixing.astype(BF16), grads)
            grad_key = dot(grad_scores, queries)
            query_parts.append(dot(key_cols[low : low + head_width], grad_scores))
            if at == 0:
                all_value, all_key = grad_value, grad_key
            else:
                all_value = jnp.where(chosen, grad_value, all_value)
                all_key = jnp.where(chosen, grad_key, all_key)
        q_ref[here, cols] = (jnp.concatenate(query_parts, axis=0).T.astype(BF16) * scale).astype(
            BF16
        )
        k_ref[here, cols] = all_key.astype(BF16)
        v_ref[here, cols] = all_value.astype(BF16)

    tile = 256

    def tile_of(step):
        return pl.ds(pl.multiple_of(step * tile, tile), tile)

    def cross_inputs(step):
        here = tile_of(step)
        dxc_ref[here, :] = (
            dot(k_ref[here, half:], wk_ref[:, half:], 1, 1)
            + dot(v_ref[here, half:], wv_ref[:, half:], 1, 1)
        ).astype(BF16)

    for at in range(4):
        loads[at].wait()
    steps(seqs * pairs // 2, functools.partial(attention, 1))
    for at in (6, 7):
        loads[at].wait()
    steps(tokens // tile, cross_inputs)
    steps(seqs * pairs // 2, functools.partial(attention, 0))
    for at in range(8, 13):
        loads[at].wait()

    def weights(step):
        mine = tile_of(step)
        left, left_cross = x_ref[:, mine].T, xc_ref[:, mine].T
        for at, ref in enumerate((q_ref, k_ref, v_ref)):
            first = dot(left, ref[:, :half])
            second = dot(left if at == 0 else left_cross, ref[:, half:])
            found = jnp.concatenate([first, second], axis=1).astype(BF16)
            natural = dot(found, sorter_ref[...], 1, 1).astype(BF16)
            heads_own[mine, at * half : (at + 1) * half] = natural[:, :half]
            heads_other[mine, at * half : (at + 1) * half] = natural[:, half:]
        gwo_ref[mine, :] = dot(ctx_ref[:, mine].T, gattnb_ref[...]).astype(BF16)

    steps(width // tile, weights)

    def last_weight(_):
        for ref, low in ((heads_own, 0), (heads_other, half)):
            natural = dot(sorter_ref[low : low + half], gwo_ref[...]).astype(BF16)
            ref[:half, 3 * half :] = natural[:, :half]
            ref[half:, 3 * half :] = natural[:, half:]
        totals = []
        for ref in (q_ref, v_ref):
            totals.append(jnp.sum(ref[...].astype(F32), axis=0, keepdims=True))
        found = jnp.concatenate(totals + [jnp.zeros((6, width), F32)], axis=0)
        high = found.astype(BF16)
        rest = found - high.astype(F32)
        middle_part = rest.astype(BF16)
        rest = rest - middle_part.astype(F32)
        bsum_ref[...] = (
            dot(high, sorter_ref[...], 1, 1)
            + dot(middle_part, sorter_ref[...], 1, 1)
            + dot(rest.astype(BF16), sorter_ref[...], 1, 1)
        )

    steps(1, last_weight)
    rows_copy().start()
    for at in range(13, 15):
        loads[at].wait()

    def inputs(step):
        here = tile_of(step)
        dq, dk, dv = q_ref[here, :], k_ref[here, :], v_ref[here, :]
        dx_ref[here, :] = (
            dx_ref[here, :]
            + dot(dq, wq_ref[...], 1, 1)
            + dot(dk[:, :half], wk_ref[:, :half], 1, 1)
            + dot(dv[:, :half], wv_ref[:, :half], 1, 1)
        )

    steps(tokens // tile, inputs)
    assert not batches
    rows_keep.wait()
    rows_copy().wait()
    sums.finish()


def attention_back(
    grads, tokens, weights, out_rows, logs, query_seg, keys_seg, grad_vecs, grad_bup, head_width,
    scale, groups,
):
    rows, cols = grads[0].shape[0], grads[0].shape[1] // 2
    count, width = tokens[0].shape
    seqs, block_len = query_seg.shape
    items = make_items([0, 1], rows, cols, FFN_ORDERS, groups)
    items += make_items([2], rows, cols, HEAD_ORDERS, groups, len(items))
    pair_steps = seqs * width // (2 * head_width)
    tiles, weight_steps = count // 256, width // 256
    half_steps = pair_steps // 2
    times = (
        [2.3] * half_steps + [0.9] * tiles + [2.3] * half_steps + [4.0] * weight_steps + [1.5]
        + [1.1] * tiles
    )
    heads_at = pair_steps + tiles + weight_steps + 1
    ready = [0] * len(FFN_ORDERS) + [heads_at] * len(HEAD_ORDERS)
    small = (8, width + cols)
    items.append(Other([("head", 1e4)] + [(axis, 7e4) for axis in small_axes(groups)]))
    ready.append(heads_at)
    for at in range(MOVES):
        items.append(Other([("x", count // MOVES * width * 2), ("head", count // MOVES * width * 2)]))
        items[-1].later = heads_at + (at + 1) * tiles // MOVES
        ready.append(half_steps + (at + 1) * tiles // MOVES)
    batches = plan(items, times, ready)
    landing = landing_shapes(items)
    vmem = pl.BlockSpec(memory_space=pltpu.VMEM)
    anywhere = pl.BlockSpec(memory_space=pl.ANY)
    slots = len(FFN_ORDERS) + len(HEAD_ORDERS)
    small_slots = 7 + groups - 1
    big = pltpu.VMEM((rows, cols), BF16)
    rows_low = pltpu.VMEM((count, width), BF16)
    square = pltpu.VMEM((width, width), BF16)
    large = [*grads, *tokens, *weights, out_rows]
    return pl.pallas_call(
        functools.partial(back_kernel, items, batches, groups, head_width, scale),
        in_specs=[anywhere] * len(large) + [vmem] * 5,
        out_specs=[vmem] * 4 + [anywhere] * 2,
        out_shape=[jax.ShapeDtypeStruct((rows, cols), BF16)] * 3
        + [jax.ShapeDtypeStruct(small, F32)]
        + [jax.ShapeDtypeStruct((2 * count, width // 2), F32)] * 2,
        scratch_shapes=[big] * 7
        + [rows_low] * 8
        + [pltpu.VMEM((count, width), F32)]
        + [square] * 4
        + [pltpu.VMEM((block_len, block_len), F32), square, pltpu.VMEM((8, width), F32)]
        + [rows_low] * 2
        + [pltpu.VMEM((small_slots, *small), F32), pltpu.VMEM((6, *small), F32)]
        + [pltpu.SemaphoreType.DMA((slots, slot_count(groups)))] * 2
        + [pltpu.SemaphoreType.DMA((small_slots,))] * 2
        + [pltpu.SemaphoreType.DMA((2 * MOVES + 1,))] * 2
        + [pltpu.SemaphoreType.DMA((len(large) + MOVES + 1,))]
        + [pltpu.VMEM(shape, BF16) for _, _, shape in landing],
        compiler_params=pltpu.CompilerParams(
            collective_id=1, has_side_effects=True, vmem_limit_bytes=63 * MIB
        ),
        name="attention_back",
    )(
        *large, logs, query_seg[:, None, :], keys_seg[:, :, None], grad_vecs, grad_bup
    )


def finish_kernel(up_ref, down_ref, heads_ref, gup_ref, gdown_ref, gq_ref, gk_ref, gv_ref, go_ref):
    width = gq_ref.shape[1]
    gup_ref[...] = up_ref[...].astype(F32)
    gdown_ref[...] = down_ref[...].astype(F32).T
    for at, ref in enumerate((gq_ref, gk_ref, gv_ref, go_ref)):
        ref[...] = heads_ref[:, at * width : (at + 1) * width].astype(F32)


def finish(up, down, heads):
    rows, cols = up.shape
    steps = 6
    tile = rows // steps
    half, quarter = cols // 2, cols // 4
    spec = pl.BlockSpec((tile, cols), lambda i: (i, 0))
    third = pl.BlockSpec((tile, quarter), lambda i: (i, 0))
    return pl.pallas_call(
        finish_kernel,
        grid=(steps,),
        in_specs=[spec, pl.BlockSpec((rows, cols // steps), lambda i: (0, i)), spec],
        out_specs=[
            spec,
            pl.BlockSpec((cols // steps, rows), lambda i: (i, 0)),
            third,
            third,
            third,
            pl.BlockSpec((tile, quarter), lambda i: (i % (steps // 2), i // (steps // 2))),
        ],
        out_shape=[
            jax.ShapeDtypeStruct((rows, cols), F32),
            jax.ShapeDtypeStruct((cols, rows), F32),
            jax.ShapeDtypeStruct((rows, quarter), F32),
            jax.ShapeDtypeStruct((rows, quarter), F32),
            jax.ShapeDtypeStruct((rows, quarter), F32),
            jax.ShapeDtypeStruct((rows // 2, half), F32),
        ],
        compiler_params=pltpu.CompilerParams(vmem_limit_bytes=48 * MIB),
        name="finish",
    )(up, down, heads)


def on_device(
    layer_in, segments, block_perm, w_query, b_query, w_key, w_value, b_value, w_attn_out,
    b_attn_out, norm1_gain, norm1_bias, w_up, b_up, w_down, b_down, norm2_gain, norm2_bias,
    grad_out,
):
    seq_count, block_len, half = layer_in.shape
    local_heads, block_count = block_perm.shape
    head_width = w_query.shape[1] // local_heads
    seqs = seq_count // 2
    scale = head_width ** (-0.5)
    head = lax.axis_index("head")
    my_block = lax.axis_index("blk")

    own_place = jnp.where(jnp.arange(block_count)[None, :] == my_block, block_perm, 0)
    crossed = jnp.repeat((jnp.sum(own_place, axis=1) != my_block).astype(F32), head_width)
    row = lax.broadcasted_iota(jnp.int32, (16, half), 0)
    vecs = jnp.pad(b_up.reshape(-1, half), ((8, 16 - 8 - b_up.shape[0] // half), (0, 0)))
    listed = [
        b_attn_out, norm1_gain, norm1_bias, b_down, norm2_gain, norm2_bias, b_query, b_value,
    ]
    for at, vec in [*enumerate(listed), (12, crossed)]:
        vecs = jnp.where(row == at, vec[None, :], vecs)

    my_segments = lax.dynamic_slice_in_dim(segments, head * seqs, seqs, 0)
    own_seg = lax.dynamic_slice_in_dim(my_segments, my_block * block_len, block_len, 1)
    cross_seg = lax.dynamic_slice_in_dim(my_segments, (1 - my_block) * block_len, block_len, 1)
    keys_seg = jnp.stack([own_seg.reshape(-1), cross_seg.reshape(-1)])
    (
        x, x_cross, queries, keys, values, ctx, wq, wk, wv, wo, sorter, up_other, down_other,
        grad_rows, vectors, b_up_all, logs,
    ) = front(
        layer_in.reshape(-1, half),
        grad_out.reshape(-1, half),
        (w_query, w_key, w_value, w_attn_out, w_up, w_down),
        vecs,
        own_seg,
        keys_seg,
        head_width,
        scale,
    )
    (
        out_rows, grad_attn, grad_attn_low, grad_ctx, grad_vecs, grad_bup, grad_up_all,
        grad_down_all,
    ) = middle(
        ctx, x, grad_rows, vectors, b_up_all, wo, (w_up, up_other), (w_down, down_other)
    )
    total_up, total_down, total_heads, small, grad_in, layer_out = attention_back(
        (grad_up_all, grad_down_all),
        (queries, keys, values, grad_ctx, x, x_cross, ctx, grad_attn_low, grad_attn),
        (wq, wk, wv, sorter),
        out_rows,
        logs,
        own_seg,
        keys_seg,
        grad_vecs,
        grad_bup,
        head_width,
        scale,
        lax.axis_size("dp") // 8,
    )
    grad_up, grad_down, grad_q, grad_k, grad_v, grad_o = finish(total_up, total_down, total_heads)
    return (
        layer_out.reshape(layer_in.shape),
        grad_in.reshape(layer_in.shape),
        grad_q,
        small[0, half : 2 * half],
        grad_k,
        grad_v,
        small[1, half : 2 * half],
        grad_o,
        small[0, :half],
        small[1, :half],
        small[2, :half],
        grad_up,
        small[0, 2 * half :],
        grad_down,
        small[3, :half],
        small[4, :half],
        small[5, :half],
    )


def solution(mesh):
    rows, cols, vec = P("head", None), P(None, "head"), P("head")
    tokens = P("dp", "blk", "head")
    return jax.shard_map(
        on_device,
        mesh=mesh,
        in_specs=(
            tokens, P("dp", None), rows, cols, vec, cols, cols, vec, rows, vec, vec, vec, cols,
            vec, rows, vec, vec, vec, tokens,
        ),
        out_specs=(
            tokens, tokens, cols, vec, cols, cols, vec, rows, vec, vec, vec, cols, vec, rows, vec,
            vec, vec,
        ),
        check_vma=False,
    )
```

```python
import functools

import jax
import jax.numpy as jnp
from jax import lax
from jax.experimental import pallas as pl
from jax.experimental.pallas import tpu as pltpu
from jax.sharding import PartitionSpec as P

EPSILON = 1e-05
NEGATIVE = -1e30
ROOT_HALF = 0.7071067811865476
DENSITY_SCALE = 0.3989422804014327
F32 = jnp.float32
BF16 = jnp.bfloat16
MIB = 1 << 20


def dot(left, right, left_dim=1, right_dim=0):
    return lax.dot_general(
        left, right, (((left_dim,), (right_dim,)), ((), ())), preferred_element_type=F32
    )


def remote(source, target, send, recv, device):
    return pltpu.make_async_remote_copy(
        src_ref=source,
        dst_ref=target,
        send_sem=send,
        recv_sem=recv,
        device_id=device,
        device_id_type=pl.DeviceIdType.MESH,
    )


def fill_bias(bias_ref, seg_ref, row, query_block, key_block):
    length = bias_ref.shape[0]

    def block(at):
        cols = pl.ds(pl.multiple_of(at * length, length), length)
        return seg_ref[pl.ds(row, 1), cols].astype(F32)

    lanes = 128
    keys = jnp.broadcast_to(block(key_block), (lanes, length)).T
    same = jnp.concatenate([keys] * (length // lanes), axis=1) == block(query_block)
    covered = jnp.max(jnp.where(same, 1.0, 0.0), axis=0, keepdims=True)
    bias_ref[...] = jnp.where(same, 0.0, covered * NEGATIVE)


def attend_pair(queries, keys, values, bias, head_width):
    pair_width = queries.shape[1]
    value_cols = values.astype(F32).T.astype(BF16)
    lane = lax.broadcasted_iota(jnp.int32, (1, pair_width), 1)
    parts, logs = [], []
    for low in range(0, pair_width, head_width):
        chosen = jnp.logical_and(lane >= low, lane < low + head_width)
        scores = dot(keys, jnp.where(chosen, queries, 0), 1, 1) + bias[...]
        top = jnp.max(scores, axis=0, keepdims=True)
        shifted = jnp.exp(scores - top)
        total = jnp.sum(shifted, axis=0, keepdims=True)
        context = dot(value_cols[low : low + head_width], shifted.astype(BF16))
        parts.append(context * (1.0 / total))
        logs.append(top + jnp.log(total))
    return jnp.concatenate(parts, axis=0).T.astype(BF16), jnp.concatenate(logs, axis=0)


def split_dot(left, right, left_dim=1, right_dim=0):
    high = left.astype(BF16)
    rest = left - high.astype(F32)
    mid = rest.astype(BF16)
    low = (rest - mid.astype(F32)).astype(BF16)
    return sum(dot(x, right, left_dim, right_dim) for x in (high, mid, low))


def front_kernel(
    head_width, scale, seqs,
    layer_hbm, gout_hbm, wq_hbm, wk_hbm, wv_hbm, wo_hbm, wup_hbm, wdn_hbm, vec_own, perm_ref,
    seg_ref,
    x_hbm, xc_hbm, q_hbm, k_hbm, v_hbm, ctx_hbm, wqs_hbm, wks_hbm, wvs_hbm, wos_hbm, sorter_hbm,
    wup_other, wdn_other, grad_hbm, vec_all, bup_all, lse_ref,
    x_ref, xc_ref, q_ref, k_ref, v_ref, ctx_ref, wn_q, wn_k, wn_v, wn_o, ws_q, ws_k, ws_v, ws_o,
    sorter_ref, sorter_t, vec_land, cross_own, cross_land, bias_ref, grad_ref, local, send, recv,
):
    head, blk = lax.axis_index("head"), lax.axis_index("blk")
    to_head, to_cross = {"head": 1 - head}, {"blk": 1 - blk}
    rows, width = x_ref.shape
    half = width // 2
    block_len = rows // seqs
    my_rows = pl.ds(pl.multiple_of(head * rows, rows), rows)
    their_rows = pl.ds(pl.multiple_of((1 - head) * rows, rows), rows)
    mine = pl.ds(pl.multiple_of(head * half, half), half)
    theirs = pl.ds(pl.multiple_of((1 - head) * half, half), half)

    started = []

    def bring(at, source, target):
        copy = pltpu.make_async_copy(source, target, local.at[at])
        copy.start()
        return copy

    def give(at, source, target, device):
        copy = remote(source, target, send.at[at], recv.at[at], device)
        copy.start()
        started.append(copy)
        return copy

    barrier = pltpu.get_barrier_semaphore()
    for device in (to_head, to_cross):
        pl.semaphore_signal(barrier, inc=1, device_id=device, device_id_type=pl.DeviceIdType.MESH)
    own_x = bring(0, layer_hbm.at[my_rows], x_ref.at[:, mine])
    own_w = [
        bring(1, wq_hbm, wn_q.at[:, :half]),
        bring(2, wk_hbm, wn_k.at[:, :half]),
        bring(3, wv_hbm, wn_v.at[:, :half]),
        bring(4, wo_hbm, wn_o.at[:half]),
    ]
    own_grad = bring(5, gout_hbm.at[my_rows], grad_ref)
    pl.semaphore_wait(barrier, 2)

    def seq_rows(seq):
        return slice(seq * block_len, (seq + 1) * block_len)

    def block_of(seq):
        return pl.ds(pl.multiple_of(head * rows + seq * block_len, block_len), block_len)

    perm = perm_ref[...]
    block = lax.broadcasted_iota(jnp.int32, perm.shape, 0)
    reads = jnp.sum(jnp.where(block == blk, perm, 0).astype(F32), axis=0, keepdims=True)
    reads = jnp.where(reads == blk.astype(F32), 0.0, 1.0)
    heads_shape = (perm.shape[1], half)
    feature_head = lax.broadcasted_iota(jnp.int32, heads_shape, 1) // head_width
    at_head = feature_head == lax.broadcasted_iota(jnp.int32, heads_shape, 0)
    cross_row = dot(
        jnp.broadcast_to(reads, (8, reads.shape[1])).astype(BF16),
        jnp.where(at_head, 1.0, 0.0).astype(BF16),
    )[0:1]
    cross_own[...] = jnp.broadcast_to(cross_row, cross_own.shape)
    flags = give(7 + 2 * seqs - 1 + 3, cross_own, cross_land, to_head)
    vecs = give(0, vec_own, vec_land, to_head)
    features = give(1, layer_hbm.at[their_rows], x_ref.at[:, mine], to_head)
    cross = [[give(2, layer_hbm.at[block_of(0)], xc_ref.at[seq_rows(0), mine], to_cross)]]
    other_w = [
        give(3, wq_hbm, wn_q.at[:, half:], to_head),
        give(4, wk_hbm, wn_k.at[:, half:], to_head),
        give(5, wv_hbm, wn_v.at[:, half:], to_head),
        give(6, wo_hbm, wn_o.at[half:], to_head),
    ]
    features.wait_recv()
    base = 7
    for seq in range(seqs):
        if seq > 0:
            cross.append(
                [give(base, layer_hbm.at[block_of(seq)], xc_ref.at[seq_rows(seq), mine], to_cross)]
            )
            base += 1
        here = seq_rows(seq)
        cross[seq].append(give(base, x_ref.at[here, theirs], xc_ref.at[here, theirs], to_cross))
        base += 1
    later = [
        give(base, wup_hbm, wup_other, to_head),
        give(base + 1, wdn_hbm, wdn_other, to_head),
        give(base + 2, gout_hbm.at[their_rows], grad_hbm.at[:, mine], to_head),
    ]

    vecs.wait_recv()
    flags.wait_recv()
    crossed = jnp.concatenate([cross_own[0:1, :], cross_land[0:1, :]], axis=1)
    row = lax.broadcasted_iota(jnp.int32, (width, width), 0)
    col = lax.broadcasted_iota(jnp.int32, (width, width), 1)
    earlier = jnp.where(row // head_width < col // head_width, 1.0, 0.0).astype(BF16)
    before = dot(jnp.broadcast_to(crossed, (8, width)).astype(BF16), earlier)[0:1]
    lane = lax.broadcasted_iota(jnp.int32, (1, width), 1)
    place = jnp.where(
        crossed > 0.5, half + before + (lane % head_width).astype(F32), lane.astype(F32) - before
    )
    found = jnp.where(row.astype(F32) == place, 1.0, 0.0)
    sorter_t[...] = found.astype(BF16)
    sorter_ref[...] = found.T.astype(BF16)
    vec_all[:, mine] = vec_own[0:8, :]
    vec_all[:, theirs] = vec_land[0:8, :]
    for at in range(bup_all.shape[1] // half):
        source = vec_own if at < 4 else vec_land
        bup_all[:, at * half : (at + 1) * half] = source[8 + at % 4 : 9 + at % 4, :]
    b_local = jnp.concatenate([vec_own[0:8, :], vec_land[0:8, :]], axis=1)
    b_sorted = split_dot(b_local, sorter_ref[...])
    bq, bv = b_sorted[6:7], b_sorted[7:8]

    own_grad.wait()
    out = [bring(17, grad_ref, grad_hbm.at[:, mine])]
    pairs_w = ((wn_q, ws_q, wqs_hbm), (wn_k, ws_k, wks_hbm), (wn_v, ws_v, wvs_hbm))
    for at, (natural, ordered, target) in enumerate(pairs_w):
        own_w[at].wait()
        other_w[at].wait_recv()
        ordered[...] = dot(natural[...], sorter_ref[...]).astype(BF16)
        out.append(bring(6 + at, ordered, target))
    out.append(bring(9, sorter_ref, sorter_hbm))
    own_x.wait()
    out.append(bring(10, x_ref, x_hbm))
    x = x_ref[...]
    q_ref[...] = ((dot(x, ws_q[...]) + bq) * scale).astype(BF16)
    out.append(bring(11, q_ref, q_hbm))
    k_ref[:, :half] = dot(x, ws_k[:, :half]).astype(BF16)
    v_ref[:, :half] = (dot(x, ws_v[:, :half]) + bv[:, :half]).astype(BF16)

    pair_width = 2 * head_width
    pairs = half // pair_width

    def attention(seq, first_pair, kind):
        here = pl.ds(pl.multiple_of(seq * block_len, block_len), block_len)
        fill_bias(bias_ref, seg_ref, head * seqs + seq, blk, 1 - blk if kind else blk)

        @pl.loop(0, pairs)
        def _(at):
            pair = first_pair + at
            cols = pl.ds(pl.multiple_of(pair * pair_width, pair_width), pair_width)
            context, logs = attend_pair(
                q_ref[here, cols], k_ref[here, cols], v_ref[here, cols], bias_ref, head_width
            )
            ctx_ref[here, cols] = context
            lse_ref[seq, pair] = logs

    @pl.loop(0, seqs)
    def _(seq):
        attention(seq, 0, 0)

    own_w[3].wait()
    other_w[3].wait_recv()
    ws_o[...] = dot(sorter_t[...], wn_o[...]).astype(BF16)
    out.append(bring(12, ws_o, wos_hbm))
    for seq in range(seqs):
        here = seq_rows(seq)
        for copy in cross[seq]:
            copy.wait_recv()
        x_cross = xc_ref[here, :]
        k_ref[here, half:] = dot(x_cross, ws_k[:, half:]).astype(BF16)
        v_ref[here, half:] = (dot(x_cross, ws_v[:, half:]) + bv[:, half:]).astype(BF16)
        attention(seq, pairs, 1)
    out.append(bring(13, xc_ref, xc_hbm))
    out.append(bring(14, k_ref, k_hbm))
    out.append(bring(15, v_ref, v_hbm))
    out.append(bring(16, ctx_ref, ctx_hbm))
    for copy in later:
        copy.wait_recv()
    for copy in out:
        copy.wait()
    for copy in started:
        copy.wait_send()


def front(layer_in, grad_out, weights, vecs, perm, segments, block_len, head_width, scale):
    width = weights[0].shape[0]
    half = width // 2
    seqs = segments.shape[0] // 2
    rows = seqs * block_len
    part = weights[4].shape[1]
    anywhere = pl.BlockSpec(memory_space=pl.ANY)
    vmem = pl.BlockSpec(memory_space=pltpu.VMEM)
    tokens = jax.ShapeDtypeStruct((rows, width), BF16)
    square = jax.ShapeDtypeStruct((width, width), BF16)
    low_rows, low_square = pltpu.VMEM((rows, width), BF16), pltpu.VMEM((width, width), BF16)
    copies = 7 + 2 * seqs - 1 + 3 + 1
    return pl.pallas_call(
        functools.partial(front_kernel, head_width, scale, seqs),
        in_specs=[anywhere] * 8 + [vmem] * 3,
        out_specs=[anywhere] * 14 + [vmem] * 3,
        out_shape=[tokens] * 6
        + [square] * 5
        + [
            jax.ShapeDtypeStruct(weights[4].shape, BF16),
            jax.ShapeDtypeStruct(weights[5].shape, BF16),
            jax.ShapeDtypeStruct((rows, width), F32),
            jax.ShapeDtypeStruct((8, width), F32),
            jax.ShapeDtypeStruct((1, 2 * part), F32),
            jax.ShapeDtypeStruct((seqs, width // (2 * head_width), 2, block_len), F32),
        ],
        scratch_shapes=[low_rows] * 6
        + [low_square] * 10
        + [
            pltpu.VMEM((16, half), F32),
            pltpu.VMEM((8, half), F32),
            pltpu.VMEM((8, half), F32),
            pltpu.VMEM((block_len, block_len), F32),
            pltpu.VMEM((rows, half), F32),
            pltpu.SemaphoreType.DMA((18,)),
            pltpu.SemaphoreType.DMA((copies,)),
            pltpu.SemaphoreType.DMA((copies,)),
        ],
        compiler_params=pltpu.CompilerParams(
            collective_id=3, has_side_effects=True, vmem_limit_bytes=60 * MIB
        ),
        name="front",
    )(layer_in, grad_out, *weights, vecs, perm, segments)


def unit_rows(rows, width):
    mean = jnp.sum(rows, axis=1, keepdims=True) * (1.0 / width)
    centered = rows - mean
    variance = jnp.sum(centered * centered, axis=1, keepdims=True) * (1.0 / width)
    inverse = lax.rsqrt(variance + EPSILON)
    return centered * inverse, inverse


def unit_back(grad, unit, inverse, gain, width):
    scaled = grad * gain
    plain = jnp.sum(scaled, axis=1, keepdims=True) * (1.0 / width)
    along = jnp.sum(scaled * unit, axis=1, keepdims=True) * (1.0 / width)
    return (scaled - plain - unit * along) * inverse


def middle_kernel(
    chunk, tiles, ctx_ref, x_ref, gout_ref, vec_ref, bup_ref, wo_hbm,
    wup0_hbm, wup1_hbm, wdn0_hbm, wdn1_hbm,
    out_ref, gattn_ref, gattnb_ref, gctx_ref, gvec_ref, gbup_ref, gwup_ref, gwdn_ref,
    slope_ref, act_ref, gup_ref, normed_t, gffn_t, wo_ref, wup0_ref, wup1_ref, wdn0_ref, wdn1_ref,
    staged, landed, local, send, recv,
):
    tile, width = x_ref.shape
    part = wup0_ref.shape[1]
    at_step = pl.program_id(0)
    to_head = {"head": 1 - lax.axis_index("head")}
    loads = [
        pltpu.make_async_copy(source, target, local.at[at])
        for at, (source, target) in enumerate(
            (
                (wo_hbm, wo_ref), (wup0_hbm, wup0_ref), (wdn0_hbm, wdn0_ref),
                (wup1_hbm, wup1_ref), (wdn1_hbm, wdn1_ref),
            )
        )
    ]

    @pl.when(at_step == 0)
    def _():
        for load in loads:
            load.start()
        barrier = pltpu.get_barrier_semaphore()
        pl.semaphore_signal(
            barrier, inc=1, device_id=to_head, device_id_type=pl.DeviceIdType.MESH
        )
        for load in loads:
            load.wait()
        pl.semaphore_wait(barrier, 1)
        gvec_ref[...] = jnp.zeros_like(gvec_ref)
        gbup_ref[...] = jnp.zeros_like(gbup_ref)

    def vec(i):
        return vec_ref[i : i + 1, :]

    def add_vec(i, rows):
        gvec_ref[i : i + 1, :] += jnp.sum(rows, axis=0, keepdims=True)

    @pl.when(at_step < tiles)
    def _():
        here = pl.ds(pl.multiple_of(at_step * tile, tile), tile)
        attended = dot(ctx_ref[...], wo_ref[...])
        unit1, inverse1 = unit_rows(x_ref[...].astype(F32) + attended + vec(0), width)
        normed = unit1 * vec(1) + vec(2)
        normed_low = normed.astype(BF16)
        normed_t[:, here] = normed_low.T
        pieces = ((wup0_ref, wdn0_ref), (wup1_ref, wdn1_ref))
        down = jnp.zeros_like(normed)
        for at, (wup, wdn) in enumerate(pieces):
            for low in range(0, part, chunk):
                cols = slice(at * part + low, at * part + low + chunk)
                up = dot(normed_low, wup[:, low : low + chunk]) + bup_ref[:, cols]
                cumulative = 0.5 + 0.5 * lax.erf(up * ROOT_HALF)
                slope_ref[:, cols] = cumulative + up * (jnp.exp(-0.5 * up * up) * DENSITY_SCALE)
                activated = (up * cumulative).astype(BF16)
                act_ref[here, cols] = activated
                down += dot(activated, wdn[low : low + chunk, :])
        unit2, inverse2 = unit_rows(normed + down + vec(3), width)
        out_ref[...] = unit2 * vec(4) + vec(5)
        grad_out = gout_ref[...]
        add_vec(4, grad_out * unit2)
        add_vec(5, grad_out)
        grad_ffn = unit_back(grad_out, unit2, inverse2, vec(4), width)
        add_vec(3, grad_ffn)
        grad_ffn_low = grad_ffn.astype(BF16)
        gffn_t[:, here] = grad_ffn_low.T
        back = jnp.zeros_like(normed)
        for at, (wup, wdn) in enumerate(pieces):
            for low in range(0, part, chunk):
                cols = slice(at * part + low, at * part + low + chunk)
                grad_act = dot(grad_ffn_low, wdn[low : low + chunk, :], 1, 1)
                grad_up = (grad_act * slope_ref[:, cols]).astype(BF16)
                gup_ref[here, cols] = grad_up
                gbup_ref[0:1, cols] += jnp.sum(grad_up.astype(F32), axis=0, keepdims=True)
                back += dot(grad_up, wup[:, low : low + chunk], 1, 1)
        grad_mid = grad_ffn + back
        add_vec(1, grad_mid * unit1)
        add_vec(2, grad_mid)
        grad_attn = unit_back(grad_mid, unit1, inverse1, vec(1), width)
        add_vec(0, grad_attn)
        gattn_ref[...] = grad_attn
        grad_attn_low = grad_attn.astype(BF16)
        gattnb_ref[...] = grad_attn_low
        gctx_ref[...] = dot(grad_attn_low, wo_ref[...], 1, 1).astype(BF16)

    cols_step = gwup_ref.shape[1]
    count = part // cols_step

    def gradients(low):
        cols = pl.ds(pl.multiple_of(low, cols_step), cols_step)
        return dot(normed_t[...], gup_ref[:, cols]), dot(gffn_t[...], act_ref[:, cols])

    def exchange(slot):
        return remote(staged.at[slot], landed.at[slot], send.at[slot], recv.at[slot], to_head)

    @pl.when(jnp.logical_and(at_step >= tiles, at_step < tiles + count))
    def _():
        at = at_step - tiles
        for kind, value in enumerate(gradients(part + at * cols_step)):
            staged[kind * count + at] = value.astype(BF16)
            exchange(kind * count + at).start()

    @pl.when(at_step >= tiles + count)
    def _():
        at = at_step - tiles - count
        found = gradients(at * cols_step)
        for kind, (value, target) in enumerate(zip(found, (gwup_ref, gwdn_ref))):
            exchange(kind * count + at).wait()
            target[...] = (value + landed[kind * count + at].astype(F32)).astype(BF16)


def middle(ctx, x, grad_out, vectors, b_up, w_out, w_up, w_down):
    rows, width = x.shape
    part = w_up[0].shape[1]
    tile = 256
    tiles = rows // tile
    chunk = part // 2
    cols_step = part // 3

    def tiled(cols):
        return pl.BlockSpec((tile, cols), lambda i: (jnp.minimum(i, tiles - 1), 0))

    def whole(array):
        return pl.BlockSpec(array.shape, lambda i: (0, 0), pipeline_mode=pl.Buffered(1))

    def shape(cols, kind):
        return jax.ShapeDtypeStruct((rows, cols), kind)

    outs = [(width, F32), (width, F32), (width, BF16), (width, BF16)]
    sums = [jax.ShapeDtypeStruct((8, width), F32), jax.ShapeDtypeStruct((8, b_up.shape[1]), F32)]
    grads = [jax.ShapeDtypeStruct((width, part), BF16)] * 2
    count = part // cols_step
    grad_spec = pl.BlockSpec((width, cols_step), lambda i: (0, jnp.maximum(i - tiles - count, 0)))
    slots = pltpu.VMEM((2 * count, width, cols_step), BF16)
    weights = [vectors, b_up, w_out, *w_up, *w_down]
    return pl.pallas_call(
        functools.partial(middle_kernel, chunk, tiles),
        grid=(tiles + 2 * part // cols_step,),
        in_specs=[tiled(width), tiled(width), tiled(width)]
        + [whole(vectors), whole(b_up)]
        + [pl.BlockSpec(memory_space=pl.ANY)] * 5,
        out_specs=[tiled(c) for c, _ in outs]
        + [pl.BlockSpec(s.shape, lambda i: (0, 0)) for s in sums]
        + [grad_spec] * 2,
        out_shape=[shape(c, k) for c, k in outs] + sums + grads,
        scratch_shapes=[
            pltpu.VMEM((tile, 2 * part), F32),
            pltpu.VMEM((rows, 2 * part), BF16),
            pltpu.VMEM((rows, 2 * part), BF16),
            pltpu.VMEM((width, rows), BF16),
            pltpu.VMEM((width, rows), BF16),
        ]
        + [pltpu.VMEM(w.shape, BF16) for w in weights[2:]]
        + [slots, slots]
        + [pltpu.SemaphoreType.DMA((5,))]
        + [pltpu.SemaphoreType.DMA((2 * count,))] * 2,
        compiler_params=pltpu.CompilerParams(
            collective_id=4, has_side_effects=True, vmem_limit_bytes=62 * MIB
        ),
        name="middle",
    )(ctx, x, grad_out, *weights)


LINKS = {
    "head": (("core", 1),),
    "x": (("x", 1),),
    "y": (("y", 1),),
    "u": (("outer", 1),),
    "w": (("outer", 1), ("inner", 2)),
    "group": (("group", 1),),
}
RATES = {"core": 500e3, "x": 46e3, "y": 46e3, "outer": 46e3, "inner": 46e3, "group": 46e3}
DELAY = 4.5
OP_TIME = 0.3
URGENCY = 1.0
AHEAD = 5.0
ORDERS = {
    "A": "xyuw", "B": "yxuw", "C": "uwxy", "D": "uxyw", "E": "xuyw", "F": "yuxw", "G": "uyxw",
    "H": "uwyx",
}


class Item:
    action = None
    later = 0

    def __init__(self, at, array, first, cols, rows, order, groups, from_head):
        self.at, self.array, self.first, self.cols, self.rows = at, array, first, cols, rows
        self.groups = groups
        self.sums = []
        size = rows
        for axis in [*ORDERS[order]] + (["group"] if groups > 1 else []):
            before = size
            size = size if axis == "group" else size // 2
            self.sums.append((axis, before, size))
        self.size = size
        self.stages = (
            [("head", "head", rows, rows)] * from_head
            + [("sum", *s) for s in self.sums]
            + [("result", *s) for s in reversed(self.sums) if s[0] != "group"]
        )

    def load(self, stage):
        kind, axis, before, size = self.stages[stage]
        moved = size * (self.groups - 1 if axis == "group" else 1)
        return axis, moved * self.cols * 2


def plan(items, steps, ready):
    free = {link: 0.0 for link in RATES}
    due = {i: (0.0, 0) for i in range(len(items))}
    batches = []
    now = 0.0

    def links(index, stage):
        item = items[index]
        return LINKS[item.load(stage)[0]] if stage < len(item.stages) else ()

    behind = []
    for index, item in enumerate(items):
        times = [
            DELAY + max(t * item.load(k)[1] / RATES[link] for link, t in links(index, k))
            for k in range(len(item.stages))
        ]
        behind.append([sum(times[k:]) for k in range(len(times) + 1)])

    def rank(i):
        return due[i][0] - URGENCY * behind[i][due[i][1]]

    def opens(i):
        return max([due[i][0]] + [free[link] - AHEAD for link, _ in links(i, due[i][1])])

    def run(index, batch):
        nonlocal now
        stage = due[index][1]
        batch.append((index, stage))
        now += OP_TIME
        if stage == len(items[index].stages):
            del due[index]
            return
        size = items[index].load(stage)[1]
        end = now
        for link, times in links(index, stage):
            free[link] = max(free[link], now) + times * size / RATES[link]
            end = max(end, free[link])
        due[index] = (end + DELAY, stage + 1)

    for at, time in enumerate([0.0] + steps):
        now += time
        batch = []
        while True:
            able = [
                i
                for i in due
                if opens(i) <= now and at >= (items[i].later if due[i][1] else ready[i])
            ]
            if not able:
                break
            run(min(able, key=rank), batch)
        batches.append(batch)
    while due:
        here = [i for i in due if opens(i) <= now]
        first = min(here, key=rank) if here else min(due, key=lambda i: (opens(i), i))
        now = max(now, opens(first))
        run(first, batches[-1])
    return batches


class Places:
    def __init__(self, groups):
        head, blk, dp = lax.axis_index("head"), lax.axis_index("blk"), lax.axis_index("dp")
        group = dp // 8
        self.head = head
        self.bit = {"x": blk, "y": dp % 2, "u": (dp // 2) % 2, "w": (dp // 4) % 2}
        self.partners = {
            "head": [{"head": 1 - head}],
            "x": [{"blk": 1 - blk}],
            "y": [{"dp": dp + 1 - 2 * self.bit["y"]}],
            "u": [{"dp": dp + 2 - 4 * self.bit["u"]}],
            "w": [{"dp": dp + 4 - 8 * self.bit["w"]}],
            "group": [{"dp": (group + d) % groups * 8 + dp % 8} for d in range(1, groups)],
        }

    def greet(self):
        barrier = pltpu.get_barrier_semaphore()
        everyone = [device for devices in self.partners.values() for device in devices]
        for device in everyone:
            pl.semaphore_signal(
                barrier, inc=1, device_id=device, device_id_type=pl.DeviceIdType.MESH
            )
        pl.semaphore_wait(barrier, len(everyone))


SUM_SLOT = {"x": 1, "y": 2, "u": 3, "w": 4, "group": 9}
RESULT_SLOT = {"x": 5, "y": 6, "u": 7, "w": 8}


def slot_count(groups):
    return 9 + groups - 1


class Sums:
    def __init__(
        self, items, places, own, other, total, result, final, landing, send, recv, store
    ):
        self.items, self.places, self.final, self.store = items, places, final, store
        self.own, self.other, self.total, self.result = own, other, total, result
        self.landing, self.send, self.recv = landing, send, recv
        self.sent = []

    def start_of(self, item, stop):
        start = 0
        for name, before, after in item.sums:
            if name == stop:
                return start
            start = self.within(start, name, after)
        return start

    def within(self, start, axis, after):
        if axis == "group":
            return start
        return start + self.places.bit[axis] * after

    def part(self, ref, start, size, item):
        return ref.at[
            pl.ds(pl.multiple_of(start, 16), size), item.first : item.first + item.cols
        ]

    def copies_of(self, item, stage):
        kind, axis, before, after = item.stages[stage]
        devices = self.places.partners[axis]
        out = []

        def add(source, target, slot, device):
            out.append(
                remote(
                    source, target, self.send.at[item.at, slot], self.recv.at[item.at, slot], device
                )
            )

        if kind == "head":
            cols = slice(item.first, item.first + item.cols)
            add(self.other[item.array].at[:, cols], self.total[item.array].at[:, cols], 0, devices[0])
            return out
        if kind == "sum":
            start = self.start_of(item, axis)
            ref = self.total[item.array]
            buf = self.landing[item.at][axis]
            for d, device in enumerate(devices):
                if axis == "group":
                    row = start
                else:
                    row = start + (1 - self.places.bit[axis]) * after
                add(self.part(ref, row, after, item), buf.at[d], SUM_SLOT[axis] + d, device)
            return out
        start, size = self.held(item, stage)
        here = self.part(self.result[item.array], start, size, item)
        for device in devices:
            add(here, here, RESULT_SLOT[axis], device)
        return out

    def held(self, item, stage):
        start, size = self.start_of(item, None), item.size
        for kind, axis, before, after in item.stages[:stage]:
            if kind == "result":
                start, size = self.start_of(item, axis), before
        return start, size

    def op(self, index, stage):
        item = self.items[index]
        if item.action is not None:
            item.action(stage)
            if stage < len(item.stages):
                self.sent.append((item, stage))
            return
        if stage > 0:
            kind, axis, before, after = item.stages[stage - 1]
            copies = self.copies_of(item, stage - 1)
            for copy in copies:
                copy.wait_recv()
            if kind == "head":
                cols = slice(item.first, item.first + item.cols)
                total = self.total[item.array]
                total[:, cols] = (
                    self.own[item.array][:, cols].astype(F32) + total[:, cols].astype(F32)
                ).astype(BF16)
            elif kind == "sum":
                start = self.within(self.start_of(item, axis), axis, after)
                here = self.part(self.total[item.array], start, after, item)
                value = here[...].astype(F32)
                for d in range(len(copies)):
                    value = value + self.landing[item.at][axis][d].astype(F32)
                if item.stages[stage][0] != "result":
                    here[...] = value.astype(BF16)
                else:
                    self.part(self.result[item.array], start, after, item)[...] = value.astype(BF16)
        if stage < len(item.stages):
            for copy in self.copies_of(item, stage):
                copy.start()
            self.sent.append((item, stage))
        else:
            self.store_of(item).start()

    def store_of(self, item):
        cols = slice(item.first, item.first + item.cols)
        return pltpu.make_async_copy(
            self.result[item.array].at[:, cols], self.final[item.array].at[:, cols],
            self.store.at[item.at],
        )

    def finish(self):
        for item in self.items:
            if item.action is None and self.sent:
                self.store_of(item).wait()
        for item, stage in self.sent:
            copies = self.copies_of(item, stage) if item.action is None else item.copies(stage)
            for copy in copies:
                copy.wait_send()


class Other:
    def __init__(self, loads):
        self.stages, self.action, self.copies = loads, None, None
        self.later = 0

    def load(self, stage):
        return self.stages[stage]


def landing_shapes(items):
    shapes = []
    for item in items:
        if isinstance(item, Other):
            continue
        for kind, axis, before, after in item.stages:
            if kind == "sum":
                slots = item.groups - 1 if axis == "group" else 1
                shapes.append((item.at, axis, (slots, after, item.cols)))
    return shapes


def make_items(arrays, rows, cols, orders, groups, from_head, at=0):
    items = []
    step = len(arrays) * cols // len(orders)
    for index in range(len(orders)):
        array, first = divmod(index * step, cols)
        items.append(
            Item(at + index, arrays[array], first, step, rows, orders[index], groups, from_head)
        )
    return items


def run_batch(sums, batch):
    for index, stage in batch:
        sums.op(index, stage)


FFN_ORDERS = "GGAAAFFB"
HEAD_ORDERS = "DBDBBA"
MOVES = 4


def small_axes(groups):
    return ("x", "y", "u", "w") + (("group",) if groups > 1 else ())


def small_slot(axis):
    return 3 + {"x": 0, "y": 1, "u": 2, "w": 3, "group": 4}[axis]


def back_kernel(
    items, batches, groups, head_width, scale,
    up_hbm, down_hbm, q_hbm, k_hbm, v_hbm, g_hbm, x_hbm, xc_hbm, ctx_hbm, gattnb_hbm, gattn_hbm,
    wq_hbm, wk_hbm, wv_hbm, sorter_hbm, rows_hbm, lse_ref, seg_ref, gvec_ref, gbup_ref,
    out_up, out_down, out_heads, small_ref, din_all, rows_all,
    res_up, res_down, res_heads, total_up, total_down, total_heads, heads_own, heads_other,
    q_ref, k_ref, v_ref, g_ref, x_ref, xc_ref, ctx_ref, gattnb_ref, dx_ref, wq_ref, wk_ref, wv_ref,
    sorter_ref, bias_ref, gwo_ref, bsum_ref, dxc_ref, cross_land, small_land, small_stage,
    send, recv, small_send, small_recv, move_send, move_recv, local, store, *landing_refs,
):
    places = Places(groups)
    tokens, width = x_ref.shape
    block_len = bias_ref.shape[0]
    seqs = tokens // block_len
    blk = places.bit["x"]
    half = width // 2
    part = gbup_ref.shape[1] // 2
    head = places.head
    mine_cols = pl.ds(pl.multiple_of(head * half, half), half)
    their_cols = pl.ds(pl.multiple_of((1 - head) * half, half), half)

    pairs_in = [
        (up_hbm, total_up), (down_hbm, total_down),
        (q_hbm, q_ref), (k_hbm, k_ref), (v_hbm, v_ref), (g_hbm, g_ref),
        (wk_hbm, wk_ref), (wv_hbm, wv_ref), (x_hbm, x_ref), (xc_hbm, xc_ref), (ctx_hbm, ctx_ref),
        (gattnb_hbm, gattnb_ref), (sorter_hbm, sorter_ref), (gattn_hbm, dx_ref), (wq_hbm, wq_ref),
    ]
    loads = [
        pltpu.make_async_copy(source, target, local.at[at])
        for at, (source, target) in enumerate(pairs_in)
    ]
    for load in loads:
        load.start()
    places.greet()
    landing = {}
    for (at, axis, _), ref in zip(landing_shapes(items), landing_refs):
        landing.setdefault(at, {})[axis] = ref
    sums = Sums(
        items, places, {2: heads_own}, {2: heads_other}, [total_up, total_down, total_heads],
        [res_up, res_down, res_heads], [out_up, out_down, out_heads], landing, send, recv, store,
    )

    each = tokens // MOVES

    def kept(at):
        return pl.ds(pl.multiple_of(head * tokens + at * each, each), each)

    my_rows = pl.ds(pl.multiple_of(head * tokens, tokens), tokens)

    def rows_copy():
        return remote(
            rows_hbm.at[:, their_cols], rows_all.at[my_rows], move_send.at[2 * MOVES],
            move_recv.at[2 * MOVES], places.partners["head"][0],
        )

    rows_keep = pltpu.make_async_copy(
        rows_hbm.at[:, mine_cols], rows_all.at[my_rows], local.at[len(pairs_in) + MOVES]
    )
    rows_keep.start()

    def cross_copy(at):
        here = slice(at * each, (at + 1) * each)
        return remote(
            dxc_ref.at[here], cross_land.at[here], move_send.at[at], move_recv.at[at],
            places.partners["x"][0],
        )

    def head_copy(at):
        here = slice(at * each, (at + 1) * each)
        return remote(
            dx_ref.at[here, their_cols], din_all.at[kept(at)], move_send.at[MOVES + at],
            move_recv.at[MOVES + at], places.partners["head"][0],
        )

    def keep_copy(at):
        here = slice(at * each, (at + 1) * each)
        return pltpu.make_async_copy(
            dx_ref.at[here, mine_cols], din_all.at[kept(at)], local.at[len(pairs_in) + at]
        )

    def move_copies(at, stage):
        return [cross_copy(at) if stage == 0 else head_copy(at)]

    def move(at, stage):
        here = slice(at * each, (at + 1) * each)
        if stage == 0:
            cross_copy(at).start()
        elif stage == 1:
            cross_copy(at).wait_recv()
            dx_ref[here, :] = dx_ref[here, :] + cross_land[here, :].astype(F32)
            head_copy(at).start()
            keep_copy(at).start()
        else:
            head_copy(at).wait_recv()
            keep_copy(at).wait()

    axes = small_axes(groups)

    def small_copies(stage):
        if stage == 0:
            device = places.partners["head"][0]
            spans = (
                (gvec_ref.at[:, their_cols], slice(0, half)),
                (bsum_ref.at[:, half:], slice(half, 2 * half)),
                (gbup_ref.at[:, part:], slice(2 * half, 2 * half + part)),
            )
            return [
                remote(
                    source, small_land.at[at, :, span], small_send.at[at], small_recv.at[at], device
                )
                for at, (source, span) in enumerate(spans)
            ]
        first = small_slot(axes[stage - 1])
        return [
            remote(
                small_stage.at[stage], small_land.at[first + d], small_send.at[first + d],
                small_recv.at[first + d], device,
            )
            for d, device in enumerate(places.partners[axes[stage - 1]])
        ]

    def small(stage):
        if stage == 1:
            for copy in small_copies(0):
                copy.wait_recv()
            small_stage[1, :, :half] = gvec_ref[:, mine_cols] + small_land[0, :, :half]
            small_stage[1, :, half : 2 * half] = (
                bsum_ref[:, :half] + small_land[1, :, half : 2 * half]
            )
            small_stage[1, :, 2 * half :] = gbup_ref[:, :part] + small_land[2, :, 2 * half :]
        elif stage > 1:
            value = small_stage[stage - 1]
            first = small_slot(axes[stage - 2])
            for d, copy in enumerate(small_copies(stage - 1)):
                copy.wait_recv()
                value = value + small_land[first + d]
            if stage <= len(axes):
                small_stage[stage] = value
            else:
                small_ref[...] = value
        if stage <= len(axes):
            for copy in small_copies(stage):
                copy.start()

    others = [item for item in items if isinstance(item, Other)]
    others[0].action, others[0].copies = small, small_copies
    for at, item in enumerate(others[1:]):
        item.action = functools.partial(move, at)
        item.copies = functools.partial(move_copies, at)

    pair_width = 2 * head_width
    pairs = width // pair_width
    batches = list(batches)
    for at in (0, 1):
        loads[at].wait()
    run_batch(sums, batches.pop(0))

    def steps(count, body):
        last = len(batches) == count

        @pl.loop(0, count)
        def _(step):
            body(step)
            for at in range(count - 1 if last else count):
                if batches[at]:
                    @pl.when(step == at)
                    def _():
                        run_batch(sums, batches[at])

        if last:
            run_batch(sums, batches[-1])
        del batches[:count]

    def attention(crossed, step):
        seq = step // (pairs // 2)
        pair = crossed * (pairs // 2) + step % (pairs // 2)
        here = pl.ds(pl.multiple_of(seq * block_len, block_len), block_len)
        cols = pl.ds(pl.multiple_of(pair * pair_width, pair_width), pair_width)

        @pl.when(step % (pairs // 2) == 0)
        def _():
            fill_bias(bias_ref, seg_ref, head * seqs + seq, blk, 1 - blk if crossed else blk)

        queries, keys = q_ref[here, cols], k_ref[here, cols]
        values, grads = v_ref[here, cols], g_ref[here, cols]
        logs = lse_ref[seq, pair]
        key_cols = keys.astype(F32).T.astype(BF16)
        lane = lax.broadcasted_iota(jnp.int32, (1, pair_width), 1)
        query_parts = []
        for at, low in enumerate(range(0, pair_width, head_width)):
            chosen = jnp.logical_and(lane >= low, lane < low + head_width)
            scores = dot(keys, jnp.where(chosen, queries, 0), 1, 1) + bias_ref[...]
            mixing = jnp.exp(scores - logs[at : at + 1, :])
            grad_mixing = dot(values, jnp.where(chosen, grads, 0), 1, 1)
            inner = jnp.sum(mixing * grad_mixing, axis=0, keepdims=True)
            grad_scores = (mixing * (grad_mixing - inner)).astype(BF16)
            grad_value = dot(mixing.astype(BF16), grads)
            grad_key = dot(grad_scores, queries)
            query_parts.append(dot(key_cols[low : low + head_width], grad_scores))
            if at == 0:
                all_value, all_key = grad_value, grad_key
            else:
                all_value = jnp.where(chosen, grad_value, all_value)
                all_key = jnp.where(chosen, grad_key, all_key)
        q_ref[here, cols] = (jnp.concatenate(query_parts, axis=0).T.astype(BF16) * scale).astype(
            BF16
        )
        k_ref[here, cols] = all_key.astype(BF16)
        v_ref[here, cols] = all_value.astype(BF16)

    tile = 256

    def tile_of(step):
        return pl.ds(pl.multiple_of(step * tile, tile), tile)

    def cross_inputs(step):
        here = tile_of(step)
        dxc_ref[here, :] = (
            dot(k_ref[here, half:], wk_ref[:, half:], 1, 1)
            + dot(v_ref[here, half:], wv_ref[:, half:], 1, 1)
        ).astype(BF16)

    for at in range(2, 6):
        loads[at].wait()
    steps(seqs * pairs // 2, functools.partial(attention, 1))
    for at in (6, 7):
        loads[at].wait()
    steps(tokens // tile, cross_inputs)
    steps(seqs * pairs // 2, functools.partial(attention, 0))
    for at in range(8, 13):
        loads[at].wait()

    def weights(step):
        mine = tile_of(step)
        left, left_cross = x_ref[:, mine].T, xc_ref[:, mine].T
        for at, ref in enumerate((q_ref, k_ref, v_ref)):
            first = dot(left, ref[:, :half])
            second = dot(left if at == 0 else left_cross, ref[:, half:])
            found = jnp.concatenate([first, second], axis=1).astype(BF16)
            natural = dot(found, sorter_ref[...], 1, 1).astype(BF16)
            heads_own[mine, at * half : (at + 1) * half] = natural[:, :half]
            heads_other[mine, at * half : (at + 1) * half] = natural[:, half:]
        gwo_ref[mine, :] = dot(ctx_ref[:, mine].T, gattnb_ref[...]).astype(BF16)

    steps(width // tile, weights)

    def last_weight(_):
        for ref, low in ((heads_own, 0), (heads_other, half)):
            natural = dot(sorter_ref[low : low + half], gwo_ref[...]).astype(BF16)
            ref[:half, 3 * half :] = natural[:, :half]
            ref[half:, 3 * half :] = natural[:, half:]
        totals = []
        for ref in (q_ref, v_ref):
            totals.append(jnp.sum(ref[...].astype(F32), axis=0, keepdims=True))
        found = jnp.concatenate(totals + [jnp.zeros((6, width), F32)], axis=0)
        high = found.astype(BF16)
        rest = found - high.astype(F32)
        middle_part = rest.astype(BF16)
        rest = rest - middle_part.astype(F32)
        bsum_ref[...] = (
            dot(high, sorter_ref[...], 1, 1)
            + dot(middle_part, sorter_ref[...], 1, 1)
            + dot(rest.astype(BF16), sorter_ref[...], 1, 1)
        )

    steps(1, last_weight)
    rows_copy().start()
    for at in range(13, 15):
        loads[at].wait()

    def inputs(step):
        here = tile_of(step)
        dq, dk, dv = q_ref[here, :], k_ref[here, :], v_ref[here, :]
        dx_ref[here, :] = (
            dx_ref[here, :]
            + dot(dq, wq_ref[...], 1, 1)
            + dot(dk[:, :half], wk_ref[:, :half], 1, 1)
            + dot(dv[:, :half], wv_ref[:, :half], 1, 1)
        )

    steps(tokens // tile, inputs)
    assert not batches
    rows_keep.wait()
    rows_copy().wait()
    sums.finish()


def attention_back(
    grads, tokens, weights, out_rows, logs, segments, grad_vecs, grad_bup, block_len, head_width,
    scale, groups,
):
    rows, cols = grads[0].shape
    count, width = tokens[0].shape
    seqs = count // block_len
    items = make_items([0, 1], rows, cols, FFN_ORDERS, groups, False)
    items += make_items([2], rows, cols, HEAD_ORDERS, groups, True, len(items))
    pair_steps = seqs * width // (2 * head_width)
    tiles, weight_steps = count // 256, width // 256
    half_steps = pair_steps // 2
    times = (
        [2.3] * half_steps + [0.9] * tiles + [2.3] * half_steps + [4.0] * weight_steps + [1.5]
        + [1.1] * tiles
    )
    heads_at = pair_steps + tiles + weight_steps + 1
    ready = [0] * len(FFN_ORDERS) + [heads_at] * len(HEAD_ORDERS)
    small = (8, width + cols)
    items.append(Other([("head", 1e4)] + [(axis, 7e4) for axis in small_axes(groups)]))
    ready.append(heads_at)
    for at in range(MOVES):
        items.append(Other([("x", count // MOVES * width * 2), ("head", count // MOVES * width * 2)]))
        items[-1].later = heads_at + (at + 1) * tiles // MOVES
        ready.append(half_steps + (at + 1) * tiles // MOVES)
    batches = plan(items, times, ready)
    landing = landing_shapes(items)
    vmem = pl.BlockSpec(memory_space=pltpu.VMEM)
    anywhere = pl.BlockSpec(memory_space=pl.ANY)
    slots = len(FFN_ORDERS) + len(HEAD_ORDERS)
    small_slots = 7 + groups - 1
    big = pltpu.VMEM((rows, cols), BF16)
    rows_low = pltpu.VMEM((count, width), BF16)
    square = pltpu.VMEM((width, width), BF16)
    large = [*grads, *tokens, *weights, out_rows]
    return pl.pallas_call(
        functools.partial(back_kernel, items, batches, groups, head_width, scale),
        in_specs=[anywhere] * len(large) + [vmem] * 4,
        out_specs=[anywhere] * 3 + [vmem] + [anywhere] * 2,
        out_shape=[jax.ShapeDtypeStruct((rows, cols), BF16)] * 3
        + [jax.ShapeDtypeStruct(small, F32)]
        + [jax.ShapeDtypeStruct((2 * count, width // 2), F32)] * 2,
        scratch_shapes=[big] * 8
        + [rows_low] * 8
        + [pltpu.VMEM((count, width), F32)]
        + [square] * 4
        + [pltpu.VMEM((block_len, block_len), F32), square, pltpu.VMEM((8, width), F32)]
        + [rows_low] * 2
        + [pltpu.VMEM((small_slots, *small), F32), pltpu.VMEM((6, *small), F32)]
        + [pltpu.SemaphoreType.DMA((slots, slot_count(groups)))] * 2
        + [pltpu.SemaphoreType.DMA((small_slots,))] * 2
        + [pltpu.SemaphoreType.DMA((2 * MOVES + 1,))] * 2
        + [pltpu.SemaphoreType.DMA((len(large) + MOVES + 1,)), pltpu.SemaphoreType.DMA((slots,))]
        + [pltpu.VMEM(shape, BF16) for _, _, shape in landing],
        compiler_params=pltpu.CompilerParams(
            collective_id=1, has_side_effects=True, vmem_limit_bytes=63 * MIB
        ),
        name="attention_back",
    )(*large, logs, segments, grad_vecs, grad_bup)


def finish_kernel(moved, up_ref, down_ref, heads_ref, *refs):
    sources, refs = refs[:moved], refs[moved:]
    gup_ref, gdown_ref, gq_ref, gk_ref, gv_ref, go_ref, *targets = refs
    width = gq_ref.shape[1]
    gup_ref[...] = up_ref[...].astype(F32)
    gdown_ref[...] = down_ref[...].astype(F32).T
    for at, ref in enumerate((gq_ref, gk_ref, gv_ref, go_ref)):
        ref[...] = heads_ref[:, at * width : (at + 1) * width].astype(F32)
    for source, target in zip(sources, targets):
        target[...] = source[...]


def finish(up, down, heads, moved):
    rows, cols = up.shape
    steps = 4
    tile = rows // steps
    half, quarter = cols // 2, cols // 4
    spec = pl.BlockSpec((tile, cols), lambda i: (i, 0))
    third = pl.BlockSpec((tile, quarter), lambda i: (i, 0))
    moves = [
        pl.BlockSpec((array.shape[0] // steps, array.shape[1]), lambda i: (i, 0)) for array in moved
    ]
    return pl.pallas_call(
        functools.partial(finish_kernel, len(moved)),
        grid=(steps,),
        in_specs=[spec, pl.BlockSpec((rows, cols // steps), lambda i: (0, i)), spec] + moves,
        out_specs=[
            spec,
            pl.BlockSpec((cols // steps, rows), lambda i: (i, 0)),
            third,
            third,
            third,
            pl.BlockSpec((tile, quarter), lambda i: (i % (steps // 2), i // (steps // 2))),
        ]
        + moves,
        out_shape=[
            jax.ShapeDtypeStruct((rows, cols), F32),
            jax.ShapeDtypeStruct((cols, rows), F32),
            jax.ShapeDtypeStruct((rows, quarter), F32),
            jax.ShapeDtypeStruct((rows, quarter), F32),
            jax.ShapeDtypeStruct((rows, quarter), F32),
            jax.ShapeDtypeStruct((rows // 2, half), F32),
        ]
        + [jax.ShapeDtypeStruct(array.shape, array.dtype) for array in moved],
        compiler_params=pltpu.CompilerParams(vmem_limit_bytes=63 * MIB),
        name="finish",
    )(up, down, heads, *moved)


def on_device(
    layer_in, segments, block_perm, w_query, b_query, w_key, w_value, b_value, w_attn_out,
    b_attn_out, norm1_gain, norm1_bias, w_up, b_up, w_down, b_down, norm2_gain, norm2_bias,
    grad_out,
):
    _, block_len, half = layer_in.shape
    head_width = w_query.shape[1] // block_perm.shape[0]
    scale = head_width ** (-0.5)

    row = lax.broadcasted_iota(jnp.int32, (16, half), 0)
    vecs = jnp.pad(b_up.reshape(-1, half), ((8, 16 - 8 - b_up.shape[0] // half), (0, 0)))
    listed = [
        b_attn_out, norm1_gain, norm1_bias, b_down, norm2_gain, norm2_bias, b_query, b_value,
    ]
    for at, vec in enumerate(listed):
        vecs = jnp.where(row == at, vec[None, :], vecs)
    (
        x, x_cross, queries, keys, values, ctx, wq, wk, wv, wo, sorter, up_other, down_other,
        grad_rows, vectors, b_up_all, logs,
    ) = front(
        layer_in.reshape(-1, half),
        grad_out.reshape(-1, half),
        (w_query, w_key, w_value, w_attn_out, w_up, w_down),
        vecs,
        block_perm.T,
        segments,
        block_len,
        head_width,
        scale,
    )
    (
        out_rows, grad_attn, grad_attn_low, grad_ctx, grad_vecs, grad_bup, grad_up_all,
        grad_down_all,
    ) = middle(
        ctx, x, grad_rows, vectors, b_up_all, wo, (w_up, up_other), (w_down, down_other)
    )
    total_up, total_down, total_heads, small, grad_in, layer_out = attention_back(
        (grad_up_all, grad_down_all),
        (queries, keys, values, grad_ctx, x, x_cross, ctx, grad_attn_low, grad_attn),
        (wq, wk, wv, sorter),
        out_rows,
        logs,
        segments,
        grad_vecs,
        grad_bup,
        block_len,
        head_width,
        scale,
        lax.axis_size("dp") // 8,
    )
    grad_up, grad_down, grad_q, grad_k, grad_v, grad_o, grad_in, layer_out = finish(
        total_up, total_down, total_heads, (grad_in, layer_out)
    )
    return (
        layer_out.reshape(layer_in.shape),
        grad_in.reshape(layer_in.shape),
        grad_q,
        small[0, half : 2 * half],
        grad_k,
        grad_v,
        small[1, half : 2 * half],
        grad_o,
        small[0, :half],
        small[1, :half],
        small[2, :half],
        grad_up,
        small[0, 2 * half :],
        grad_down,
        small[3, :half],
        small[4, :half],
        small[5, :half],
    )


def solution(mesh):
    rows, cols, vec = P("head", None), P(None, "head"), P("head")
    tokens = P("dp", "blk", "head")
    return jax.shard_map(
        on_device,
        mesh=mesh,
        in_specs=(
            tokens, P("dp", None), rows, cols, vec, cols, cols, vec, rows, vec, vec, vec, cols,
            vec, rows, vec, vec, vec, tokens,
        ),
        out_specs=(
            tokens, tokens, cols, vec, cols, cols, vec, rows, vec, vec, vec, cols, vec, rows, vec,
            vec, vec,
        ),
        check_vma=False,
    )
```

```python
import functools

import jax
import jax.numpy as jnp
from jax import lax
from jax.experimental import pallas as pl
from jax.experimental.pallas import tpu as pltpu
from jax.sharding import PartitionSpec as P

EPSILON = 1e-05
NEGATIVE = -1e30
ROOT_HALF = 0.7071067811865476
DENSITY_SCALE = 0.3989422804014327
F32 = jnp.float32
BF16 = jnp.bfloat16
MIB = 1 << 20


def dot(left, right, left_dim=1, right_dim=0):
    return lax.dot_general(
        left, right, (((left_dim,), (right_dim,)), ((), ())), preferred_element_type=F32
    )


def remote(source, target, send, recv, device):
    return pltpu.make_async_remote_copy(
        src_ref=source,
        dst_ref=target,
        send_sem=send,
        recv_sem=recv,
        device_id=device,
        device_id_type=pl.DeviceIdType.MESH,
    )


def fill_bias(bias_ref, seg_ref, row, query_block, key_block):
    length = bias_ref.shape[0]

    def block(at):
        cols = pl.ds(pl.multiple_of(at * length, length), length)
        return seg_ref[pl.ds(row, 1), cols].astype(F32)

    lanes = 128
    keys = jnp.broadcast_to(block(key_block), (lanes, length)).T
    same = jnp.concatenate([keys] * (length // lanes), axis=1) == block(query_block)
    covered = jnp.max(jnp.where(same, 1.0, 0.0), axis=0, keepdims=True)
    bias_ref[...] = jnp.where(same, 0.0, covered * NEGATIVE)


def attend_pair(queries, keys, values, bias, head_width):
    pair_width = queries.shape[1]
    value_cols = values.astype(F32).T.astype(BF16)
    lane = lax.broadcasted_iota(jnp.int32, (1, pair_width), 1)
    parts, logs = [], []
    for low in range(0, pair_width, head_width):
        chosen = jnp.logical_and(lane >= low, lane < low + head_width)
        scores = dot(keys, jnp.where(chosen, queries, 0), 1, 1) + bias[...]
        top = jnp.max(scores, axis=0, keepdims=True)
        shifted = jnp.exp(scores - top)
        total = jnp.sum(shifted, axis=0, keepdims=True)
        context = dot(value_cols[low : low + head_width], shifted.astype(BF16))
        parts.append(context * (1.0 / total))
        logs.append(top + jnp.log(total))
    return jnp.concatenate(parts, axis=0).T.astype(BF16), jnp.concatenate(logs, axis=0)


def split_dot(left, right, left_dim=1, right_dim=0):
    high = left.astype(BF16)
    rest = left - high.astype(F32)
    mid = rest.astype(BF16)
    low = (rest - mid.astype(F32)).astype(BF16)
    return sum(dot(x, right, left_dim, right_dim) for x in (high, mid, low))


def front_kernel(
    head_width, scale, seqs,
    layer_hbm, gout_hbm, wq_hbm, wk_hbm, wv_hbm, wo_hbm, wup_hbm, wdn_hbm, vec_own, perm_ref,
    seg_ref,
    x_hbm, xc_hbm, q_hbm, k_hbm, v_hbm, ctx_hbm, wqs_hbm, wks_hbm, wvs_hbm, wos_hbm, sorter_hbm,
    wup_other, wdn_other, grad_hbm, vec_all, bup_all, lse_ref,
    x_ref, xc_ref, q_ref, k_ref, v_ref, ctx_ref, wn_q, wn_k, wn_v, wn_o, ws_q, ws_k, ws_v, ws_o,
    sorter_ref, sorter_t, vec_land, cross_own, cross_land, bias_ref, grad_ref, local, send, recv,
):
    head, blk = lax.axis_index("head"), lax.axis_index("blk")
    to_head, to_cross = {"head": 1 - head}, {"blk": 1 - blk}
    rows, width = x_ref.shape
    half = width // 2
    block_len = rows // seqs
    my_rows = pl.ds(pl.multiple_of(head * rows, rows), rows)
    their_rows = pl.ds(pl.multiple_of((1 - head) * rows, rows), rows)
    mine = pl.ds(pl.multiple_of(head * half, half), half)
    theirs = pl.ds(pl.multiple_of((1 - head) * half, half), half)

    started = []

    def bring(at, source, target):
        copy = pltpu.make_async_copy(source, target, local.at[at])
        copy.start()
        return copy

    def give(at, source, target, device):
        copy = remote(source, target, send.at[at], recv.at[at], device)
        copy.start()
        started.append(copy)
        return copy

    barrier = pltpu.get_barrier_semaphore()
    for device in (to_head, to_cross):
        pl.semaphore_signal(barrier, inc=1, device_id=device, device_id_type=pl.DeviceIdType.MESH)
    own_x = bring(0, layer_hbm.at[my_rows], x_ref.at[:, mine])
    own_w = [
        bring(1, wq_hbm, wn_q.at[:, :half]),
        bring(2, wk_hbm, wn_k.at[:, :half]),
        bring(3, wv_hbm, wn_v.at[:, :half]),
        bring(4, wo_hbm, wn_o.at[:half]),
    ]
    own_grad = bring(5, gout_hbm.at[my_rows], grad_ref)
    pl.semaphore_wait(barrier, 2)

    def seq_rows(seq):
        return slice(seq * block_len, (seq + 1) * block_len)

    def block_of(seq):
        return pl.ds(pl.multiple_of(head * rows + seq * block_len, block_len), block_len)

    perm = perm_ref[...]
    block = lax.broadcasted_iota(jnp.int32, perm.shape, 0)
    reads = jnp.sum(jnp.where(block == blk, perm, 0).astype(F32), axis=0, keepdims=True)
    reads = jnp.where(reads == blk.astype(F32), 0.0, 1.0)
    heads_shape = (perm.shape[1], half)
    feature_head = lax.broadcasted_iota(jnp.int32, heads_shape, 1) // head_width
    at_head = feature_head == lax.broadcasted_iota(jnp.int32, heads_shape, 0)
    cross_row = dot(
        jnp.broadcast_to(reads, (8, reads.shape[1])).astype(BF16),
        jnp.where(at_head, 1.0, 0.0).astype(BF16),
    )[0:1]
    cross_own[...] = jnp.broadcast_to(cross_row, cross_own.shape)
    flags = give(7 + 2 * seqs - 1 + 3, cross_own, cross_land, to_head)
    vecs = give(0, vec_own, vec_land, to_head)
    features = give(1, layer_hbm.at[their_rows], x_ref.at[:, mine], to_head)
    cross = [[give(2, layer_hbm.at[block_of(0)], xc_ref.at[seq_rows(0), mine], to_cross)]]
    other_w = [
        give(3, wq_hbm, wn_q.at[:, half:], to_head),
        give(4, wk_hbm, wn_k.at[:, half:], to_head),
        give(5, wv_hbm, wn_v.at[:, half:], to_head),
        give(6, wo_hbm, wn_o.at[half:], to_head),
    ]
    features.wait_recv()
    base = 7
    for seq in range(seqs):
        if seq > 0:
            cross.append(
                [give(base, layer_hbm.at[block_of(seq)], xc_ref.at[seq_rows(seq), mine], to_cross)]
            )
            base += 1
        here = seq_rows(seq)
        cross[seq].append(give(base, x_ref.at[here, theirs], xc_ref.at[here, theirs], to_cross))
        base += 1
    later = [
        give(base, wup_hbm, wup_other, to_head),
        give(base + 1, wdn_hbm, wdn_other, to_head),
        give(base + 2, gout_hbm.at[their_rows], grad_hbm.at[:, mine], to_head),
    ]

    vecs.wait_recv()
    flags.wait_recv()
    crossed = jnp.concatenate([cross_own[0:1, :], cross_land[0:1, :]], axis=1)
    row = lax.broadcasted_iota(jnp.int32, (width, width), 0)
    col = lax.broadcasted_iota(jnp.int32, (width, width), 1)
    earlier = jnp.where(row // head_width < col // head_width, 1.0, 0.0).astype(BF16)
    before = dot(jnp.broadcast_to(crossed, (8, width)).astype(BF16), earlier)[0:1]
    lane = lax.broadcasted_iota(jnp.int32, (1, width), 1)
    place = jnp.where(
        crossed > 0.5, half + before + (lane % head_width).astype(F32), lane.astype(F32) - before
    )
    found = jnp.where(row.astype(F32) == place, 1.0, 0.0)
    sorter_t[...] = found.astype(BF16)
    sorter_ref[...] = found.T.astype(BF16)
    vec_all[:, mine] = vec_own[0:8, :]
    vec_all[:, theirs] = vec_land[0:8, :]
    for at in range(bup_all.shape[1] // half):
        source = vec_own if at < 4 else vec_land
        bup_all[:, at * half : (at + 1) * half] = source[8 + at % 4 : 9 + at % 4, :]
    b_local = jnp.concatenate([vec_own[0:8, :], vec_land[0:8, :]], axis=1)
    b_sorted = split_dot(b_local, sorter_ref[...])
    bq, bv = b_sorted[6:7], b_sorted[7:8]

    own_grad.wait()
    out = [bring(17, grad_ref, grad_hbm.at[:, mine])]
    pairs_w = ((wn_q, ws_q, wqs_hbm), (wn_k, ws_k, wks_hbm), (wn_v, ws_v, wvs_hbm))
    for at, (natural, ordered, target) in enumerate(pairs_w):
        own_w[at].wait()
        other_w[at].wait_recv()
        ordered[...] = dot(natural[...], sorter_ref[...]).astype(BF16)
        out.append(bring(6 + at, ordered, target))
    out.append(bring(9, sorter_ref, sorter_hbm))
    own_x.wait()
    out.append(bring(10, x_ref, x_hbm))
    x = x_ref[...]
    q_ref[...] = ((dot(x, ws_q[...]) + bq) * scale).astype(BF16)
    out.append(bring(11, q_ref, q_hbm))
    k_ref[:, :half] = dot(x, ws_k[:, :half]).astype(BF16)
    v_ref[:, :half] = (dot(x, ws_v[:, :half]) + bv[:, :half]).astype(BF16)

    pair_width = 2 * head_width
    pairs = half // pair_width

    def attention(seq, first_pair, kind):
        here = pl.ds(pl.multiple_of(seq * block_len, block_len), block_len)
        fill_bias(bias_ref, seg_ref, head * seqs + seq, blk, 1 - blk if kind else blk)

        @pl.loop(0, pairs)
        def _(at):
            pair = first_pair + at
            cols = pl.ds(pl.multiple_of(pair * pair_width, pair_width), pair_width)
            context, logs = attend_pair(
                q_ref[here, cols], k_ref[here, cols], v_ref[here, cols], bias_ref, head_width
            )
            ctx_ref[here, cols] = context
            lse_ref[seq, pair] = logs

    @pl.loop(0, seqs)
    def _(seq):
        attention(seq, 0, 0)

    own_w[3].wait()
    other_w[3].wait_recv()
    ws_o[...] = dot(sorter_t[...], wn_o[...]).astype(BF16)
    out.append(bring(12, ws_o, wos_hbm))
    for seq in range(seqs):
        here = seq_rows(seq)
        for copy in cross[seq]:
            copy.wait_recv()
        out.append(bring(18 + 4 * seq, xc_ref.at[here], xc_hbm.at[here]))
        x_cross = xc_ref[here, :]
        k_ref[here, half:] = dot(x_cross, ws_k[:, half:]).astype(BF16)
        v_ref[here, half:] = (dot(x_cross, ws_v[:, half:]) + bv[:, half:]).astype(BF16)
        out.append(bring(19 + 4 * seq, k_ref.at[here], k_hbm.at[here]))
        out.append(bring(20 + 4 * seq, v_ref.at[here], v_hbm.at[here]))
        attention(seq, pairs, 1)
        out.append(bring(21 + 4 * seq, ctx_ref.at[here], ctx_hbm.at[here]))
    for copy in later:
        copy.wait_recv()
    for copy in out:
        copy.wait()
    for copy in started:
        copy.wait_send()


def front(layer_in, grad_out, weights, vecs, perm, segments, block_len, head_width, scale):
    width = weights[0].shape[0]
    half = width // 2
    seqs = segments.shape[0] // 2
    rows = seqs * block_len
    part = weights[4].shape[1]
    anywhere = pl.BlockSpec(memory_space=pl.ANY)
    vmem = pl.BlockSpec(memory_space=pltpu.VMEM)
    tokens = jax.ShapeDtypeStruct((rows, width), BF16)
    square = jax.ShapeDtypeStruct((width, width), BF16)
    low_rows, low_square = pltpu.VMEM((rows, width), BF16), pltpu.VMEM((width, width), BF16)
    copies = 7 + 2 * seqs - 1 + 3 + 1
    return pl.pallas_call(
        functools.partial(front_kernel, head_width, scale, seqs),
        in_specs=[anywhere] * 8 + [vmem] * 3,
        out_specs=[anywhere] * 14 + [vmem] * 3,
        out_shape=[tokens] * 6
        + [square] * 5
        + [
            jax.ShapeDtypeStruct(weights[4].shape, BF16),
            jax.ShapeDtypeStruct(weights[5].shape, BF16),
            jax.ShapeDtypeStruct((rows, width), F32),
            jax.ShapeDtypeStruct((8, width), F32),
            jax.ShapeDtypeStruct((1, 2 * part), F32),
            jax.ShapeDtypeStruct((seqs, width // (2 * head_width), 2, block_len), F32),
        ],
        scratch_shapes=[low_rows] * 6
        + [low_square] * 10
        + [
            pltpu.VMEM((16, half), F32),
            pltpu.VMEM((8, half), F32),
            pltpu.VMEM((8, half), F32),
            pltpu.VMEM((block_len, block_len), F32),
            pltpu.VMEM((rows, half), F32),
            pltpu.SemaphoreType.DMA((18 + 4 * seqs,)),
            pltpu.SemaphoreType.DMA((copies,)),
            pltpu.SemaphoreType.DMA((copies,)),
        ],
        compiler_params=pltpu.CompilerParams(
            collective_id=3, has_side_effects=True, vmem_limit_bytes=60 * MIB
        ),
        name="front",
    )(layer_in, grad_out, *weights, vecs, perm, segments)


def unit_rows(rows, width):
    mean = jnp.sum(rows, axis=1, keepdims=True) * (1.0 / width)
    centered = rows - mean
    variance = jnp.sum(centered * centered, axis=1, keepdims=True) * (1.0 / width)
    inverse = lax.rsqrt(variance + EPSILON)
    return centered * inverse, inverse


def unit_back(grad, unit, inverse, gain, width):
    scaled = grad * gain
    plain = jnp.sum(scaled, axis=1, keepdims=True) * (1.0 / width)
    along = jnp.sum(scaled * unit, axis=1, keepdims=True) * (1.0 / width)
    return (scaled - plain - unit * along) * inverse


def middle_kernel(
    chunk, tiles, ctx_ref, x_ref, gout_ref, vec_ref, bup_ref, wo_hbm,
    wup0_hbm, wup1_hbm, wdn0_hbm, wdn1_hbm,
    out_ref, gattn_ref, gattnb_ref, gctx_ref, gvec_ref, gbup_ref, gwup_ref, gwdn_ref,
    slope_ref, act_ref, gup_ref, normed_t, gffn_t, wo_ref, wup0_ref, wup1_ref, wdn0_ref, wdn1_ref,
    staged, landed, local, send, recv,
):
    tile, width = x_ref.shape
    part = wup0_ref.shape[1]
    at_step = pl.program_id(0)
    to_head = {"head": 1 - lax.axis_index("head")}
    loads = [
        pltpu.make_async_copy(source, target, local.at[at])
        for at, (source, target) in enumerate(
            (
                (wo_hbm, wo_ref), (wup0_hbm, wup0_ref), (wdn0_hbm, wdn0_ref),
                (wup1_hbm, wup1_ref), (wdn1_hbm, wdn1_ref),
            )
        )
    ]

    @pl.when(at_step == 0)
    def _():
        for load in loads:
            load.start()
        barrier = pltpu.get_barrier_semaphore()
        pl.semaphore_signal(
            barrier, inc=1, device_id=to_head, device_id_type=pl.DeviceIdType.MESH
        )
        for load in loads:
            load.wait()
        pl.semaphore_wait(barrier, 1)
        gvec_ref[...] = jnp.zeros_like(gvec_ref)
        gbup_ref[...] = jnp.zeros_like(gbup_ref)

    def vec(i):
        return vec_ref[i : i + 1, :]

    def add_vec(i, rows):
        gvec_ref[i : i + 1, :] += jnp.sum(rows, axis=0, keepdims=True)

    @pl.when(at_step < tiles)
    def _():
        here = pl.ds(pl.multiple_of(at_step * tile, tile), tile)
        attended = dot(ctx_ref[...], wo_ref[...])
        unit1, inverse1 = unit_rows(x_ref[...].astype(F32) + attended + vec(0), width)
        normed = unit1 * vec(1) + vec(2)
        normed_low = normed.astype(BF16)
        normed_t[:, here] = normed_low.T
        pieces = ((wup0_ref, wdn0_ref), (wup1_ref, wdn1_ref))
        down = jnp.zeros_like(normed)
        for at, (wup, wdn) in enumerate(pieces):
            for low in range(0, part, chunk):
                cols = slice(at * part + low, at * part + low + chunk)
                up = dot(normed_low, wup[:, low : low + chunk]) + bup_ref[:, cols]
                cumulative = 0.5 + 0.5 * lax.erf(up * ROOT_HALF)
                slope_ref[:, cols] = cumulative + up * (jnp.exp(-0.5 * up * up) * DENSITY_SCALE)
                activated = (up * cumulative).astype(BF16)
                act_ref[here, cols] = activated
                down += dot(activated, wdn[low : low + chunk, :])
        unit2, inverse2 = unit_rows(normed + down + vec(3), width)
        out_ref[...] = unit2 * vec(4) + vec(5)
        grad_out = gout_ref[...]
        add_vec(4, grad_out * unit2)
        add_vec(5, grad_out)
        grad_ffn = unit_back(grad_out, unit2, inverse2, vec(4), width)
        add_vec(3, grad_ffn)
        grad_ffn_low = grad_ffn.astype(BF16)
        gffn_t[:, here] = grad_ffn_low.T
        back = jnp.zeros_like(normed)
        for at, (wup, wdn) in enumerate(pieces):
            for low in range(0, part, chunk):
                cols = slice(at * part + low, at * part + low + chunk)
                grad_act = dot(grad_ffn_low, wdn[low : low + chunk, :], 1, 1)
                grad_up = (grad_act * slope_ref[:, cols]).astype(BF16)
                gup_ref[here, cols] = grad_up
                gbup_ref[0:1, cols] += jnp.sum(grad_up.astype(F32), axis=0, keepdims=True)
                back += dot(grad_up, wup[:, low : low + chunk], 1, 1)
        grad_mid = grad_ffn + back
        add_vec(1, grad_mid * unit1)
        add_vec(2, grad_mid)
        grad_attn = unit_back(grad_mid, unit1, inverse1, vec(1), width)
        add_vec(0, grad_attn)
        gattn_ref[...] = grad_attn
        grad_attn_low = grad_attn.astype(BF16)
        gattnb_ref[...] = grad_attn_low
        gctx_ref[...] = dot(grad_attn_low, wo_ref[...], 1, 1).astype(BF16)

    cols_step = gwup_ref.shape[1]
    count = part // cols_step

    def gradients(low):
        cols = pl.ds(pl.multiple_of(low, cols_step), cols_step)
        return dot(normed_t[...], gup_ref[:, cols]), dot(gffn_t[...], act_ref[:, cols])

    def exchange(slot):
        return remote(staged.at[slot], landed.at[slot], send.at[slot], recv.at[slot], to_head)

    @pl.when(jnp.logical_and(at_step >= tiles, at_step < tiles + count))
    def _():
        at = at_step - tiles
        for kind, value in enumerate(gradients(part + at * cols_step)):
            staged[kind * count + at] = value.astype(BF16)
            exchange(kind * count + at).start()

    @pl.when(at_step >= tiles + count)
    def _():
        at = at_step - tiles - count
        found = gradients(at * cols_step)
        for kind, (value, target) in enumerate(zip(found, (gwup_ref, gwdn_ref))):
            exchange(kind * count + at).wait()
            target[...] = (value + landed[kind * count + at].astype(F32)).astype(BF16)


def middle(ctx, x, grad_out, vectors, b_up, w_out, w_up, w_down):
    rows, width = x.shape
    part = w_up[0].shape[1]
    tile = 256
    tiles = rows // tile
    chunk = part // 2
    cols_step = part // 3

    def tiled(cols):
        return pl.BlockSpec((tile, cols), lambda i: (jnp.minimum(i, tiles - 1), 0))

    def whole(array):
        return pl.BlockSpec(array.shape, lambda i: (0, 0), pipeline_mode=pl.Buffered(1))

    def shape(cols, kind):
        return jax.ShapeDtypeStruct((rows, cols), kind)

    outs = [(width, F32), (width, F32), (width, BF16), (width, BF16)]
    sums = [jax.ShapeDtypeStruct((8, width), F32), jax.ShapeDtypeStruct((8, b_up.shape[1]), F32)]
    grads = [jax.ShapeDtypeStruct((width, part), BF16)] * 2
    count = part // cols_step
    grad_spec = pl.BlockSpec((width, cols_step), lambda i: (0, jnp.maximum(i - tiles - count, 0)))
    slots = pltpu.VMEM((2 * count, width, cols_step), BF16)
    weights = [vectors, b_up, w_out, *w_up, *w_down]
    return pl.pallas_call(
        functools.partial(middle_kernel, chunk, tiles),
        grid=(tiles + 2 * part // cols_step,),
        in_specs=[tiled(width), tiled(width), tiled(width)]
        + [whole(vectors), whole(b_up)]
        + [pl.BlockSpec(memory_space=pl.ANY)] * 5,
        out_specs=[tiled(c) for c, _ in outs]
        + [pl.BlockSpec(s.shape, lambda i: (0, 0)) for s in sums]
        + [grad_spec] * 2,
        out_shape=[shape(c, k) for c, k in outs] + sums + grads,
        scratch_shapes=[
            pltpu.VMEM((tile, 2 * part), F32),
            pltpu.VMEM((rows, 2 * part), BF16),
            pltpu.VMEM((rows, 2 * part), BF16),
            pltpu.VMEM((width, rows), BF16),
            pltpu.VMEM((width, rows), BF16),
        ]
        + [pltpu.VMEM(w.shape, BF16) for w in weights[2:]]
        + [slots, slots]
        + [pltpu.SemaphoreType.DMA((5,))]
        + [pltpu.SemaphoreType.DMA((2 * count,))] * 2,
        compiler_params=pltpu.CompilerParams(
            collective_id=4, has_side_effects=True, vmem_limit_bytes=62 * MIB
        ),
        name="middle",
    )(ctx, x, grad_out, *weights)


LINKS = {
    "head": (("core", 1),),
    "x": (("x", 1),),
    "y": (("y", 1),),
    "u": (("outer", 1),),
    "w": (("outer", 1), ("inner", 2)),
    "group": (("group", 1),),
}
RATES = {"core": 500e3, "x": 46e3, "y": 46e3, "outer": 46e3, "inner": 46e3, "group": 46e3}
DELAY = 4.5
OP_TIME = 0.3
URGENCY = 2.0
AHEAD = 8.0
ORDERS = {
    "A": "xyuw", "B": "yxuw", "C": "uwxy", "D": "uxyw", "E": "xuyw", "F": "yuxw", "G": "uyxw",
    "H": "uwyx", "I": "xuwy", "J": "yuwx", "K": "uxwy", "L": "uywx",
}


class Item:
    action = None
    later = 0

    def __init__(self, at, array, first, cols, rows, order, groups, from_head):
        self.at, self.array, self.first, self.cols, self.rows = at, array, first, cols, rows
        self.groups = groups
        self.sums = []
        size = rows
        for axis in [*ORDERS[order]] + (["group"] if groups > 1 else []):
            before = size
            size = size if axis == "group" else size // 2
            self.sums.append((axis, before, size))
        self.size = size
        self.stages = (
            [("head", "head", rows, rows)] * from_head
            + [("sum", *s) for s in self.sums]
            + [("result", *s) for s in reversed(self.sums) if s[0] != "group"]
        )

    def load(self, stage):
        kind, axis, before, size = self.stages[stage]
        moved = size * (self.groups - 1 if axis == "group" else 1)
        return axis, moved * self.cols * 2


def plan(items, steps, ready):
    free = {link: 0.0 for link in RATES}
    due = {i: (0.0, 0) for i in range(len(items))}
    batches = []
    now = 0.0

    def links(index, stage):
        item = items[index]
        return LINKS[item.load(stage)[0]] if stage < len(item.stages) else ()

    behind = []
    for index, item in enumerate(items):
        times = [
            DELAY + max(t * item.load(k)[1] / RATES[link] for link, t in links(index, k))
            for k in range(len(item.stages))
        ]
        behind.append([sum(times[k:]) for k in range(len(times) + 1)])

    def rank(i):
        return due[i][0] - URGENCY * behind[i][due[i][1]]

    def opens(i):
        return max([due[i][0]] + [free[link] - AHEAD for link, _ in links(i, due[i][1])])

    def run(index, batch):
        nonlocal now
        stage = due[index][1]
        batch.append((index, stage))
        now += OP_TIME
        if stage == len(items[index].stages):
            del due[index]
            return
        size = items[index].load(stage)[1]
        end = now
        for link, times in links(index, stage):
            free[link] = max(free[link], now) + times * size / RATES[link]
            end = max(end, free[link])
        due[index] = (end + DELAY, stage + 1)

    for at, time in enumerate([0.0] + steps):
        now += time
        batch = []
        while True:
            able = [
                i
                for i in due
                if opens(i) <= now and at >= (items[i].later if due[i][1] else ready[i])
            ]
            if not able:
                break
            run(min(able, key=rank), batch)
        batches.append(batch)
    while due:
        here = [i for i in due if opens(i) <= now]
        first = min(here, key=rank) if here else min(due, key=lambda i: (opens(i), i))
        now = max(now, opens(first))
        run(first, batches[-1])
    return batches


class Places:
    def __init__(self, groups):
        head, blk, dp = lax.axis_index("head"), lax.axis_index("blk"), lax.axis_index("dp")
        group = dp // 8
        self.head = head
        self.bit = {"x": blk, "y": dp % 2, "u": (dp // 2) % 2, "w": (dp // 4) % 2}
        self.partners = {
            "head": [{"head": 1 - head}],
            "x": [{"blk": 1 - blk}],
            "y": [{"dp": dp + 1 - 2 * self.bit["y"]}],
            "u": [{"dp": dp + 2 - 4 * self.bit["u"]}],
            "w": [{"dp": dp + 4 - 8 * self.bit["w"]}],
            "group": [{"dp": (group + d) % groups * 8 + dp % 8} for d in range(1, groups)],
        }

    def greet(self):
        barrier = pltpu.get_barrier_semaphore()
        everyone = [device for devices in self.partners.values() for device in devices]
        for device in everyone:
            pl.semaphore_signal(
                barrier, inc=1, device_id=device, device_id_type=pl.DeviceIdType.MESH
            )
        pl.semaphore_wait(barrier, len(everyone))


SUM_SLOT = {"x": 1, "y": 2, "u": 3, "w": 4, "group": 9}
RESULT_SLOT = {"x": 5, "y": 6, "u": 7, "w": 8}


def slot_count(groups):
    return 9 + groups - 1


class Sums:
    def __init__(
        self, items, places, own, other, total, result, final, landing, send, recv, store
    ):
        self.items, self.places, self.final, self.store = items, places, final, store
        self.own, self.other, self.total, self.result = own, other, total, result
        self.landing, self.send, self.recv = landing, send, recv
        self.sent = []

    def start_of(self, item, stop):
        start = 0
        for name, before, after in item.sums:
            if name == stop:
                return start
            start = self.within(start, name, after)
        return start

    def within(self, start, axis, after):
        if axis == "group":
            return start
        return start + self.places.bit[axis] * after

    def part(self, ref, start, size, item):
        return ref.at[
            pl.ds(pl.multiple_of(start, 16), size), item.first : item.first + item.cols
        ]

    def copies_of(self, item, stage):
        kind, axis, before, after = item.stages[stage]
        devices = self.places.partners[axis]
        out = []

        def add(source, target, slot, device):
            out.append(
                remote(
                    source, target, self.send.at[item.at, slot], self.recv.at[item.at, slot], device
                )
            )

        if kind == "head":
            cols = slice(item.first, item.first + item.cols)
            add(self.other[item.array].at[:, cols], self.total[item.array].at[:, cols], 0, devices[0])
            return out
        if kind == "sum":
            start = self.start_of(item, axis)
            ref = self.total[item.array]
            buf = self.landing[item.at][axis]
            for d, device in enumerate(devices):
                if axis == "group":
                    row = start
                else:
                    row = start + (1 - self.places.bit[axis]) * after
                add(self.part(ref, row, after, item), buf.at[d], SUM_SLOT[axis] + d, device)
            return out
        start, size = self.held(item, stage)
        here = self.part(self.result[item.array], start, size, item)
        for device in devices:
            add(here, here, RESULT_SLOT[axis], device)
        return out

    def held(self, item, stage):
        start, size = self.start_of(item, None), item.size
        for kind, axis, before, after in item.stages[:stage]:
            if kind == "result":
                start, size = self.start_of(item, axis), before
        return start, size

    def op(self, index, stage):
        item = self.items[index]
        if item.action is not None:
            item.action(stage)
            if stage < len(item.stages):
                self.sent.append((item, stage))
            return
        if stage > 0:
            kind, axis, before, after = item.stages[stage - 1]
            copies = self.copies_of(item, stage - 1)
            for copy in copies:
                copy.wait_recv()
            if kind == "head":
                cols = slice(item.first, item.first + item.cols)
                total = self.total[item.array]
                total[:, cols] = (
                    self.own[item.array][:, cols].astype(F32) + total[:, cols].astype(F32)
                ).astype(BF16)
            elif kind == "sum":
                start = self.within(self.start_of(item, axis), axis, after)
                here = self.part(self.total[item.array], start, after, item)
                value = here[...].astype(F32)
                for d in range(len(copies)):
                    value = value + self.landing[item.at][axis][d].astype(F32)
                if item.stages[stage][0] != "result":
                    here[...] = value.astype(BF16)
                else:
                    self.part(self.result[item.array], start, after, item)[...] = value.astype(BF16)
        if stage < len(item.stages):
            for copy in self.copies_of(item, stage):
                copy.start()
            self.sent.append((item, stage))
        else:
            self.store_of(item).start()

    def store_of(self, item):
        cols = slice(item.first, item.first + item.cols)
        return pltpu.make_async_copy(
            self.result[item.array].at[:, cols], self.final[item.array].at[:, cols],
            self.store.at[item.at],
        )

    def finish(self):
        for item in self.items:
            if item.action is None and self.sent:
                self.store_of(item).wait()
        for item, stage in self.sent:
            copies = self.copies_of(item, stage) if item.action is None else item.copies(stage)
            for copy in copies:
                copy.wait_send()


class Other:
    def __init__(self, loads):
        self.stages, self.action, self.copies = loads, None, None
        self.later = 0

    def load(self, stage):
        return self.stages[stage]


def landing_shapes(items):
    shapes = []
    for item in items:
        if isinstance(item, Other):
            continue
        for kind, axis, before, after in item.stages:
            if kind == "sum":
                slots = item.groups - 1 if axis == "group" else 1
                shapes.append((item.at, axis, (slots, after, item.cols)))
    return shapes


def make_items(spans, rows, groups, from_head, at=0):
    return [
        Item(at + index, array, first, cols, rows, order, groups, from_head)
        for index, (array, first, cols, order) in enumerate(spans)
    ]


def run_batch(sums, batch):
    for index, stage in batch:
        sums.op(index, stage)


FFN_ORDERS = "LBBLBBAA"
HEAD_ITEMS = [("o", 0, 3, "D"), ("v", 0, 3, "B"), ("k", 0, 3, "G"), ("q", 0, 3, "B")]
MOVES = 4


def small_axes(groups):
    return ("x", "y", "u", "w") + (("group",) if groups > 1 else ())


def small_slot(axis):
    return 3 + {"x": 0, "y": 1, "u": 2, "w": 3, "group": 4}[axis]


def back_kernel(
    items, batches, groups, head_width, scale,
    up_hbm, down_hbm, q_hbm, k_hbm, v_hbm, g_hbm, x_hbm, xc_hbm, ctx_hbm, gattnb_hbm, gattn_hbm,
    wq_hbm, wk_hbm, wv_hbm, sorter_hbm, rows_hbm, lse_ref, seg_ref, gvec_ref, gbup_ref,
    out_up, out_down, out_heads, small_ref, din_all, rows_all,
    res_up, res_down, res_heads, total_up, total_down, total_heads, heads_own, heads_other,
    q_ref, k_ref, v_ref, g_ref, x_ref, xc_ref, ctx_ref, gattnb_ref, dx_ref, wq_ref, wk_ref, wv_ref,
    sorter_ref, bias_ref, gwo_ref, bsum_ref, dxc_ref, cross_land, small_land, small_stage,
    send, recv, small_send, small_recv, move_send, move_recv, local, store, *landing_refs,
):
    places = Places(groups)
    tokens, width = x_ref.shape
    block_len = bias_ref.shape[0]
    seqs = tokens // block_len
    blk = places.bit["x"]
    half = width // 2
    part = gbup_ref.shape[1] // 2
    head = places.head
    mine_cols = pl.ds(pl.multiple_of(head * half, half), half)
    their_cols = pl.ds(pl.multiple_of((1 - head) * half, half), half)

    pairs_in = [
        (up_hbm, total_up), (down_hbm, total_down),
        (q_hbm, q_ref), (k_hbm, k_ref), (v_hbm, v_ref), (g_hbm, g_ref),
        (wk_hbm, wk_ref), (wv_hbm, wv_ref), (x_hbm, x_ref), (xc_hbm, xc_ref), (ctx_hbm, ctx_ref),
        (gattnb_hbm, gattnb_ref), (sorter_hbm, sorter_ref), (gattn_hbm, dx_ref), (wq_hbm, wq_ref),
    ]
    loads = [
        pltpu.make_async_copy(source, target, local.at[at])
        for at, (source, target) in enumerate(pairs_in)
    ]
    for load in loads:
        load.start()
    places.greet()
    landing = {}
    for (at, axis, _), ref in zip(landing_shapes(items), landing_refs):
        landing.setdefault(at, {})[axis] = ref
    sums = Sums(
        items, places, {2: heads_own}, {2: heads_other}, [total_up, total_down, total_heads],
        [res_up, res_down, res_heads], [out_up, out_down, out_heads], landing, send, recv, store,
    )

    each = tokens // MOVES

    def kept(at):
        return pl.ds(pl.multiple_of(head * tokens + at * each, each), each)

    my_rows = pl.ds(pl.multiple_of(head * tokens, tokens), tokens)

    def rows_copy():
        return remote(
            rows_hbm.at[:, their_cols], rows_all.at[my_rows], move_send.at[2 * MOVES],
            move_recv.at[2 * MOVES], places.partners["head"][0],
        )

    rows_keep = pltpu.make_async_copy(
        rows_hbm.at[:, mine_cols], rows_all.at[my_rows], local.at[len(pairs_in) + MOVES]
    )
    rows_keep.start()

    def cross_copy(at):
        here = slice(at * each, (at + 1) * each)
        return remote(
            dxc_ref.at[here], cross_land.at[here], move_send.at[at], move_recv.at[at],
            places.partners["x"][0],
        )

    def head_copy(at):
        here = slice(at * each, (at + 1) * each)
        return remote(
            dx_ref.at[here, their_cols], din_all.at[kept(at)], move_send.at[MOVES + at],
            move_recv.at[MOVES + at], places.partners["head"][0],
        )

    def keep_copy(at):
        here = slice(at * each, (at + 1) * each)
        return pltpu.make_async_copy(
            dx_ref.at[here, mine_cols], din_all.at[kept(at)], local.at[len(pairs_in) + at]
        )

    def move_copies(at, stage):
        return [cross_copy(at) if stage == 0 else head_copy(at)]

    def move(at, stage):
        here = slice(at * each, (at + 1) * each)
        if stage == 0:
            cross_copy(at).start()
        elif stage == 1:
            cross_copy(at).wait_recv()
            dx_ref[here, :] = dx_ref[here, :] + cross_land[here, :].astype(F32)
            head_copy(at).start()
            keep_copy(at).start()
        else:
            head_copy(at).wait_recv()
            keep_copy(at).wait()

    axes = small_axes(groups)

    def small_copies(stage):
        if stage == 0:
            device = places.partners["head"][0]
            spans = (
                (gvec_ref.at[:, their_cols], slice(0, half)),
                (bsum_ref.at[:, half:], slice(half, 2 * half)),
                (gbup_ref.at[:, part:], slice(2 * half, 2 * half + part)),
            )
            return [
                remote(
                    source, small_land.at[at, :, span], small_send.at[at], small_recv.at[at], device
                )
                for at, (source, span) in enumerate(spans)
            ]
        first = small_slot(axes[stage - 1])
        return [
            remote(
                small_stage.at[stage], small_land.at[first + d], small_send.at[first + d],
                small_recv.at[first + d], device,
            )
            for d, device in enumerate(places.partners[axes[stage - 1]])
        ]

    def small(stage):
        if stage == 1:
            for copy in small_copies(0):
                copy.wait_recv()
            small_stage[1, :, :half] = gvec_ref[:, mine_cols] + small_land[0, :, :half]
            small_stage[1, :, half : 2 * half] = (
                bsum_ref[:, :half] + small_land[1, :, half : 2 * half]
            )
            small_stage[1, :, 2 * half :] = gbup_ref[:, :part] + small_land[2, :, 2 * half :]
        elif stage > 1:
            value = small_stage[stage - 1]
            first = small_slot(axes[stage - 2])
            for d, copy in enumerate(small_copies(stage - 1)):
                copy.wait_recv()
                value = value + small_land[first + d]
            if stage <= len(axes):
                small_stage[stage] = value
            else:
                small_ref[...] = value
        if stage <= len(axes):
            for copy in small_copies(stage):
                copy.start()

    others = [item for item in items if isinstance(item, Other)]
    others[0].action, others[0].copies = small, small_copies
    for at, item in enumerate(others[1:]):
        item.action = functools.partial(move, at)
        item.copies = functools.partial(move_copies, at)

    pair_width = 2 * head_width
    pairs = width // pair_width
    batches = list(batches)
    for at in (0, 1):
        loads[at].wait()
    run_batch(sums, batches.pop(0))

    def steps(count, body):
        last = len(batches) == count

        @pl.loop(0, count)
        def _(step):
            body(step)
            for at in range(count - 1 if last else count):
                if batches[at]:
                    @pl.when(step == at)
                    def _():
                        run_batch(sums, batches[at])

        if last:
            run_batch(sums, batches[-1])
        del batches[:count]

    def attention(crossed, step):
        seq = step // (pairs // 2)
        pair = crossed * (pairs // 2) + step % (pairs // 2)
        here = pl.ds(pl.multiple_of(seq * block_len, block_len), block_len)
        cols = pl.ds(pl.multiple_of(pair * pair_width, pair_width), pair_width)

        @pl.when(step % (pairs // 2) == 0)
        def _():
            fill_bias(bias_ref, seg_ref, head * seqs + seq, blk, 1 - blk if crossed else blk)

        queries, keys = q_ref[here, cols], k_ref[here, cols]
        values, grads = v_ref[here, cols], g_ref[here, cols]
        logs = lse_ref[seq, pair]
        key_cols = keys.astype(F32).T.astype(BF16)
        lane = lax.broadcasted_iota(jnp.int32, (1, pair_width), 1)
        query_parts = []
        for at, low in enumerate(range(0, pair_width, head_width)):
            chosen = jnp.logical_and(lane >= low, lane < low + head_width)
            scores = dot(keys, jnp.where(chosen, queries, 0), 1, 1) + bias_ref[...]
            mixing = jnp.exp(scores - logs[at : at + 1, :])
            grad_mixing = dot(values, jnp.where(chosen, grads, 0), 1, 1)
            inner = jnp.sum(mixing * grad_mixing, axis=0, keepdims=True)
            grad_scores = (mixing * (grad_mixing - inner)).astype(BF16)
            grad_value = dot(mixing.astype(BF16), grads)
            grad_key = dot(grad_scores, queries)
            query_parts.append(dot(key_cols[low : low + head_width], grad_scores))
            if at == 0:
                all_value, all_key = grad_value, grad_key
            else:
                all_value = jnp.where(chosen, grad_value, all_value)
                all_key = jnp.where(chosen, grad_key, all_key)
        q_ref[here, cols] = (jnp.concatenate(query_parts, axis=0).T.astype(BF16) * scale).astype(
            BF16
        )
        k_ref[here, cols] = all_key.astype(BF16)
        v_ref[here, cols] = all_value.astype(BF16)

    tile = 256

    def tile_of(step):
        return pl.ds(pl.multiple_of(step * tile, tile), tile)

    def cross_inputs(step):
        here = tile_of(step)
        dxc_ref[here, :] = (
            dot(k_ref[here, half:], wk_ref[:, half:], 1, 1)
            + dot(v_ref[here, half:], wv_ref[:, half:], 1, 1)
        ).astype(BF16)

    for at in range(2, 6):
        loads[at].wait()
    steps(seqs * pairs // 2, functools.partial(attention, 1))
    for at in (6, 7):
        loads[at].wait()
    steps(tokens // tile, cross_inputs)
    for at in range(8, 13):
        loads[at].wait()

    def out_weight(_):
        @pl.loop(0, width // tile)
        def _(at):
            mine = tile_of(at)
            gwo_ref[mine, :] = dot(ctx_ref[:, mine].T, gattnb_ref[...]).astype(BF16)

        for ref, low in ((heads_own, 0), (heads_other, half)):
            natural = dot(sorter_ref[low : low + half], gwo_ref[...]).astype(BF16)
            ref[:half, 3 * half :] = natural[:, :half]
            ref[half:, 3 * half :] = natural[:, half:]

    steps(1, out_weight)
    steps(seqs * pairs // 2, functools.partial(attention, 0))

    def weight(kind, ref, left_cross, _):
        @pl.loop(0, width // tile)
        def _(at):
            mine = tile_of(at)
            first = dot(x_ref[:, mine].T, ref[:, :half])
            second = dot(left_cross[:, mine].T, ref[:, half:])
            found = jnp.concatenate([first, second], axis=1).astype(BF16)
            natural = dot(found, sorter_ref[...], 1, 1).astype(BF16)
            heads_own[mine, kind * half : (kind + 1) * half] = natural[:, :half]
            heads_other[mine, kind * half : (kind + 1) * half] = natural[:, half:]

    for kind, ref, left_cross in ((2, v_ref, xc_ref), (1, k_ref, xc_ref), (0, q_ref, x_ref)):
        steps(1, functools.partial(weight, kind, ref, left_cross))

    def vector_sums(_):
        totals = []
        for ref in (q_ref, v_ref):
            totals.append(jnp.sum(ref[...].astype(F32), axis=0, keepdims=True))
        found = jnp.concatenate(totals + [jnp.zeros((6, width), F32)], axis=0)
        bsum_ref[...] = split_dot(found, sorter_ref[...], 1, 1)

    steps(1, vector_sums)
    rows_copy().start()
    for at in range(13, 15):
        loads[at].wait()

    def inputs(step):
        here = tile_of(step)
        dq, dk, dv = q_ref[here, :], k_ref[here, :], v_ref[here, :]
        dx_ref[here, :] = (
            dx_ref[here, :]
            + dot(dq, wq_ref[...], 1, 1)
            + dot(dk[:, :half], wk_ref[:, :half], 1, 1)
            + dot(dv[:, :half], wv_ref[:, :half], 1, 1)
        )

    steps(tokens // tile, inputs)
    assert not batches
    rows_keep.wait()
    rows_copy().wait()
    sums.finish()


def attention_back(
    grads, tokens, weights, out_rows, logs, segments, grad_vecs, grad_bup, block_len, head_width,
    scale, groups,
):
    rows, cols = grads[0].shape
    count, width = tokens[0].shape
    seqs = count // block_len
    step = 2 * cols // len(FFN_ORDERS)
    spans = [(*divmod(at * step, cols), step, order) for at, order in enumerate(FFN_ORDERS)]
    items = make_items(spans, rows, groups, False)
    quarter = cols // 4
    spans = [
        (2, "qkvo".index(kind) * quarter + low * quarter // 3, size * quarter // 3, order)
        for kind, low, size, order in HEAD_ITEMS
    ]
    items += make_items(spans, rows, groups, True, len(items))
    pair_steps = seqs * width // (2 * head_width)
    tiles = count // 256
    half_steps = pair_steps // 2
    times = (
        [2.3] * half_steps + [0.9] * tiles + [3.0] + [2.3] * half_steps + [3.9] * 3 + [1.0]
        + [1.1] * tiles
    )
    after = pair_steps + tiles + 1
    kind_ready = {"o": half_steps + tiles + 1, "v": after + 1, "k": after + 2, "q": after + 3}
    ready = [0] * len(FFN_ORDERS) + [kind_ready[kind] for kind, _, _, _ in HEAD_ITEMS]
    small = (8, width + cols)
    items.append(Other([("head", 1e4)] + [(axis, 7e4) for axis in small_axes(groups)]))
    ready.append(after + 4)
    for at in range(MOVES):
        items.append(Other([("x", count // MOVES * width * 2), ("head", count // MOVES * width * 2)]))
        items[-1].later = after + 4 + (at + 1) * tiles // MOVES
        ready.append(half_steps + (at + 1) * tiles // MOVES)
    batches = plan(items, times, ready)
    landing = landing_shapes(items)
    vmem = pl.BlockSpec(memory_space=pltpu.VMEM)
    anywhere = pl.BlockSpec(memory_space=pl.ANY)
    slots = len(FFN_ORDERS) + len(HEAD_ITEMS)
    small_slots = 7 + groups - 1
    big = pltpu.VMEM((rows, cols), BF16)
    rows_low = pltpu.VMEM((count, width), BF16)
    square = pltpu.VMEM((width, width), BF16)
    large = [*grads, *tokens, *weights, out_rows]
    return pl.pallas_call(
        functools.partial(back_kernel, items, batches, groups, head_width, scale),
        in_specs=[anywhere] * len(large) + [vmem] * 4,
        out_specs=[anywhere] * 3 + [vmem] + [anywhere] * 2,
        out_shape=[jax.ShapeDtypeStruct((rows, cols), BF16)] * 3
        + [jax.ShapeDtypeStruct(small, F32)]
        + [jax.ShapeDtypeStruct((2 * count, width // 2), F32)] * 2,
        scratch_shapes=[big] * 8
        + [rows_low] * 8
        + [pltpu.VMEM((count, width), F32)]
        + [square] * 4
        + [pltpu.VMEM((block_len, block_len), F32), square, pltpu.VMEM((8, width), F32)]
        + [rows_low] * 2
        + [pltpu.VMEM((small_slots, *small), F32), pltpu.VMEM((6, *small), F32)]
        + [pltpu.SemaphoreType.DMA((slots, slot_count(groups)))] * 2
        + [pltpu.SemaphoreType.DMA((small_slots,))] * 2
        + [pltpu.SemaphoreType.DMA((2 * MOVES + 1,))] * 2
        + [pltpu.SemaphoreType.DMA((len(large) + MOVES + 1,)), pltpu.SemaphoreType.DMA((slots,))]
        + [pltpu.VMEM(shape, BF16) for _, _, shape in landing],
        compiler_params=pltpu.CompilerParams(
            collective_id=1, has_side_effects=True, vmem_limit_bytes=63 * MIB
        ),
        name="attention_back",
    )(*large, logs, segments, grad_vecs, grad_bup)


def finish_kernel(moved, up_ref, down_ref, heads_ref, *refs):
    sources, refs = refs[:moved], refs[moved:]
    gup_ref, gdown_ref, gq_ref, gk_ref, gv_ref, go_ref, *targets = refs
    width = gq_ref.shape[1]
    gup_ref[...] = up_ref[...].astype(F32)
    gdown_ref[...] = down_ref[...].astype(F32).T
    for at, ref in enumerate((gq_ref, gk_ref, gv_ref, go_ref)):
        ref[...] = heads_ref[:, at * width : (at + 1) * width].astype(F32)
    for source, target in zip(sources, targets):
        target[...] = source[...]


def finish(up, down, heads, moved):
    rows, cols = up.shape
    steps = 4
    tile = rows // steps
    half, quarter = cols // 2, cols // 4
    spec = pl.BlockSpec((tile, cols), lambda i: (i, 0))
    third = pl.BlockSpec((tile, quarter), lambda i: (i, 0))
    moves = [
        pl.BlockSpec((array.shape[0] // steps, array.shape[1]), lambda i: (i, 0)) for array in moved
    ]
    return pl.pallas_call(
        functools.partial(finish_kernel, len(moved)),
        grid=(steps,),
        in_specs=[spec, pl.BlockSpec((rows, cols // steps), lambda i: (0, i)), spec] + moves,
        out_specs=[
            spec,
            pl.BlockSpec((cols // steps, rows), lambda i: (i, 0)),
            third,
            third,
            third,
            pl.BlockSpec((tile, quarter), lambda i: (i % (steps // 2), i // (steps // 2))),
        ]
        + moves,
        out_shape=[
            jax.ShapeDtypeStruct((rows, cols), F32),
            jax.ShapeDtypeStruct((cols, rows), F32),
            jax.ShapeDtypeStruct((rows, quarter), F32),
            jax.ShapeDtypeStruct((rows, quarter), F32),
            jax.ShapeDtypeStruct((rows, quarter), F32),
            jax.ShapeDtypeStruct((rows // 2, half), F32),
        ]
        + [jax.ShapeDtypeStruct(array.shape, array.dtype) for array in moved],
        compiler_params=pltpu.CompilerParams(vmem_limit_bytes=63 * MIB),
        name="finish",
    )(up, down, heads, *moved)


def on_device(
    layer_in, segments, block_perm, w_query, b_query, w_key, w_value, b_value, w_attn_out,
    b_attn_out, norm1_gain, norm1_bias, w_up, b_up, w_down, b_down, norm2_gain, norm2_bias,
    grad_out,
):
    _, block_len, half = layer_in.shape
    head_width = w_query.shape[1] // block_perm.shape[0]
    scale = head_width ** (-0.5)

    row = lax.broadcasted_iota(jnp.int32, (16, half), 0)
    vecs = jnp.pad(b_up.reshape(-1, half), ((8, 16 - 8 - b_up.shape[0] // half), (0, 0)))
    listed = [
        b_attn_out, norm1_gain, norm1_bias, b_down, norm2_gain, norm2_bias, b_query, b_value,
    ]
    for at, vec in enumerate(listed):
        vecs = jnp.where(row == at, vec[None, :], vecs)
    (
        x, x_cross, queries, keys, values, ctx, wq, wk, wv, wo, sorter, up_other, down_other,
        grad_rows, vectors, b_up_all, logs,
    ) = front(
        layer_in.reshape(-1, half),
        grad_out.reshape(-1, half),
        (w_query, w_key, w_value, w_attn_out, w_up, w_down),
        vecs,
        block_perm.T,
        segments,
        block_len,
        head_width,
        scale,
    )
    (
        out_rows, grad_attn, grad_attn_low, grad_ctx, grad_vecs, grad_bup, grad_up_all,
        grad_down_all,
    ) = middle(
        ctx, x, grad_rows, vectors, b_up_all, wo, (w_up, up_other), (w_down, down_other)
    )
    total_up, total_down, total_heads, small, grad_in, layer_out = attention_back(
        (grad_up_all, grad_down_all),
        (queries, keys, values, grad_ctx, x, x_cross, ctx, grad_attn_low, grad_attn),
        (wq, wk, wv, sorter),
        out_rows,
        logs,
        segments,
        grad_vecs,
        grad_bup,
        block_len,
        head_width,
        scale,
        lax.axis_size("dp") // 8,
    )
    grad_up, grad_down, grad_q, grad_k, grad_v, grad_o, grad_in, layer_out = finish(
        total_up, total_down, total_heads, (grad_in, layer_out)
    )
    return (
        layer_out.reshape(layer_in.shape),
        grad_in.reshape(layer_in.shape),
        grad_q,
        small[0, half : 2 * half],
        grad_k,
        grad_v,
        small[1, half : 2 * half],
        grad_o,
        small[0, :half],
        small[1, :half],
        small[2, :half],
        grad_up,
        small[0, 2 * half :],
        grad_down,
        small[3, :half],
        small[4, :half],
        small[5, :half],
    )


def solution(mesh):
    rows, cols, vec = P("head", None), P(None, "head"), P("head")
    tokens = P("dp", "blk", "head")
    return jax.shard_map(
        on_device,
        mesh=mesh,
        in_specs=(
            tokens, P("dp", None), rows, cols, vec, cols, cols, vec, rows, vec, vec, vec, cols,
            vec, rows, vec, vec, vec, tokens,
        ),
        out_specs=(
            tokens, tokens, cols, vec, cols, cols, vec, rows, vec, vec, vec, cols, vec, rows, vec,
            vec, vec,
        ),
        check_vma=False,
    )
```

```python
import functools

import jax
import jax.numpy as jnp
from jax import lax
from jax.experimental import pallas as pl
from jax.experimental.pallas import tpu as pltpu
from jax.sharding import PartitionSpec as P

EPSILON = 1e-05
NEGATIVE = -1e30
ROOT_HALF = 0.7071067811865476
DENSITY_SCALE = 0.3989422804014327
F32 = jnp.float32
BF16 = jnp.bfloat16
MIB = 1 << 20


def dot(left, right, left_dim=1, right_dim=0):
    return lax.dot_general(
        left, right, (((left_dim,), (right_dim,)), ((), ())), preferred_element_type=F32
    )


def remote(source, target, send, recv, device):
    return pltpu.make_async_remote_copy(
        src_ref=source,
        dst_ref=target,
        send_sem=send,
        recv_sem=recv,
        device_id=device,
        device_id_type=pl.DeviceIdType.MESH,
    )


def fill_bias(bias_ref, seg_ref, row, query_block, key_block):
    length = bias_ref.shape[0]

    def block(at):
        cols = pl.ds(pl.multiple_of(at * length, length), length)
        return seg_ref[pl.ds(row, 1), cols].astype(F32)

    lanes = 128
    keys = jnp.broadcast_to(block(key_block), (lanes, length)).T
    same = jnp.concatenate([keys] * (length // lanes), axis=1) == block(query_block)
    covered = jnp.max(jnp.where(same, 1.0, 0.0), axis=0, keepdims=True)
    bias_ref[...] = jnp.where(same, 0.0, covered * NEGATIVE)


def attend_pair(queries, keys, values, bias, head_width):
    pair_width = queries.shape[1]
    value_cols = values.astype(F32).T.astype(BF16)
    lane = lax.broadcasted_iota(jnp.int32, (1, pair_width), 1)
    parts, logs = [], []
    for low in range(0, pair_width, head_width):
        chosen = jnp.logical_and(lane >= low, lane < low + head_width)
        scores = dot(keys, jnp.where(chosen, queries, 0), 1, 1) + bias[...]
        top = jnp.max(scores, axis=0, keepdims=True)
        shifted = jnp.exp(scores - top)
        total = jnp.sum(shifted, axis=0, keepdims=True)
        context = dot(value_cols[low : low + head_width], shifted.astype(BF16))
        parts.append(context * (1.0 / total))
        logs.append(top + jnp.log(total))
    return jnp.concatenate(parts, axis=0).T.astype(BF16), jnp.concatenate(logs, axis=0)


def split_dot(left, right, left_dim=1, right_dim=0):
    high = left.astype(BF16)
    rest = left - high.astype(F32)
    mid = rest.astype(BF16)
    low = (rest - mid.astype(F32)).astype(BF16)
    return sum(dot(x, right, left_dim, right_dim) for x in (high, mid, low))


def front_kernel(
    head_width, scale, seqs,
    layer_hbm, gout_hbm, wq_hbm, wk_hbm, wv_hbm, wo_hbm, wup_hbm, wdn_hbm, vec_own, perm_ref,
    seg_ref,
    x_hbm, xc_hbm, q_hbm, k_hbm, v_hbm, ctx_hbm, wqs_hbm, wks_hbm, wvs_hbm, wos_hbm, sorter_hbm,
    wup_other, wdn_other, grad_hbm, vec_all, bup_all, lse_ref,
    x_ref, xc_ref, q_ref, k_ref, v_ref, ctx_ref, wn_q, wn_k, wn_v, wn_o, ws_q, ws_k, ws_v, ws_o,
    sorter_ref, sorter_t, vec_land, cross_own, cross_land, bias_ref, grad_ref, local, send, recv,
):
    head, blk = lax.axis_index("head"), lax.axis_index("blk")
    to_head, to_cross = {"head": 1 - head}, {"blk": 1 - blk}
    rows, width = x_ref.shape
    half = width // 2
    block_len = rows // seqs
    my_rows = pl.ds(pl.multiple_of(head * rows, rows), rows)
    their_rows = pl.ds(pl.multiple_of((1 - head) * rows, rows), rows)
    mine = pl.ds(pl.multiple_of(head * half, half), half)
    theirs = pl.ds(pl.multiple_of((1 - head) * half, half), half)

    started = []

    def bring(at, source, target):
        copy = pltpu.make_async_copy(source, target, local.at[at])
        copy.start()
        return copy

    def give(at, source, target, device):
        copy = remote(source, target, send.at[at], recv.at[at], device)
        copy.start()
        started.append(copy)
        return copy

    barrier = pltpu.get_barrier_semaphore()
    for device in (to_head, to_cross):
        pl.semaphore_signal(barrier, inc=1, device_id=device, device_id_type=pl.DeviceIdType.MESH)
    own_x = bring(0, layer_hbm.at[my_rows], x_ref.at[:, mine])
    own_w = [
        bring(1, wq_hbm, wn_q.at[:, :half]),
        bring(2, wk_hbm, wn_k.at[:, :half]),
        bring(3, wv_hbm, wn_v.at[:, :half]),
        bring(4, wo_hbm, wn_o.at[:half]),
    ]
    own_grad = bring(5, gout_hbm.at[my_rows], grad_ref)
    pl.semaphore_wait(barrier, 2)

    def seq_rows(seq):
        return slice(seq * block_len, (seq + 1) * block_len)

    def block_of(seq):
        return pl.ds(pl.multiple_of(head * rows + seq * block_len, block_len), block_len)

    perm = perm_ref[...]
    block = lax.broadcasted_iota(jnp.int32, perm.shape, 0)
    reads = jnp.sum(jnp.where(block == blk, perm, 0).astype(F32), axis=0, keepdims=True)
    reads = jnp.where(reads == blk.astype(F32), 0.0, 1.0)
    heads_shape = (perm.shape[1], half)
    feature_head = lax.broadcasted_iota(jnp.int32, heads_shape, 1) // head_width
    at_head = feature_head == lax.broadcasted_iota(jnp.int32, heads_shape, 0)
    cross_row = dot(
        jnp.broadcast_to(reads, (8, reads.shape[1])).astype(BF16),
        jnp.where(at_head, 1.0, 0.0).astype(BF16),
    )[0:1]
    cross_own[...] = jnp.broadcast_to(cross_row, cross_own.shape)
    flags = give(7 + 2 * seqs - 1 + 3, cross_own, cross_land, to_head)
    vecs = give(0, vec_own, vec_land, to_head)
    features = give(1, layer_hbm.at[their_rows], x_ref.at[:, mine], to_head)
    cross = [[give(2, layer_hbm.at[block_of(0)], xc_ref.at[seq_rows(0), mine], to_cross)]]
    other_w = [
        give(3, wq_hbm, wn_q.at[:, half:], to_head),
        give(4, wk_hbm, wn_k.at[:, half:], to_head),
        give(5, wv_hbm, wn_v.at[:, half:], to_head),
        give(6, wo_hbm, wn_o.at[half:], to_head),
    ]
    features.wait_recv()
    base = 7
    for seq in range(seqs):
        if seq > 0:
            cross.append(
                [give(base, layer_hbm.at[block_of(seq)], xc_ref.at[seq_rows(seq), mine], to_cross)]
            )
            base += 1
        here = seq_rows(seq)
        cross[seq].append(give(base, x_ref.at[here, theirs], xc_ref.at[here, theirs], to_cross))
        base += 1
    later = [
        give(base, wup_hbm, wup_other, to_head),
        give(base + 1, wdn_hbm, wdn_other, to_head),
        give(base + 2, gout_hbm.at[their_rows], grad_hbm.at[:, mine], to_head),
    ]

    vecs.wait_recv()
    flags.wait_recv()
    crossed = jnp.concatenate([cross_own[0:1, :], cross_land[0:1, :]], axis=1)
    row = lax.broadcasted_iota(jnp.int32, (width, width), 0)
    col = lax.broadcasted_iota(jnp.int32, (width, width), 1)
    earlier = jnp.where(row // head_width < col // head_width, 1.0, 0.0).astype(BF16)
    before = dot(jnp.broadcast_to(crossed, (8, width)).astype(BF16), earlier)[0:1]
    lane = lax.broadcasted_iota(jnp.int32, (1, width), 1)
    place = jnp.where(
        crossed > 0.5, half + before + (lane % head_width).astype(F32), lane.astype(F32) - before
    )
    found = jnp.where(row.astype(F32) == place, 1.0, 0.0)
    sorter_t[...] = found.astype(BF16)
    sorter_ref[...] = found.T.astype(BF16)
    vec_all[:, mine] = vec_own[0:8, :]
    vec_all[:, theirs] = vec_land[0:8, :]
    for at in range(bup_all.shape[1] // half):
        source = vec_own if at < 4 else vec_land
        bup_all[:, at * half : (at + 1) * half] = source[8 + at % 4 : 9 + at % 4, :]
    b_local = jnp.concatenate([vec_own[0:8, :], vec_land[0:8, :]], axis=1)
    b_sorted = split_dot(b_local, sorter_ref[...])
    bq, bv = b_sorted[6:7], b_sorted[7:8]

    own_grad.wait()
    out = [bring(17, grad_ref, grad_hbm.at[:, mine])]
    pairs_w = ((wn_q, ws_q, wqs_hbm), (wn_k, ws_k, wks_hbm), (wn_v, ws_v, wvs_hbm))
    for at, (natural, ordered, target) in enumerate(pairs_w):
        own_w[at].wait()
        other_w[at].wait_recv()
        ordered[...] = dot(natural[...], sorter_ref[...]).astype(BF16)
        out.append(bring(6 + at, ordered, target))
    out.append(bring(9, sorter_ref, sorter_hbm))
    own_x.wait()
    out.append(bring(10, x_ref, x_hbm))
    x = x_ref[...]
    q_ref[...] = ((dot(x, ws_q[...]) + bq) * scale).astype(BF16)
    out.append(bring(11, q_ref, q_hbm))
    k_ref[:, :half] = dot(x, ws_k[:, :half]).astype(BF16)
    v_ref[:, :half] = (dot(x, ws_v[:, :half]) + bv[:, :half]).astype(BF16)

    pair_width = 2 * head_width
    pairs = half // pair_width

    def attention(seq, first_pair, kind):
        here = pl.ds(pl.multiple_of(seq * block_len, block_len), block_len)
        fill_bias(bias_ref, seg_ref, head * seqs + seq, blk, 1 - blk if kind else blk)

        @pl.loop(0, pairs)
        def _(at):
            pair = first_pair + at
            cols = pl.ds(pl.multiple_of(pair * pair_width, pair_width), pair_width)
            context, logs = attend_pair(
                q_ref[here, cols], k_ref[here, cols], v_ref[here, cols], bias_ref, head_width
            )
            ctx_ref[here, cols] = context
            lse_ref[seq, pair] = logs

    @pl.loop(0, seqs)
    def _(seq):
        attention(seq, 0, 0)

    own_w[3].wait()
    other_w[3].wait_recv()
    ws_o[...] = dot(sorter_t[...], wn_o[...]).astype(BF16)
    out.append(bring(12, ws_o, wos_hbm))
    for seq in range(seqs):
        here = seq_rows(seq)
        for copy in cross[seq]:
            copy.wait_recv()
        out.append(bring(18 + 4 * seq, xc_ref.at[here], xc_hbm.at[here]))
        x_cross = xc_ref[here, :]
        k_ref[here, half:] = dot(x_cross, ws_k[:, half:]).astype(BF16)
        v_ref[here, half:] = (dot(x_cross, ws_v[:, half:]) + bv[:, half:]).astype(BF16)
        out.append(bring(19 + 4 * seq, k_ref.at[here], k_hbm.at[here]))
        out.append(bring(20 + 4 * seq, v_ref.at[here], v_hbm.at[here]))
        attention(seq, pairs, 1)
        out.append(bring(21 + 4 * seq, ctx_ref.at[here], ctx_hbm.at[here]))
    for copy in later:
        copy.wait_recv()
    for copy in out:
        copy.wait()
    for copy in started:
        copy.wait_send()


def front(layer_in, grad_out, weights, vecs, perm, segments, block_len, head_width, scale):
    width = weights[0].shape[0]
    half = width // 2
    seqs = segments.shape[0] // 2
    rows = seqs * block_len
    part = weights[4].shape[1]
    anywhere = pl.BlockSpec(memory_space=pl.ANY)
    vmem = pl.BlockSpec(memory_space=pltpu.VMEM)
    tokens = jax.ShapeDtypeStruct((rows, width), BF16)
    square = jax.ShapeDtypeStruct((width, width), BF16)
    low_rows, low_square = pltpu.VMEM((rows, width), BF16), pltpu.VMEM((width, width), BF16)
    copies = 7 + 2 * seqs - 1 + 3 + 1
    return pl.pallas_call(
        functools.partial(front_kernel, head_width, scale, seqs),
        in_specs=[anywhere] * 8 + [vmem] * 3,
        out_specs=[anywhere] * 14 + [vmem] * 3,
        out_shape=[tokens] * 6
        + [square] * 5
        + [
            jax.ShapeDtypeStruct(weights[4].shape, BF16),
            jax.ShapeDtypeStruct(weights[5].shape, BF16),
            jax.ShapeDtypeStruct((rows, width), F32),
            jax.ShapeDtypeStruct((8, width), F32),
            jax.ShapeDtypeStruct((1, 2 * part), F32),
            jax.ShapeDtypeStruct((seqs, width // (2 * head_width), 2, block_len), F32),
        ],
        scratch_shapes=[low_rows] * 6
        + [low_square] * 10
        + [
            pltpu.VMEM((16, half), F32),
            pltpu.VMEM((8, half), F32),
            pltpu.VMEM((8, half), F32),
            pltpu.VMEM((block_len, block_len), F32),
            pltpu.VMEM((rows, half), F32),
            pltpu.SemaphoreType.DMA((18 + 4 * seqs,)),
            pltpu.SemaphoreType.DMA((copies,)),
            pltpu.SemaphoreType.DMA((copies,)),
        ],
        compiler_params=pltpu.CompilerParams(
            collective_id=3, has_side_effects=True, vmem_limit_bytes=60 * MIB
        ),
        name="front",
    )(layer_in, grad_out, *weights, vecs, perm, segments)


def unit_rows(rows, width):
    mean = jnp.sum(rows, axis=1, keepdims=True) * (1.0 / width)
    centered = rows - mean
    variance = jnp.sum(centered * centered, axis=1, keepdims=True) * (1.0 / width)
    inverse = lax.rsqrt(variance + EPSILON)
    return centered * inverse, inverse


def unit_back(grad, unit, inverse, gain, width):
    scaled = grad * gain
    plain = jnp.sum(scaled, axis=1, keepdims=True) * (1.0 / width)
    along = jnp.sum(scaled * unit, axis=1, keepdims=True) * (1.0 / width)
    return (scaled - plain - unit * along) * inverse


def middle_kernel(
    chunk, tiles, ctx_ref, x_ref, gout_ref, vec_ref, bup_ref, wo_hbm,
    wup0_hbm, wup1_hbm, wdn0_hbm, wdn1_hbm,
    out_ref, gattn_ref, gattnb_ref, gctx_ref, gvec_ref, gbup_ref, gwup_ref, gwdn_ref,
    slope_ref, act_ref, gup_ref, normed_t, gffn_t, wo_ref, wup0_ref, wup1_ref, wdn0_ref, wdn1_ref,
    staged, landed, local, send, recv,
):
    tile, width = x_ref.shape
    part = wup0_ref.shape[1]
    at_step = pl.program_id(0)
    to_head = {"head": 1 - lax.axis_index("head")}
    loads = [
        pltpu.make_async_copy(source, target, local.at[at])
        for at, (source, target) in enumerate(
            (
                (wo_hbm, wo_ref), (wup0_hbm, wup0_ref), (wdn0_hbm, wdn0_ref),
                (wup1_hbm, wup1_ref), (wdn1_hbm, wdn1_ref),
            )
        )
    ]

    @pl.when(at_step == 0)
    def _():
        for load in loads:
            load.start()
        barrier = pltpu.get_barrier_semaphore()
        pl.semaphore_signal(
            barrier, inc=1, device_id=to_head, device_id_type=pl.DeviceIdType.MESH
        )
        for load in loads[:3]:
            load.wait()
        pl.semaphore_wait(barrier, 1)
        gvec_ref[...] = jnp.zeros_like(gvec_ref)
        gbup_ref[...] = jnp.zeros_like(gbup_ref)

    def vec(i):
        return vec_ref[i : i + 1, :]

    def add_vec(i, rows):
        gvec_ref[i : i + 1, :] += jnp.sum(rows, axis=0, keepdims=True)

    @pl.when(at_step < tiles)
    def _():
        here = pl.ds(pl.multiple_of(at_step * tile, tile), tile)
        attended = dot(ctx_ref[...], wo_ref[...])
        unit1, inverse1 = unit_rows(x_ref[...].astype(F32) + attended + vec(0), width)
        normed = unit1 * vec(1) + vec(2)
        normed_low = normed.astype(BF16)
        normed_t[:, here] = normed_low.T
        pieces = ((wup0_ref, wdn0_ref), (wup1_ref, wdn1_ref))
        down = jnp.zeros_like(normed)
        for at, (wup, wdn) in enumerate(pieces):
            if at == 1:
                @pl.when(at_step == 0)
                def _():
                    for load in loads[3:]:
                        load.wait()

            for low in range(0, part, chunk):
                cols = slice(at * part + low, at * part + low + chunk)
                up = dot(normed_low, wup[:, low : low + chunk]) + bup_ref[:, cols]
                cumulative = 0.5 + 0.5 * lax.erf(up * ROOT_HALF)
                slope_ref[:, cols] = cumulative + up * (jnp.exp(-0.5 * up * up) * DENSITY_SCALE)
                activated = (up * cumulative).astype(BF16)
                act_ref[here, cols] = activated
                down += dot(activated, wdn[low : low + chunk, :])
        unit2, inverse2 = unit_rows(normed + down + vec(3), width)
        out_ref[...] = unit2 * vec(4) + vec(5)
        grad_out = gout_ref[...]
        add_vec(4, grad_out * unit2)
        add_vec(5, grad_out)
        grad_ffn = unit_back(grad_out, unit2, inverse2, vec(4), width)
        add_vec(3, grad_ffn)
        grad_ffn_low = grad_ffn.astype(BF16)
        gffn_t[:, here] = grad_ffn_low.T
        back = jnp.zeros_like(normed)
        for at, (wup, wdn) in enumerate(pieces):
            for low in range(0, part, chunk):
                cols = slice(at * part + low, at * part + low + chunk)
                grad_act = dot(grad_ffn_low, wdn[low : low + chunk, :], 1, 1)
                grad_up = (grad_act * slope_ref[:, cols]).astype(BF16)
                gup_ref[here, cols] = grad_up
                gbup_ref[0:1, cols] += jnp.sum(grad_up.astype(F32), axis=0, keepdims=True)
                back += dot(grad_up, wup[:, low : low + chunk], 1, 1)
        grad_mid = grad_ffn + back
        add_vec(1, grad_mid * unit1)
        add_vec(2, grad_mid)
        grad_attn = unit_back(grad_mid, unit1, inverse1, vec(1), width)
        add_vec(0, grad_attn)
        gattn_ref[...] = grad_attn
        grad_attn_low = grad_attn.astype(BF16)
        gattnb_ref[...] = grad_attn_low
        gctx_ref[...] = dot(grad_attn_low, wo_ref[...], 1, 1).astype(BF16)

    cols_step = gwup_ref.shape[1]
    count = part // cols_step

    def gradients(low):
        cols = pl.ds(pl.multiple_of(low, cols_step), cols_step)
        return dot(normed_t[...], gup_ref[:, cols]), dot(gffn_t[...], act_ref[:, cols])

    def exchange(slot):
        return remote(staged.at[slot], landed.at[slot], send.at[slot], recv.at[slot], to_head)

    @pl.when(jnp.logical_and(at_step >= tiles, at_step < tiles + count))
    def _():
        at = at_step - tiles
        for kind, value in enumerate(gradients(part + at * cols_step)):
            staged[kind * count + at] = value.astype(BF16)
            exchange(kind * count + at).start()

    @pl.when(at_step >= tiles + count)
    def _():
        at = at_step - tiles - count
        found = gradients(at * cols_step)
        for kind, (value, target) in enumerate(zip(found, (gwup_ref, gwdn_ref))):
            exchange(kind * count + at).wait()
            target[...] = (value + landed[kind * count + at].astype(F32)).astype(BF16)


def middle(ctx, x, grad_out, vectors, b_up, w_out, w_up, w_down):
    rows, width = x.shape
    part = w_up[0].shape[1]
    tile = 256
    tiles = rows // tile
    chunk = part // 2
    cols_step = part // 3

    def tiled(cols):
        return pl.BlockSpec((tile, cols), lambda i: (jnp.minimum(i, tiles - 1), 0))

    def whole(array):
        return pl.BlockSpec(array.shape, lambda i: (0, 0), pipeline_mode=pl.Buffered(1))

    def shape(cols, kind):
        return jax.ShapeDtypeStruct((rows, cols), kind)

    outs = [(width, F32), (width, F32), (width, BF16), (width, BF16)]
    sums = [jax.ShapeDtypeStruct((8, width), F32), jax.ShapeDtypeStruct((8, b_up.shape[1]), F32)]
    grads = [jax.ShapeDtypeStruct((width, part), BF16)] * 2
    count = part // cols_step
    grad_spec = pl.BlockSpec((width, cols_step), lambda i: (0, jnp.maximum(i - tiles - count, 0)))
    slots = pltpu.VMEM((2 * count, width, cols_step), BF16)
    weights = [vectors, b_up, w_out, *w_up, *w_down]
    return pl.pallas_call(
        functools.partial(middle_kernel, chunk, tiles),
        grid=(tiles + 2 * part // cols_step,),
        in_specs=[tiled(width), tiled(width), tiled(width)]
        + [whole(vectors), whole(b_up)]
        + [pl.BlockSpec(memory_space=pl.ANY)] * 5,
        out_specs=[tiled(c) for c, _ in outs]
        + [pl.BlockSpec(s.shape, lambda i: (0, 0)) for s in sums]
        + [grad_spec] * 2,
        out_shape=[shape(c, k) for c, k in outs] + sums + grads,
        scratch_shapes=[
            pltpu.VMEM((tile, 2 * part), F32),
            pltpu.VMEM((rows, 2 * part), BF16),
            pltpu.VMEM((rows, 2 * part), BF16),
            pltpu.VMEM((width, rows), BF16),
            pltpu.VMEM((width, rows), BF16),
        ]
        + [pltpu.VMEM(w.shape, BF16) for w in weights[2:]]
        + [slots, slots]
        + [pltpu.SemaphoreType.DMA((5,))]
        + [pltpu.SemaphoreType.DMA((2 * count,))] * 2,
        compiler_params=pltpu.CompilerParams(
            collective_id=4, has_side_effects=True, vmem_limit_bytes=62 * MIB
        ),
        name="middle",
    )(ctx, x, grad_out, *weights)


LINKS = {
    "head": (("core", 1),),
    "x": (("x", 1),),
    "y": (("y", 1),),
    "u": (("outer", 1),),
    "w": (("outer", 1), ("inner", 2)),
    "group": (("group", 1),),
}
RATES = {"core": 500e3, "x": 46e3, "y": 46e3, "outer": 46e3, "inner": 46e3, "group": 46e3}
DELAY = 4.5
OP_TIME = 0.3
URGENCY = 2.0
AHEAD = 8.0
ORDERS = {
    "A": "xyuw", "B": "yxuw", "C": "uwxy", "D": "uxyw", "E": "xuyw", "F": "yuxw", "G": "uyxw",
    "H": "uwyx", "I": "xuwy", "J": "yuwx", "K": "uxwy", "L": "uywx",
}


class Item:
    action = None
    later = 0

    def __init__(self, at, array, first, cols, rows, order, groups, from_head):
        self.at, self.array, self.first, self.cols, self.rows = at, array, first, cols, rows
        self.groups = groups
        self.sums = []
        size = rows
        for axis in [*ORDERS[order]] + (["group"] if groups > 1 else []):
            before = size
            size = size if axis == "group" else size // 2
            self.sums.append((axis, before, size))
        self.size = size
        self.stages = (
            [("head", "head", rows, rows)] * from_head
            + [("sum", *s) for s in self.sums]
            + [("result", *s) for s in reversed(self.sums) if s[0] != "group"]
        )

    def load(self, stage):
        kind, axis, before, size = self.stages[stage]
        moved = size * (self.groups - 1 if axis == "group" else 1)
        return axis, moved * self.cols * 2


def plan(items, steps, ready):
    free = {link: 0.0 for link in RATES}
    due = {i: (0.0, 0) for i in range(len(items))}
    batches = []
    now = 0.0

    def links(index, stage):
        item = items[index]
        return LINKS[item.load(stage)[0]] if stage < len(item.stages) else ()

    behind = []
    for index, item in enumerate(items):
        times = [
            DELAY + max(t * item.load(k)[1] / RATES[link] for link, t in links(index, k))
            for k in range(len(item.stages))
        ]
        behind.append([sum(times[k:]) for k in range(len(times) + 1)])

    def rank(i):
        return due[i][0] - URGENCY * behind[i][due[i][1]]

    def opens(i):
        return max([due[i][0]] + [free[link] - AHEAD for link, _ in links(i, due[i][1])])

    def run(index, batch):
        nonlocal now
        stage = due[index][1]
        batch.append((index, stage))
        now += OP_TIME
        if stage == len(items[index].stages):
            del due[index]
            return
        size = items[index].load(stage)[1]
        end = now
        for link, times in links(index, stage):
            free[link] = max(free[link], now) + times * size / RATES[link]
            end = max(end, free[link])
        due[index] = (end + DELAY, stage + 1)

    for at, time in enumerate([0.0] + steps):
        now += time
        batch = []
        while True:
            able = [
                i
                for i in due
                if opens(i) <= now and at >= (items[i].later if due[i][1] else ready[i])
            ]
            if not able:
                break
            run(min(able, key=rank), batch)
        batches.append(batch)
    while due:
        here = [i for i in due if opens(i) <= now]
        first = min(here, key=rank) if here else min(due, key=lambda i: (opens(i), i))
        now = max(now, opens(first))
        run(first, batches[-1])
    return batches


class Places:
    def __init__(self, groups):
        head, blk, dp = lax.axis_index("head"), lax.axis_index("blk"), lax.axis_index("dp")
        group = dp // 8
        self.head = head
        self.bit = {"x": blk, "y": dp % 2, "u": (dp // 2) % 2, "w": (dp // 4) % 2}
        self.partners = {
            "head": [{"head": 1 - head}],
            "x": [{"blk": 1 - blk}],
            "y": [{"dp": dp + 1 - 2 * self.bit["y"]}],
            "u": [{"dp": dp + 2 - 4 * self.bit["u"]}],
            "w": [{"dp": dp + 4 - 8 * self.bit["w"]}],
            "group": [{"dp": (group + d) % groups * 8 + dp % 8} for d in range(1, groups)],
        }

    def greet(self):
        barrier = pltpu.get_barrier_semaphore()
        everyone = [device for devices in self.partners.values() for device in devices]
        for device in everyone:
            pl.semaphore_signal(
                barrier, inc=1, device_id=device, device_id_type=pl.DeviceIdType.MESH
            )
        pl.semaphore_wait(barrier, len(everyone))


SUM_SLOT = {"x": 1, "y": 2, "u": 3, "w": 4, "group": 9}
RESULT_SLOT = {"x": 5, "y": 6, "u": 7, "w": 8}


def slot_count(groups):
    return 9 + groups - 1


class Sums:
    def __init__(
        self, items, places, own, other, total, result, final, landing, send, recv, store
    ):
        self.items, self.places, self.final, self.store = items, places, final, store
        self.own, self.other, self.total, self.result = own, other, total, result
        self.landing, self.send, self.recv = landing, send, recv
        self.sent = []

    def start_of(self, item, stop):
        start = 0
        for name, before, after in item.sums:
            if name == stop:
                return start
            start = self.within(start, name, after)
        return start

    def within(self, start, axis, after):
        if axis == "group":
            return start
        return start + self.places.bit[axis] * after

    def part(self, ref, start, size, item):
        return ref.at[
            pl.ds(pl.multiple_of(start, 16), size), item.first : item.first + item.cols
        ]

    def copies_of(self, item, stage):
        kind, axis, before, after = item.stages[stage]
        devices = self.places.partners[axis]
        out = []

        def add(source, target, slot, device):
            out.append(
                remote(
                    source, target, self.send.at[item.at, slot], self.recv.at[item.at, slot], device
                )
            )

        if kind == "head":
            cols = slice(item.first, item.first + item.cols)
            add(self.other[item.array].at[:, cols], self.total[item.array].at[:, cols], 0, devices[0])
            return out
        if kind == "sum":
            start = self.start_of(item, axis)
            ref = self.total[item.array]
            buf = self.landing[item.at][axis]
            for d, device in enumerate(devices):
                if axis == "group":
                    row = start
                else:
                    row = start + (1 - self.places.bit[axis]) * after
                add(self.part(ref, row, after, item), buf.at[d], SUM_SLOT[axis] + d, device)
            return out
        start, size = self.held(item, stage)
        here = self.part(self.result[item.array], start, size, item)
        for device in devices:
            add(here, here, RESULT_SLOT[axis], device)
        return out

    def held(self, item, stage):
        start, size = self.start_of(item, None), item.size
        for kind, axis, before, after in item.stages[:stage]:
            if kind == "result":
                start, size = self.start_of(item, axis), before
        return start, size

    def op(self, index, stage):
        item = self.items[index]
        if item.action is not None:
            item.action(stage)
            if stage < len(item.stages):
                self.sent.append((item, stage))
            return
        if stage > 0:
            kind, axis, before, after = item.stages[stage - 1]
            copies = self.copies_of(item, stage - 1)
            for copy in copies:
                copy.wait_recv()
            if kind == "head":
                cols = slice(item.first, item.first + item.cols)
                total = self.total[item.array]
                total[:, cols] = (
                    self.own[item.array][:, cols].astype(F32) + total[:, cols].astype(F32)
                ).astype(BF16)
            elif kind == "sum":
                start = self.within(self.start_of(item, axis), axis, after)
                here = self.part(self.total[item.array], start, after, item)
                value = here[...].astype(F32)
                for d in range(len(copies)):
                    value = value + self.landing[item.at][axis][d].astype(F32)
                if item.stages[stage][0] != "result":
                    here[...] = value.astype(BF16)
                else:
                    self.part(self.result[item.array], start, after, item)[...] = value.astype(BF16)
        if stage < len(item.stages):
            for copy in self.copies_of(item, stage):
                copy.start()
            self.sent.append((item, stage))
        else:
            self.store_of(item).start()

    def store_of(self, item):
        cols = slice(item.first, item.first + item.cols)
        return pltpu.make_async_copy(
            self.result[item.array].at[:, cols], self.final[item.array].at[:, cols],
            self.store.at[item.at],
        )

    def finish(self):
        for item in self.items:
            if item.action is None and self.sent:
                self.store_of(item).wait()
        for item, stage in self.sent:
            copies = self.copies_of(item, stage) if item.action is None else item.copies(stage)
            for copy in copies:
                copy.wait_send()


class Other:
    def __init__(self, loads):
        self.stages, self.action, self.copies = loads, None, None
        self.later = 0

    def load(self, stage):
        return self.stages[stage]


def landing_shapes(items):
    shapes = []
    for item in items:
        if isinstance(item, Other):
            continue
        for kind, axis, before, after in item.stages:
            if kind == "sum":
                slots = item.groups - 1 if axis == "group" else 1
                shapes.append((item.at, axis, (slots, after, item.cols)))
    return shapes


def make_items(spans, rows, groups, from_head, at=0):
    return [
        Item(at + index, array, first, cols, rows, order, groups, from_head)
        for index, (array, first, cols, order) in enumerate(spans)
    ]


def run_batch(sums, batch):
    for index, stage in batch:
        sums.op(index, stage)


FFN_ORDERS = "LBBLBBAA"
HEAD_ITEMS = [("o", 0, 3, "D"), ("v", 0, 3, "B"), ("k", 0, 3, "G"), ("q", 0, 3, "B")]
MOVES = 4


def small_axes(groups):
    return ("x", "y", "u", "w") + (("group",) if groups > 1 else ())


def small_slot(axis):
    return 3 + {"x": 0, "y": 1, "u": 2, "w": 3, "group": 4}[axis]


def back_kernel(
    items, batches, groups, head_width, scale,
    up_hbm, down_hbm, q_hbm, k_hbm, v_hbm, g_hbm, x_hbm, xc_hbm, ctx_hbm, gattnb_hbm, gattn_hbm,
    wq_hbm, wk_hbm, wv_hbm, sorter_hbm, rows_hbm, lse_ref, seg_ref, gvec_ref, gbup_ref,
    out_up, out_down, out_heads, small_ref, din_all, rows_all,
    res_up, res_down, res_heads, total_up, total_down, total_heads, heads_own, heads_other,
    q_ref, k_ref, v_ref, g_ref, x_ref, xc_ref, ctx_ref, gattnb_ref, dx_ref, wq_ref, wk_ref, wv_ref,
    sorter_ref, bias_ref, gwo_ref, bsum_ref, dxc_ref, cross_land, small_land, small_stage,
    send, recv, small_send, small_recv, move_send, move_recv, local, store, *landing_refs,
):
    places = Places(groups)
    tokens, width = x_ref.shape
    block_len = bias_ref.shape[0]
    seqs = tokens // block_len
    blk = places.bit["x"]
    half = width // 2
    part = gbup_ref.shape[1] // 2
    head = places.head
    mine_cols = pl.ds(pl.multiple_of(head * half, half), half)
    their_cols = pl.ds(pl.multiple_of((1 - head) * half, half), half)

    pairs_in = [
        (up_hbm, total_up), (down_hbm, total_down),
        (q_hbm, q_ref), (k_hbm, k_ref), (v_hbm, v_ref), (g_hbm, g_ref),
        (wk_hbm, wk_ref), (wv_hbm, wv_ref), (x_hbm, x_ref), (xc_hbm, xc_ref), (ctx_hbm, ctx_ref),
        (gattnb_hbm, gattnb_ref), (sorter_hbm, sorter_ref), (gattn_hbm, dx_ref), (wq_hbm, wq_ref),
    ]
    loads = [
        pltpu.make_async_copy(source, target, local.at[at])
        for at, (source, target) in enumerate(pairs_in)
    ]
    for load in loads:
        load.start()
    places.greet()
    landing = {}
    for (at, axis, _), ref in zip(landing_shapes(items), landing_refs):
        landing.setdefault(at, {})[axis] = ref
    sums = Sums(
        items, places, {2: heads_own}, {2: heads_other}, [total_up, total_down, total_heads],
        [res_up, res_down, res_heads], [out_up, out_down, out_heads], landing, send, recv, store,
    )

    each = tokens // MOVES

    def kept(at):
        return pl.ds(pl.multiple_of(head * tokens + at * each, each), each)

    my_rows = pl.ds(pl.multiple_of(head * tokens, tokens), tokens)

    def rows_copy():
        return remote(
            rows_hbm.at[:, their_cols], rows_all.at[my_rows], move_send.at[2 * MOVES],
            move_recv.at[2 * MOVES], places.partners["head"][0],
        )

    rows_keep = pltpu.make_async_copy(
        rows_hbm.at[:, mine_cols], rows_all.at[my_rows], local.at[len(pairs_in) + MOVES]
    )
    rows_keep.start()

    def cross_copy(at):
        here = slice(at * each, (at + 1) * each)
        return remote(
            dxc_ref.at[here], cross_land.at[here], move_send.at[at], move_recv.at[at],
            places.partners["x"][0],
        )

    def head_copy(at):
        here = slice(at * each, (at + 1) * each)
        return remote(
            dx_ref.at[here, their_cols], din_all.at[kept(at)], move_send.at[MOVES + at],
            move_recv.at[MOVES + at], places.partners["head"][0],
        )

    def keep_copy(at):
        here = slice(at * each, (at + 1) * each)
        return pltpu.make_async_copy(
            dx_ref.at[here, mine_cols], din_all.at[kept(at)], local.at[len(pairs_in) + at]
        )

    def move_copies(at, stage):
        return [cross_copy(at) if stage == 0 else head_copy(at)]

    def move(at, stage):
        here = slice(at * each, (at + 1) * each)
        if stage == 0:
            cross_copy(at).start()
        elif stage == 1:
            cross_copy(at).wait_recv()
            dx_ref[here, :] = dx_ref[here, :] + cross_land[here, :].astype(F32)
            head_copy(at).start()
            keep_copy(at).start()
        else:
            head_copy(at).wait_recv()
            keep_copy(at).wait()

    axes = small_axes(groups)

    def small_copies(stage):
        if stage == 0:
            device = places.partners["head"][0]
            spans = (
                (gvec_ref.at[:, their_cols], slice(0, half)),
                (bsum_ref.at[:, half:], slice(half, 2 * half)),
                (gbup_ref.at[:, part:], slice(2 * half, 2 * half + part)),
            )
            return [
                remote(
                    source, small_land.at[at, :, span], small_send.at[at], small_recv.at[at], device
                )
                for at, (source, span) in enumerate(spans)
            ]
        first = small_slot(axes[stage - 1])
        return [
            remote(
                small_stage.at[stage], small_land.at[first + d], small_send.at[first + d],
                small_recv.at[first + d], device,
            )
            for d, device in enumerate(places.partners[axes[stage - 1]])
        ]

    def small(stage):
        if stage == 1:
            for copy in small_copies(0):
                copy.wait_recv()
            small_stage[1, :, :half] = gvec_ref[:, mine_cols] + small_land[0, :, :half]
            small_stage[1, :, half : 2 * half] = (
                bsum_ref[:, :half] + small_land[1, :, half : 2 * half]
            )
            small_stage[1, :, 2 * half :] = gbup_ref[:, :part] + small_land[2, :, 2 * half :]
        elif stage > 1:
            value = small_stage[stage - 1]
            first = small_slot(axes[stage - 2])
            for d, copy in enumerate(small_copies(stage - 1)):
                copy.wait_recv()
                value = value + small_land[first + d]
            if stage <= len(axes):
                small_stage[stage] = value
            else:
                small_ref[...] = value
        if stage <= len(axes):
            for copy in small_copies(stage):
                copy.start()

    others = [item for item in items if isinstance(item, Other)]
    others[0].action, others[0].copies = small, small_copies
    for at, item in enumerate(others[1:]):
        item.action = functools.partial(move, at)
        item.copies = functools.partial(move_copies, at)

    pair_width = 2 * head_width
    pairs = width // pair_width
    batches = list(batches)
    for at in (0, 1):
        loads[at].wait()
    run_batch(sums, batches.pop(0))

    def steps(count, body):
        last = len(batches) == count

        @pl.loop(0, count)
        def _(step):
            body(step)
            for at in range(count - 1 if last else count):
                if batches[at]:
                    @pl.when(step == at)
                    def _():
                        run_batch(sums, batches[at])

        if last:
            run_batch(sums, batches[-1])
        del batches[:count]

    def attention(crossed, step):
        seq = step // (pairs // 2)
        pair = crossed * (pairs // 2) + step % (pairs // 2)
        here = pl.ds(pl.multiple_of(seq * block_len, block_len), block_len)
        cols = pl.ds(pl.multiple_of(pair * pair_width, pair_width), pair_width)

        @pl.when(step % (pairs // 2) == 0)
        def _():
            fill_bias(bias_ref, seg_ref, head * seqs + seq, blk, 1 - blk if crossed else blk)

        queries, keys = q_ref[here, cols], k_ref[here, cols]
        values, grads = v_ref[here, cols], g_ref[here, cols]
        logs = lse_ref[seq, pair]
        key_cols = keys.astype(F32).T.astype(BF16)
        lane = lax.broadcasted_iota(jnp.int32, (1, pair_width), 1)
        query_parts = []
        for at, low in enumerate(range(0, pair_width, head_width)):
            chosen = jnp.logical_and(lane >= low, lane < low + head_width)
            scores = dot(keys, jnp.where(chosen, queries, 0), 1, 1) + bias_ref[...]
            mixing = jnp.exp(scores - logs[at : at + 1, :])
            grad_mixing = dot(values, jnp.where(chosen, grads, 0), 1, 1)
            inner = jnp.sum(mixing * grad_mixing, axis=0, keepdims=True)
            grad_scores = (mixing * (grad_mixing - inner)).astype(BF16)
            grad_value = dot(mixing.astype(BF16), grads)
            grad_key = dot(grad_scores, queries)
            query_parts.append(dot(key_cols[low : low + head_width], grad_scores))
            if at == 0:
                all_value, all_key = grad_value, grad_key
            else:
                all_value = jnp.where(chosen, grad_value, all_value)
                all_key = jnp.where(chosen, grad_key, all_key)
        q_ref[here, cols] = (jnp.concatenate(query_parts, axis=0).T.astype(BF16) * scale).astype(
            BF16
        )
        k_ref[here, cols] = all_key.astype(BF16)
        v_ref[here, cols] = all_value.astype(BF16)

    tile = 256

    def tile_of(step):
        return pl.ds(pl.multiple_of(step * tile, tile), tile)

    def cross_inputs(step):
        here = tile_of(step)
        dxc_ref[here, :] = (
            dot(k_ref[here, half:], wk_ref[:, half:], 1, 1)
            + dot(v_ref[here, half:], wv_ref[:, half:], 1, 1)
        ).astype(BF16)

    for at in range(2, 6):
        loads[at].wait()
    steps(seqs * pairs // 2, functools.partial(attention, 1))
    for at in (6, 7):
        loads[at].wait()
    steps(tokens // tile, cross_inputs)
    for at in range(8, 13):
        loads[at].wait()

    def out_weight(_):
        @pl.loop(0, width // tile)
        def _(at):
            mine = tile_of(at)
            gwo_ref[mine, :] = dot(ctx_ref[:, mine].T, gattnb_ref[...]).astype(BF16)

        for ref, low in ((heads_own, 0), (heads_other, half)):
            natural = dot(sorter_ref[low : low + half], gwo_ref[...]).astype(BF16)
            ref[:half, 3 * half :] = natural[:, :half]
            ref[half:, 3 * half :] = natural[:, half:]

    steps(1, out_weight)
    steps(seqs * pairs // 2, functools.partial(attention, 0))

    def weight(kind, ref, left_cross, _):
        @pl.loop(0, width // tile)
        def _(at):
            mine = tile_of(at)
            first = dot(x_ref[:, mine].T, ref[:, :half])
            second = dot(left_cross[:, mine].T, ref[:, half:])
            found = jnp.concatenate([first, second], axis=1).astype(BF16)
            natural = dot(found, sorter_ref[...], 1, 1).astype(BF16)
            heads_own[mine, kind * half : (kind + 1) * half] = natural[:, :half]
            heads_other[mine, kind * half : (kind + 1) * half] = natural[:, half:]

    for kind, ref, left_cross in ((2, v_ref, xc_ref), (1, k_ref, xc_ref), (0, q_ref, x_ref)):
        steps(1, functools.partial(weight, kind, ref, left_cross))

    def vector_sums(_):
        totals = []
        for ref in (q_ref, v_ref):
            totals.append(jnp.sum(ref[...].astype(F32), axis=0, keepdims=True))
        found = jnp.concatenate(totals + [jnp.zeros((6, width), F32)], axis=0)
        bsum_ref[...] = split_dot(found, sorter_ref[...], 1, 1)

    steps(1, vector_sums)
    rows_copy().start()
    for at in range(13, 15):
        loads[at].wait()

    def inputs(step):
        here = tile_of(step)
        dq, dk, dv = q_ref[here, :], k_ref[here, :], v_ref[here, :]
        dx_ref[here, :] = (
            dx_ref[here, :]
            + dot(dq, wq_ref[...], 1, 1)
            + dot(dk[:, :half], wk_ref[:, :half], 1, 1)
            + dot(dv[:, :half], wv_ref[:, :half], 1, 1)
        )

    steps(tokens // tile, inputs)
    assert not batches
    rows_keep.wait()
    rows_copy().wait()
    sums.finish()


def attention_back(
    grads, tokens, weights, out_rows, logs, segments, grad_vecs, grad_bup, block_len, head_width,
    scale, groups,
):
    rows, cols = grads[0].shape
    count, width = tokens[0].shape
    seqs = count // block_len
    step = 2 * cols // len(FFN_ORDERS)
    spans = [(*divmod(at * step, cols), step, order) for at, order in enumerate(FFN_ORDERS)]
    items = make_items(spans, rows, groups, False)
    quarter = cols // 4
    spans = [
        (2, "qkvo".index(kind) * quarter + low * quarter // 3, size * quarter // 3, order)
        for kind, low, size, order in HEAD_ITEMS
    ]
    items += make_items(spans, rows, groups, True, len(items))
    pair_steps = seqs * width // (2 * head_width)
    tiles = count // 256
    half_steps = pair_steps // 2
    times = (
        [2.3] * half_steps + [0.9] * tiles + [3.0] + [2.3] * half_steps + [3.9] * 3 + [1.0]
        + [1.1] * tiles
    )
    after = pair_steps + tiles + 1
    kind_ready = {"o": half_steps + tiles + 1, "v": after + 1, "k": after + 2, "q": after + 3}
    ready = [0] * len(FFN_ORDERS) + [kind_ready[kind] for kind, _, _, _ in HEAD_ITEMS]
    small = (8, width + cols)
    items.append(Other([("head", 1e4)] + [(axis, 7e4) for axis in small_axes(groups)]))
    ready.append(after + 4)
    for at in range(MOVES):
        items.append(Other([("x", count // MOVES * width * 2), ("head", count // MOVES * width * 2)]))
        items[-1].later = after + 4 + (at + 1) * tiles // MOVES
        ready.append(half_steps + (at + 1) * tiles // MOVES)
    batches = plan(items, times, ready)
    landing = landing_shapes(items)
    vmem = pl.BlockSpec(memory_space=pltpu.VMEM)
    anywhere = pl.BlockSpec(memory_space=pl.ANY)
    slots = len(FFN_ORDERS) + len(HEAD_ITEMS)
    small_slots = 7 + groups - 1
    big = pltpu.VMEM((rows, cols), BF16)
    rows_low = pltpu.VMEM((count, width), BF16)
    square = pltpu.VMEM((width, width), BF16)
    large = [*grads, *tokens, *weights, out_rows]
    return pl.pallas_call(
        functools.partial(back_kernel, items, batches, groups, head_width, scale),
        in_specs=[anywhere] * len(large) + [vmem] * 4,
        out_specs=[anywhere] * 3 + [vmem] + [anywhere] * 2,
        out_shape=[jax.ShapeDtypeStruct((rows, cols), BF16)] * 3
        + [jax.ShapeDtypeStruct(small, F32)]
        + [jax.ShapeDtypeStruct((2 * count, width // 2), F32)] * 2,
        scratch_shapes=[big] * 8
        + [rows_low] * 8
        + [pltpu.VMEM((count, width), F32)]
        + [square] * 4
        + [pltpu.VMEM((block_len, block_len), F32), square, pltpu.VMEM((8, width), F32)]
        + [rows_low] * 2
        + [pltpu.VMEM((small_slots, *small), F32), pltpu.VMEM((6, *small), F32)]
        + [pltpu.SemaphoreType.DMA((slots, slot_count(groups)))] * 2
        + [pltpu.SemaphoreType.DMA((small_slots,))] * 2
        + [pltpu.SemaphoreType.DMA((2 * MOVES + 1,))] * 2
        + [pltpu.SemaphoreType.DMA((len(large) + MOVES + 1,)), pltpu.SemaphoreType.DMA((slots,))]
        + [pltpu.VMEM(shape, BF16) for _, _, shape in landing],
        compiler_params=pltpu.CompilerParams(
            collective_id=1, has_side_effects=True, vmem_limit_bytes=63 * MIB
        ),
        name="attention_back",
    )(*large, logs, segments, grad_vecs, grad_bup)


def finish_kernel(moved, up_ref, down_ref, heads_ref, *refs):
    sources, refs = refs[:moved], refs[moved:]
    gup_ref, gdown_ref, gq_ref, gk_ref, gv_ref, go_ref, *targets = refs
    width = gq_ref.shape[1]
    gup_ref[...] = up_ref[...].astype(F32)
    gdown_ref[...] = down_ref[...].astype(F32).T
    for at, ref in enumerate((gq_ref, gk_ref, gv_ref, go_ref)):
        ref[...] = heads_ref[:, at * width : (at + 1) * width].astype(F32)
    for source, target in zip(sources, targets):
        target[...] = source[...]


def finish(up, down, heads, moved):
    rows, cols = up.shape
    steps = 4
    tile = rows // steps
    half, quarter = cols // 2, cols // 4
    spec = pl.BlockSpec((tile, cols), lambda i: (i, 0))
    third = pl.BlockSpec((tile, quarter), lambda i: (i, 0))
    moves = [
        pl.BlockSpec((array.shape[0] // steps, array.shape[1]), lambda i: (i, 0)) for array in moved
    ]
    return pl.pallas_call(
        functools.partial(finish_kernel, len(moved)),
        grid=(steps,),
        in_specs=[spec, pl.BlockSpec((rows, cols // steps), lambda i: (0, i)), spec] + moves,
        out_specs=[
            spec,
            pl.BlockSpec((cols // steps, rows), lambda i: (i, 0)),
            third,
            third,
            third,
            pl.BlockSpec((tile, quarter), lambda i: (i % (steps // 2), i // (steps // 2))),
        ]
        + moves,
        out_shape=[
            jax.ShapeDtypeStruct((rows, cols), F32),
            jax.ShapeDtypeStruct((cols, rows), F32),
            jax.ShapeDtypeStruct((rows, quarter), F32),
            jax.ShapeDtypeStruct((rows, quarter), F32),
            jax.ShapeDtypeStruct((rows, quarter), F32),
            jax.ShapeDtypeStruct((rows // 2, half), F32),
        ]
        + [jax.ShapeDtypeStruct(array.shape, array.dtype) for array in moved],
        compiler_params=pltpu.CompilerParams(vmem_limit_bytes=63 * MIB),
        name="finish",
    )(up, down, heads, *moved)


def on_device(
    layer_in, segments, block_perm, w_query, b_query, w_key, w_value, b_value, w_attn_out,
    b_attn_out, norm1_gain, norm1_bias, w_up, b_up, w_down, b_down, norm2_gain, norm2_bias,
    grad_out,
):
    _, block_len, half = layer_in.shape
    head_width = w_query.shape[1] // block_perm.shape[0]
    scale = head_width ** (-0.5)

    row = lax.broadcasted_iota(jnp.int32, (16, half), 0)
    vecs = jnp.pad(b_up.reshape(-1, half), ((8, 16 - 8 - b_up.shape[0] // half), (0, 0)))
    listed = [
        b_attn_out, norm1_gain, norm1_bias, b_down, norm2_gain, norm2_bias, b_query, b_value,
    ]
    for at, vec in enumerate(listed):
        vecs = jnp.where(row == at, vec[None, :], vecs)
    (
        x, x_cross, queries, keys, values, ctx, wq, wk, wv, wo, sorter, up_other, down_other,
        grad_rows, vectors, b_up_all, logs,
    ) = front(
        layer_in.reshape(-1, half),
        grad_out.reshape(-1, half),
        (w_query, w_key, w_value, w_attn_out, w_up, w_down),
        vecs,
        block_perm.T,
        segments,
        block_len,
        head_width,
        scale,
    )
    (
        out_rows, grad_attn, grad_attn_low, grad_ctx, grad_vecs, grad_bup, grad_up_all,
        grad_down_all,
    ) = middle(
        ctx, x, grad_rows, vectors, b_up_all, wo, (w_up, up_other), (w_down, down_other)
    )
    total_up, total_down, total_heads, small, grad_in, layer_out = attention_back(
        (grad_up_all, grad_down_all),
        (queries, keys, values, grad_ctx, x, x_cross, ctx, grad_attn_low, grad_attn),
        (wq, wk, wv, sorter),
        out_rows,
        logs,
        segments,
        grad_vecs,
        grad_bup,
        block_len,
        head_width,
        scale,
        lax.axis_size("dp") // 8,
    )
    grad_up, grad_down, grad_q, grad_k, grad_v, grad_o, grad_in, layer_out = finish(
        total_up, total_down, total_heads, (grad_in, layer_out)
    )
    return (
        layer_out.reshape(layer_in.shape),
        grad_in.reshape(layer_in.shape),
        grad_q,
        small[0, half : 2 * half],
        grad_k,
        grad_v,
        small[1, half : 2 * half],
        grad_o,
        small[0, :half],
        small[1, :half],
        small[2, :half],
        grad_up,
        small[0, 2 * half :],
        grad_down,
        small[3, :half],
        small[4, :half],
        small[5, :half],
    )


def solution(mesh):
    rows, cols, vec = P("head", None), P(None, "head"), P("head")
    tokens = P("dp", "blk", "head")
    return jax.shard_map(
        on_device,
        mesh=mesh,
        in_specs=(
            tokens, P("dp", None), rows, cols, vec, cols, cols, vec, rows, vec, vec, vec, cols,
            vec, rows, vec, vec, vec, tokens,
        ),
        out_specs=(
            tokens, tokens, cols, vec, cols, cols, vec, rows, vec, vec, vec, cols, vec, rows, vec,
            vec, vec,
        ),
        check_vma=False,
    )
```
